32 devices in a mesh: dp: 4 (over z), fsdp: 8 (over y, x, core).
Axes of the slice: x: 2, y: 2, z: 4, core: 2. Of those that a mesh axis runs over, the one named last changes fastest.
Arguments:
- tokens: bfloat16 [65536, 1280], P(('dp', 'fsdp')), may hold values from -6 to 6
- cotangent: bfloat16 [65536, 1280], P(('dp', 'fsdp')), may hold values from -6 to 6
- lengths: int32 [64], P(('dp', 'fsdp')), may hold values from 256 to 1024, as said below
- labels: int32 [65536], P(('dp', 'fsdp')), may hold values from 0 to 24
- w_in: float32 [1280, 640], P('dp', 'fsdp'), may hold values from -0.15625 to 0.15625
- w_conv: float32 [5, 640, 640], P(None, 'dp', 'fsdp'), may hold values from -0.109375 to 0.109375
- w_out: float32 [640, 1280], P('dp', 'fsdp'), may hold values from -0.3125 to 0.3125
- norm_params: float32 [8, 640], P('dp', 'fsdp'), may hold values from -0.75 to 1.6
- mean_w_in: float32 [1280, 640], P('dp', 'fsdp'), may hold values from -768 to 768
- mean_w_conv: float32 [5, 640, 640], P(None, 'dp', 'fsdp'), may hold values from -768 to 768
- mean_w_out: float32 [640, 1280], P('dp', 'fsdp'), may hold values from -768 to 768
- mean_norms: float32 [8, 640], P('dp', 'fsdp'), may hold values from -768 to 768
- square_w_in: float32 [1280, 640], P('dp', 'fsdp'), may hold values from 10922.667 to 43690.668
- square_w_conv: float32 [5, 640, 640], P(None, 'dp', 'fsdp'), may hold values from 10922.667 to 43690.668
- square_w_out: float32 [640, 1280], P('dp', 'fsdp'), may hold values from 10922.667 to 43690.668
- square_norms: float32 [8, 640], P('dp', 'fsdp'), may hold values from 10922.667 to 43690.668
Outputs:
- mixed: bfloat16 [65536, 1280], P(('dp', 'fsdp'))
- grad_tokens: bfloat16 [65536, 1280], P(('dp', 'fsdp'))
- type_counts: int32 [25], replicated
- new_w_in: float32 [1280, 640], P('dp', 'fsdp')
- new_w_conv: float32 [5, 640, 640], P(None, 'dp', 'fsdp')
- new_w_out: float32 [640, 1280], P('dp', 'fsdp')
- new_norms: float32 [8, 640], P('dp', 'fsdp')
- new_mean_w_in: float32 [1280, 640], P('dp', 'fsdp')
- new_mean_w_conv: float32 [5, 640, 640], P(None, 'dp', 'fsdp')
- new_mean_w_out: float32 [640, 1280], P('dp', 'fsdp')
- new_mean_norms: float32 [8, 640], P('dp', 'fsdp')
- new_square_w_in: float32 [1280, 640], P('dp', 'fsdp')
- new_square_w_conv: float32 [5, 640, 640], P(None, 'dp', 'fsdp')
- new_square_w_out: float32 [640, 1280], P('dp', 'fsdp')
- new_square_norms: float32 [8, 640], P('dp', 'fsdp')
The draws below stay inside these ranges and needn't reach their ends.
Inputs may be any that keep to these rules, and one draw needn't show every extreme that they name: `lengths`: each device holds 2 sequences; the last sequence group's first sequence fills its bucket.
All inputs are finite; a program needn't handle non-finite values.
Results may differ from the reference program's by a relative error of at most 0.018.
Values may be sent and summed in bfloat16 or wider, within the bound.
A program may use at most 192 MiB of HBM per device.

```python
import math
import jax
import jax.numpy as jnp
from jax import lax

D = 1280
INNER = 640
KERNEL_TAPS = 5
DILATION_STRIDE = 8
SEQUENCE_SLOTS = 1024
SLOTS = 2
TYPES = 25
STEP = 5
SEQS = 64
TOKENS = 65536
N_FSDP = 8
DEVICES = 32


def draw_lengths(key, part):
    key = jax.random.fold_in(key, 1)
    total_count = SLOTS * DEVICES
    index = jnp.arange(total_count, dtype=jnp.int32)
    device = index // SLOTS
    rank_dp = device // N_FSDP
    rank_fsdp = device % N_FSDP
    span_dp = max(DEVICES // N_FSDP - 1, 1)
    span_fsdp = max(N_FSDP - 1, 1)
    reach = jnp.maximum(rank_fsdp * span_dp, rank_dp * span_fsdp)
    scale = span_dp * span_fsdp
    ceiling = SEQUENCE_SLOTS * (scale + 2 * reach) // (3 * scale)
    lowest = jnp.maximum(ceiling * 3 // 4, SEQUENCE_SLOTS // 4)
    jitter = jax.random.randint(key, (total_count,), 0, 1 << 20)
    drawn = lowest + jitter % (ceiling - lowest + 1)
    return jnp.where(index == total_count - SLOTS, SEQUENCE_SLOTS, drawn).astype(jnp.int32)


def draw_norm_params(key, part):
    key = jax.random.fold_in(key, 2)
    rows = lax.broadcasted_iota(jnp.int32, (8, INNER), 0)
    is_gain = (rows == 0) | (rows == 1) | (rows == 4) | (rows == 6)
    gains = jnp.clip(1.0 + 0.25 * jax.random.normal(key, (8, INNER), jnp.float32), 0.4, 1.6)
    biases = jnp.clip(0.3 * jax.random.normal(jax.random.fold_in(key, 5), (8, INNER), jnp.float32), -0.75, 0.75)
    return jnp.where(is_gain, gains, biases).astype(jnp.float32)


def set_ends(values, rng, low, high):
    extent = values.shape
    spot = [jax.random.randint(jax.random.fold_in(rng, axis), (), 0, extent[axis]) for axis in range(len(extent))]
    values = values.at[tuple(spot)].set(low)
    longest = extent.index(max(extent))
    spot[longest] = (spot[longest] + 1) % extent[longest]
    return values.at[tuple(spot)].set(high)


def levels(key, extent, split, least, high):
    def one(dim, parts):
        draws = jax.random.uniform(jax.random.fold_in(jax.random.fold_in(key, 6), dim), (parts,), jnp.float32, least / len(split), high / len(split))
        return jnp.repeat(jnp.exp(draws), extent[dim] // parts).reshape((-1,) + (1,) * (len(extent) - dim - 1))

    level = one(*split[0])
    for cut in split[1:]:
        level = level * one(*cut)
    return level


def noise(stream_key, extent, width, bound, pieces=(), held_as=jnp.bfloat16):
    entries = width * jax.random.normal(stream_key, extent, jnp.float32)
    if pieces:
        entries = entries * levels(stream_key, extent, pieces, -0.22, 0.18)
    return jnp.clip(entries, -bound, bound).astype(held_as)


def setup_inputs(seed: int = 0) -> dict:
    keys = jax.random.split(jax.random.key(seed), 17)
    return {
        "tokens": noise(keys[0], (TOKENS, D), 1.0, 6.0, ((0, 32),)),
        "cotangent": noise(keys[1], (TOKENS, D), 1.0, 6.0, ((0, 32),)),
        "lengths": draw_lengths(jax.random.fold_in(keys[16], 71), 0),
        "labels": set_ends(jax.random.randint(keys[3], (TOKENS,), 0, TYPES), jax.random.fold_in(keys[3], 1), 0, TYPES - 1).astype(jnp.int32),
        "w_in": noise(keys[4], (D, INNER), D ** -0.5, 0.15625, ((0, 4), (1, 8)), jnp.float32),
        "w_conv": noise(keys[5], (KERNEL_TAPS, INNER, INNER), (KERNEL_TAPS * INNER) ** -0.5, 0.109375, ((1, 4), (2, 8)), jnp.float32),
        "w_out": noise(keys[6], (INNER, D), (INNER // 2) ** -0.5, 0.3125, ((0, 4), (1, 8)), jnp.float32),
        "norm_params": draw_norm_params(jax.random.fold_in(keys[16], 71), 0),
        "mean_w_in": noise(keys[8], (D, INNER), (0.5 * TOKENS ** 0.5), 768.0, ((0, 4), (1, 8)), jnp.float32),
        "mean_w_conv": noise(keys[9], (KERNEL_TAPS, INNER, INNER), (0.5 * TOKENS ** 0.5), 768.0, ((1, 4), (2, 8)), jnp.float32),
        "mean_w_out": noise(keys[10], (INNER, D), (0.5 * TOKENS ** 0.5), 768.0, ((0, 4), (1, 8)), jnp.float32),
        "mean_norms": noise(keys[11], (8, INNER), (0.5 * TOKENS ** 0.5), 768.0, ((0, 4), (1, 8)), jnp.float32),
        "square_w_in": jnp.clip(jnp.exp(math.log(43690.668) - 1.3862944 * jax.random.uniform(keys[12], (D, INNER), jnp.float32) ** levels(keys[12], (D, INNER), ((0, 4), (1, 8)), -0.2, 0.2)), 10922.667, 43690.668),
        "square_w_conv": jnp.clip(jnp.exp(math.log(43690.668) - 1.3862944 * jax.random.uniform(keys[13], (KERNEL_TAPS, INNER, INNER), jnp.float32) ** levels(keys[13], (KERNEL_TAPS, INNER, INNER), ((1, 4), (2, 8)), -0.2, 0.2)), 10922.667, 43690.668),
        "square_w_out": jnp.clip(jnp.exp(math.log(43690.668) - 1.3862944 * jax.random.uniform(keys[14], (INNER, D), jnp.float32) ** levels(keys[14], (INNER, D), ((0, 4), (1, 8)), -0.2, 0.2)), 10922.667, 43690.668),
        "square_norms": jnp.clip(jnp.exp(math.log(43690.668) - 1.3862944 * jax.random.uniform(keys[15], (8, INNER), jnp.float32) ** levels(keys[15], (8, INNER), ((0, 4), (1, 8)), -0.2, 0.2)), 10922.667, 43690.668),
    }


@jax.custom_vjp
def low(v):
    return lax.optimization_barrier(v.astype(jnp.bfloat16)).astype(jnp.float32)

@jax.custom_vjp
def low_back(v):
    return v

def low_keep(v):
    return (low(v), None)

def low_pass(kept, grad):
    return (grad,)

def back_keep(v):
    return (v, None)

def back_low(kept, grad):
    return (low(grad),)
low.defvjp(low_keep, low_pass)
low_back.defvjp(back_keep, back_low)

def normalize(value, gain, bias):
    center = value - lax.optimization_barrier(jnp.mean(value, axis=-1, keepdims=True))
    spread = lax.optimization_barrier(jnp.mean(center * center, axis=-1, keepdims=True))
    return center * lax.rsqrt(spread + 1e-05) * gain + bias

def activate(value):
    return jax.nn.gelu(value, approximate=True)

def block(source, w_in, w_conv, w_out, norm_params, keep):
    norms = low(norm_params)
    gain_a = norms[0:2].reshape(D)
    bias_a = norms[2:4].reshape(D)
    act_a = low(activate(normalize(source, gain_a, bias_a)))
    hid_a = low_back(jnp.einsum('gsd,di->gsi', act_a, low(w_in), precision=lax.Precision.HIGHEST))
    middle_activation = low(activate(normalize(hid_a, norms[4], norms[5])) * keep)
    half_width = KERNEL_TAPS // 2
    padded_input = jnp.pad(middle_activation, ((0, 0), (half_width * DILATION_STRIDE, half_width * DILATION_STRIDE), (0, 0)))
    tap_weights = low(w_conv)
    middle_hidden = jnp.zeros(middle_activation.shape, jnp.float32)
    for tap_index in range(KERNEL_TAPS):
        middle_hidden = middle_hidden + jnp.einsum('ktn,nw->ktw', padded_input[:, tap_index * DILATION_STRIDE:tap_index * DILATION_STRIDE + SEQUENCE_SLOTS], tap_weights[tap_index], precision=lax.Precision.HIGHEST)
    middle_hidden = low_back(middle_hidden)
    act_c = low(activate(normalize(middle_hidden, norms[6], norms[7])))
    hid_c = low_back(jnp.einsum('gsi,id->gsd', act_c, low(w_out), precision=lax.Precision.HIGHEST))
    return source + keep * hid_c

def adamw(master, mean_old, square_old, grad, rate, decay):
    mean_new = 0.5 * mean_old + 0.5 * grad
    square_new = 0.6 * square_old + 0.4 * grad * grad
    mean_hat = mean_new / (1.0 - 0.5 ** STEP)
    square_hat = square_new / (1.0 - 0.6 ** STEP)
    weight = master - rate * (mean_hat / (jnp.sqrt(square_hat) + 1e-08) + decay * master)
    return (weight, mean_new, square_new)

def reference(tokens, cotangent, lengths, labels, w_in, w_conv, w_out, norm_params, mean_w_in, mean_w_conv, mean_w_out, mean_norms, square_w_in, square_w_conv, square_w_out, square_norms):
    group = math.gcd(SEQS, max(1, 4096 // SEQUENCE_SLOTS))
    count = SEQS // group
    places = jnp.arange(SEQUENCE_SLOTS, dtype=jnp.int32)
    valid = places[None, :] < lengths[:, None]
    keep_all = valid.astype(jnp.float32)
    source = tokens.astype(jnp.float32).reshape(count, group, SEQUENCE_SLOTS, D)
    backs = cotangent.astype(jnp.float32).reshape(count, group, SEQUENCE_SLOTS, D)
    keeps = keep_all.reshape(count, group, SEQUENCE_SLOTS, 1)
    params = (w_in, w_conv, w_out, norm_params)

    def step_group(totals, inputs):
        value, back, keep = inputs

        def forward(first, second, third, fourth, fifth):
            return block(first, second, third, fourth, fifth, keep)
        out, pull = jax.vjp(forward, value, w_in, w_conv, w_out, norm_params)
        gradient_tree = pull(back)
        totals = tuple((t + g for t, g in zip(totals, gradient_tree[1:])))
        return (totals, (out.astype(jnp.bfloat16), gradient_tree[0].astype(jnp.bfloat16)))
    zeros = tuple((jnp.zeros(p.shape, jnp.float32) for p in params))
    totals, outs = lax.scan(step_group, zeros, (source, backs, keeps))
    mixed = outs[0].reshape(TOKENS, D)
    grad_tokens = outs[1].reshape(TOKENS, D)
    kinds = jnp.arange(TYPES, dtype=jnp.int32)
    hits = (labels[:, None] == kinds[None, :]) & valid.reshape(TOKENS, 1)
    type_counts = lax.optimization_barrier(jnp.sum(hits.astype(jnp.int32), axis=0))
    new_in = adamw(w_in, mean_w_in, square_w_in, totals[0], 0.5 * D ** (-0.5), 0.01)
    new_conv = adamw(w_conv, mean_w_conv, square_w_conv, totals[1], 0.5 * (KERNEL_TAPS * INNER) ** (-0.5), 0.01)
    new_out = adamw(w_out, mean_w_out, square_w_out, totals[2], 0.5 * (INNER // 2) ** (-0.5), 0.01)
    new_norm = adamw(norm_params, mean_norms, square_norms, totals[3], 0.3, 0.0)
    return (mixed, grad_tokens, type_counts, new_in[0], new_conv[0], new_out[0], new_norm[0], new_in[1], new_conv[1], new_out[1], new_norm[1], new_in[2], new_conv[2], new_out[2], new_norm[2])
```

```python
import functools
from types import SimpleNamespace

import jax
import jax.numpy as jnp
from jax import lax
from jax.experimental import pallas as pl
from jax.experimental.pallas import tpu as pltpu
from jax.sharding import PartitionSpec as P

D = 1280
INNER = 640
KERNEL_TAPS = 5
DILATION_STRIDE = 8
TYPES = 25
STEP = 5


EPSILON = 1e-05


def plain_normalize(value, gain, bias):
    center = value - jnp.mean(value, axis=-1, keepdims=True)
    spread = jnp.mean(center * center, axis=-1, keepdims=True)
    return center * lax.rsqrt(spread + EPSILON) * gain + bias


def activate(value):
    return jax.nn.gelu(value, approximate=True)


def norm_piece(value, gain, bias):
    return activate(plain_normalize(value, gain, bias))


def gather_params(first, second, third, fourth):
    part = (
        lax.all_gather(first, "fsdp", axis=1, tiled=True),
        lax.all_gather(second, "fsdp", axis=2, tiled=True),
        lax.all_gather(third, "fsdp", axis=1, tiled=True),
        lax.all_gather(fourth, "fsdp", axis=1, tiled=True),
    )
    return (
        lax.all_gather(part[0], "dp", axis=0, tiled=True),
        lax.all_gather(part[1], "dp", axis=1, tiled=True),
        lax.all_gather(part[2], "dp", axis=0, tiled=True),
        lax.all_gather(part[3], "dp", axis=0, tiled=True),
    )


def reduce_grads(first, second, third, fourth):
    part = (
        lax.psum_scatter(first, "fsdp", scatter_dimension=1, tiled=True),
        lax.psum_scatter(second, "fsdp", scatter_dimension=2, tiled=True),
        lax.psum_scatter(third, "fsdp", scatter_dimension=1, tiled=True),
        lax.psum_scatter(fourth, "fsdp", scatter_dimension=1, tiled=True),
    )
    return (
        lax.psum_scatter(
            part[0].astype(jnp.bfloat16), "dp", scatter_dimension=0, tiled=True
        ).astype(jnp.float32),
        lax.psum_scatter(
            part[1].astype(jnp.bfloat16), "dp", scatter_dimension=1, tiled=True
        ).astype(jnp.float32),
        lax.psum_scatter(
            part[2].astype(jnp.bfloat16), "dp", scatter_dimension=0, tiled=True
        ).astype(jnp.float32),
        lax.psum_scatter(
            part[3].astype(jnp.bfloat16), "dp", scatter_dimension=0, tiled=True
        ).astype(jnp.float32),
    )


def stack_taps(value_rows):
    sequence_rows = value_rows.shape[1]
    half_width = KERNEL_TAPS // 2
    padded_input = jnp.pad(
        value_rows, ((0, 0), (half_width * DILATION_STRIDE, half_width * DILATION_STRIDE), (0, 0))
    )
    return jnp.concatenate(
        [
            padded_input[
                :, tap_index * DILATION_STRIDE : tap_index * DILATION_STRIDE + sequence_rows
            ]
            for tap_index in range(KERNEL_TAPS)
        ],
        axis=-1,
    )


def unstack_taps(gradient_tree, sequence_rows):
    half_width = KERNEL_TAPS // 2
    padded_input = jnp.pad(
        gradient_tree,
        ((0, 0), (half_width * DILATION_STRIDE, half_width * DILATION_STRIDE), (0, 0), (0, 0)),
    )
    total_count = padded_input[
        :, 2 * half_width * DILATION_STRIDE : 2 * half_width * DILATION_STRIDE + sequence_rows, 0
    ]
    for tap_index in range(1, KERNEL_TAPS):
        start_offset = (2 * half_width - tap_index) * DILATION_STRIDE
        total_count = (
            total_count + padded_input[:, start_offset : start_offset + sequence_rows, tap_index]
        )
    return total_count


def adamw(master, mean_old, square_old, grad, rate, decay):
    mean_new = 0.5 * mean_old + 0.5 * grad
    square_new = 0.6 * square_old + 0.4 * grad * grad
    mean_hat = mean_new / (1.0 - 0.5**STEP)
    square_hat = square_new / (1.0 - 0.6**STEP)
    weight = master - rate * (mean_hat / (jnp.sqrt(square_hat) + 1e-08) + decay * master)
    return (weight, mean_new, square_new)


def contract_rows(left, right):
    return lax.dot_general(
        left, right, (((0,), (0,)), ((), ())), preferred_element_type=jnp.float32
    )


def contract_cols(left, right):
    return lax.dot_general(
        left, right, (((1,), (1,)), ((), ())), preferred_element_type=jnp.float32
    )


def plain_body(
    tokens,
    cotangent,
    lengths,
    labels,
    w_in,
    w_conv,
    w_out,
    norm_params,
    mean_w_in,
    mean_w_conv,
    mean_w_out,
    mean_norms,
    square_w_in,
    square_w_conv,
    square_w_out,
    square_norms,
):
    slots = lengths.shape[0]
    rows = tokens.shape[0]
    sequence_rows = rows // slots
    places = lax.broadcasted_iota(jnp.int32, (slots, sequence_rows), 1)
    valid = (places < lengths[:, None]).reshape(rows, 1)
    keep = valid.astype(jnp.float32)
    full_in, full_conv, full_out, full_norms = gather_params(
        w_in.astype(jnp.bfloat16),
        w_conv.astype(jnp.bfloat16),
        w_out.astype(jnp.bfloat16),
        norm_params.astype(jnp.bfloat16),
    )
    inner = full_in.shape[1]
    norms = full_norms.astype(jnp.float32)
    gain_a = norms[0:2].reshape(2 * inner)
    bias_a = norms[2:4].reshape(2 * inner)
    source = tokens.astype(jnp.float32)

    def masked_piece(value, gain, bias):
        return norm_piece(value, gain, bias) * keep

    act_a, back_a = jax.vjp(norm_piece, source, gain_a, bias_a)
    low_a = act_a.astype(jnp.bfloat16)
    hid_a = jnp.dot(low_a, full_in, preferred_element_type=jnp.float32)
    middle_activation, back_b = jax.vjp(masked_piece, hid_a, norms[4], norms[5])
    low_b = middle_activation.astype(jnp.bfloat16).reshape(slots, sequence_rows, inner)
    tap_weights = stack_taps(low_b).reshape(rows, KERNEL_TAPS * inner)
    conv_flat = full_conv.reshape(KERNEL_TAPS * inner, inner)
    middle_hidden = jnp.dot(tap_weights, conv_flat, preferred_element_type=jnp.float32)
    act_c, back_c = jax.vjp(norm_piece, middle_hidden, norms[6], norms[7])
    low_c = act_c.astype(jnp.bfloat16)
    hid_c = jnp.dot(low_c, full_out, preferred_element_type=jnp.float32)
    mixed = (source + keep * hid_c).astype(jnp.bfloat16)
    upstream = cotangent.astype(jnp.float32)
    grad_c = (keep * upstream).astype(jnp.bfloat16)
    grad_out = contract_rows(low_c, grad_c)
    d_act_c = contract_cols(grad_c, full_out)
    d_hid_b, d_gain_c, d_bias_c = back_c(d_act_c)
    grad_b = d_hid_b.astype(jnp.bfloat16)
    grad_conv = contract_rows(tap_weights, grad_b).reshape(KERNEL_TAPS, inner, inner)
    d_taps = contract_cols(grad_b, conv_flat)
    d_act_b = unstack_taps(
        d_taps.reshape(slots, sequence_rows, KERNEL_TAPS, inner), sequence_rows
    ).reshape(rows, inner)
    d_hid_a, d_gain_b, d_bias_b = back_b(d_act_b)
    grad_a = d_hid_a.astype(jnp.bfloat16)
    grad_in = contract_rows(low_a, grad_a)
    d_act_a = contract_cols(grad_a, full_in)
    d_source, d_gain_a, d_bias_a = back_a(d_act_a)
    grad_tokens = (upstream + d_source).astype(jnp.bfloat16)
    grad_norms = jnp.concatenate(
        [
            d_gain_a.reshape(2, inner),
            d_bias_a.reshape(2, inner),
            d_gain_b[None],
            d_bias_b[None],
            d_gain_c[None],
            d_bias_c[None],
        ],
        axis=0,
    )
    sum_in, sum_conv, sum_out, sum_norms = reduce_grads(grad_in, grad_conv, grad_out, grad_norms)
    kinds = lax.broadcasted_iota(jnp.int32, (1, TYPES), 1)
    hits = (labels[:, None] == kinds) & valid
    local_counts = jnp.sum(hits.astype(jnp.int32), axis=0)
    type_counts = lax.psum(local_counts, ("dp", "fsdp"))
    new_in = adamw(w_in, mean_w_in, square_w_in, sum_in, 0.5 * D ** (-0.5), 0.01)
    new_conv = adamw(
        w_conv, mean_w_conv, square_w_conv, sum_conv, 0.5 * (KERNEL_TAPS * INNER) ** (-0.5), 0.01
    )
    new_out = adamw(w_out, mean_w_out, square_w_out, sum_out, 0.5 * (INNER // 2) ** (-0.5), 0.01)
    new_norm = adamw(norm_params, mean_norms, square_norms, sum_norms, 0.3, 0.0)
    return (
        mixed,
        grad_tokens,
        type_counts,
        new_in[0],
        new_conv[0],
        new_out[0],
        new_norm[0],
        new_in[1],
        new_conv[1],
        new_out[1],
        new_norm[1],
        new_in[2],
        new_conv[2],
        new_out[2],
        new_norm[2],
    )


F32, BF16 = jnp.float32, jnp.bfloat16
MESH = pl.DeviceIdType.MESH
DP_RANKS, PLANE = 4, 8
HALO = (KERNEL_TAPS // 2) * DILATION_STRIDE
GELU_SCALE, GELU_CUBE = 0.7978845608, 0.044715
BLOCK = 256
CONV_LANES = 256
NAMES = ("in", "conv", "out")


def dot_nn(a, b):
    return lax.dot_general(a, b, (((1,), (0,)), ((), ())), preferred_element_type=F32)


def dot_nt(a, b):
    return lax.dot_general(a, b, (((1,), (1,)), ((), ())), preferred_element_type=F32)


def dot_tn(a, b):
    return lax.dot_general(a, b, (((0,), (0,)), ((), ())), preferred_element_type=F32)


def gelu(z):
    t = jnp.tanh(z * (GELU_SCALE + (GELU_SCALE * GELU_CUBE) * (z * z)))
    h = 0.5 * z
    return h + h * t


def gelu_grad(z):
    zz = z * z
    t = jnp.tanh(z * (GELU_SCALE + (GELU_SCALE * GELU_CUBE) * zz))
    slope = z * (GELU_SCALE + (3.0 * GELU_SCALE * GELU_CUBE) * zz)
    return 0.5 * (1.0 + t + (1.0 - t * t) * slope)


def stats(x):
    c = x - jnp.mean(x, axis=-1, keepdims=True)
    r = lax.rsqrt(jnp.mean(c * c, axis=-1, keepdims=True) + EPSILON)
    return c * r, r


def loop(n, step, hooks=None):
    def one(i, carry):
        step(i)
        for at, calls in (hooks or {}).items():

            @pl.when(i == at)
            def _(calls=calls):
                for call in calls:
                    call()

        return carry

    lax.fori_loop(0, n, one, 0)


def once(step, i):
    step(i)


def block(i, n):
    return pl.ds(pl.multiple_of(i * n, n), n)


def round_up(n, m=128):
    return -(-n // m) * m


class Place:
    def __init__(self):
        self.d = lax.axis_index("dp")
        f = lax.axis_index("fsdp")
        self.f = f
        self.c, self.x, self.y = f % 2, (f // 2) % 2, f // 4
        self.oc, self.ox, self.oy = 1 - self.c, 1 - self.x, 1 - self.y
        self.ranks = [(self.d + j) % DP_RANKS for j in range(DP_RANKS)]
        self.sib = {"fsdp": f + 1 - 2 * self.c}
        self.xn = {"fsdp": f + 2 - 4 * self.x}
        self.yn = {"fsdp": f + 4 - 8 * self.y}
        self.zn = [{"dp": p} for p in self.ranks[1:]]


def barrier(pc):
    sem = pltpu.get_barrier_semaphore()
    peers = [pc.sib, pc.xn, pc.yn] + pc.zn
    for p in peers:
        pl.semaphore_signal(sem, inc=1, device_id=p, device_id_type=MESH)
    pl.semaphore_wait(sem, len(peers))


def remote(src, dst, send, recv, device):
    return pltpu.make_async_remote_copy(
        src_ref=src, dst_ref=dst, send_sem=send, recv_sem=recv, device_id=device, device_id_type=MESH
    )


def halves(name, shape):
    h, lanes = shape[-2:]
    if name == "out":
        return (slice(0, h // 2), slice(None)), (slice(h // 2, h), slice(None))
    cut = round_up(lanes // 2)
    return (slice(None), slice(0, cut)), (slice(None), slice(cut, lanes))


class Gather:
    SEMS = 13

    def __init__(self, pc, name, w, zr, send, recv):
        self.pc, self.w, self.zr, self.send, self.recv = pc, w, zr, send, recv
        self.name = name
        self.cut = halves(name, w.shape)
        self.sent = []

    def z(self, j):
        pc = self.pc
        mine = self.zr.at[pc.d]
        return remote(mine, mine, self.send.at[j - 1], self.recv.at[pc.d], pc.zn[j - 1])

    def z_in(self, j):
        pc = self.pc
        p = pc.ranks[j]
        return remote(self.zr.at[p], self.zr.at[p], self.send.at[j - 1], self.recv.at[p], pc.zn[j - 1])

    def start(self):
        for j in (2, 1, 3):
            self.z(j).start()

    def go(self, ref, i, device):
        c = remote(ref, ref, self.send.at[i], self.recv.at[i], device)
        c.start()
        self.sent.append((i, ref, device))

    def arrived(self, i, ref):
        remote(ref, ref, self.send.at[i], self.recv.at[i], self.pc.sib).wait_recv()

    def at(self, y, x, c, half=None):
        r = self.w.at[y, x, c]
        return r if half is None else r.at[self.cut[half]]

    def own(self):
        pc = self.pc
        for j in range(1, DP_RANKS):
            self.z_in(j).wait_recv()
        ASSEMBLE[self.name](self.w, self.zr, (pc.y, pc.x, pc.c))
        mine = self.at(pc.y, pc.x, pc.c)
        self.go(mine, 4, pc.xn)
        self.go(mine, 5, pc.yn)
        self.go(mine, 8, pc.sib)

    def from_x(self):
        pc = self.pc
        r = self.at(pc.y, pc.ox, pc.c)
        self.arrived(4, r)
        self.go(self.at(pc.y, pc.ox, pc.c, 1), 7, pc.yn)
        self.go(r, 9, pc.sib)

    def from_y(self):
        pc = self.pc
        r = self.at(pc.oy, pc.x, pc.c)
        self.arrived(5, r)
        self.go(self.at(pc.oy, pc.x, pc.c, 0), 6, pc.xn)
        self.go(r, 10, pc.sib)

    def from_diagonal(self):
        pc = self.pc
        for half in (0, 1):
            r = self.at(pc.oy, pc.ox, pc.c, half)
            self.arrived(6 + half, r)
            self.go(r, 11 + half, pc.sib)

    def from_sibling(self):
        pc = self.pc
        o = pc.oc
        self.arrived(8, self.at(pc.y, pc.x, o))
        self.arrived(9, self.at(pc.y, pc.ox, o))
        self.arrived(10, self.at(pc.oy, pc.x, o))
        for half in (0, 1):
            self.arrived(11 + half, self.at(pc.oy, pc.ox, o, half))

    def finish(self):
        for j in range(1, DP_RANKS):
            self.z(j).wait_send()
        for i, ref, device in self.sent:
            remote(ref, ref, self.send.at[i], self.recv.at[i], device).wait_send()


def assemble_in(w, zr, own):
    n = w.shape[-1] // DP_RANKS
    w[own] = jnp.concatenate([zr[i][:, :n] for i in range(DP_RANKS)], axis=1)


def assemble_conv(w, zr, own):
    n = w.shape[-1] // (DP_RANKS * KERNEL_TAPS)
    w[own] = jnp.concatenate(
        [zr[i][:, k * n : (k + 1) * n] for k in range(KERNEL_TAPS) for i in range(DP_RANKS)], axis=1
    )


def assemble_out(w, zr, own):
    n = w.shape[-1] // DP_RANKS
    h = zr.shape[1]
    for part in range(2):
        w[own + (slice(part * h, (part + 1) * h),)] = jnp.concatenate(
            [zr[i][:, part * n : (part + 1) * n] for i in range(DP_RANKS)], axis=1
        )


ASSEMBLE = {"in": assemble_in, "conv": assemble_conv, "out": assemble_out}


class Scatter:
    SEMS = 9

    def __init__(self, pc, name, g, rcv, r1a, r1b, r2a, r2b, zs, zr, send, recv):
        self.pc, self.name, self.g, self.rcv = pc, name, g, rcv
        self.r1a, self.r1b, self.r2a, self.r2b = r1a, r1b, r2a, r2b
        self.zs, self.zr, self.send, self.recv = zs, zr, send, recv
        self.cut = halves(name, g.shape)

    def copy(self, i, src, dst, device):
        return remote(src, dst, self.send.at[i], self.recv.at[i], device)

    def half(self, ref, k):
        return ref.at[(slice(None),) * (len(ref.shape) - 2) + self.cut[k]]

    def c0(self):
        pc = self.pc
        return self.copy(0, self.g.at[:, :, pc.oc], self.rcv, pc.sib)

    def a1(self):
        pc = self.pc
        return self.copy(1, self.half(self.g.at[:, pc.ox, pc.c], 0), self.r1a, pc.xn)

    def b1(self):
        pc = self.pc
        return self.copy(2, self.half(self.g.at[pc.oy, :, pc.c], 1), self.r1b, pc.yn)

    def a2(self):
        pc = self.pc
        return self.copy(3, self.half(self.g.at[pc.oy, pc.x, pc.c], 0), self.r2a, pc.yn)

    def b2(self):
        pc = self.pc
        return self.copy(4, self.half(self.g.at[pc.y, pc.ox, pc.c], 1), self.r2b, pc.xn)

    def z(self, j):
        pc = self.pc
        return remote(
            self.zs.at[pc.ranks[j]], self.zr.at[pc.d], self.send.at[4 + j], self.recv.at[5 + pc.d], pc.zn[j - 1]
        )

    def z_in(self, j):
        pc = self.pc
        p = pc.ranks[j]
        return remote(self.zs.at[p], self.zr.at[p], self.send.at[4 + j], self.recv.at[5 + p], pc.zn[j - 1])

    def start(self):
        self.c0().start()

    def step1(self):
        pc = self.pc
        self.c0().wait_recv()
        for y in range(2):
            for x in range(2):
                self.g[y, x, pc.c] = (self.g[y, x, pc.c].astype(F32) + self.rcv[y, x].astype(F32)).astype(BF16)
        self.a1().start()
        self.b1().start()

    def add(self, y, x, k, ref):
        idx = (y, x, self.pc.c) + self.cut[k]
        self.g[idx] = (self.g[idx].astype(F32) + ref[...].astype(F32)).astype(BF16)

    def step2(self):
        pc = self.pc
        self.a1().wait_recv()
        self.add(pc.oy, pc.x, 0, self.r1a.at[pc.oy])
        self.a2().start()
        self.b1().wait_recv()
        self.add(pc.y, pc.ox, 1, self.r1b.at[pc.ox])
        self.b2().start()
        self.add(pc.y, pc.x, 0, self.r1a.at[pc.y])
        self.add(pc.y, pc.x, 1, self.r1b.at[pc.x])

    def step3(self):
        pc = self.pc
        self.a2().wait_recv()
        self.add(pc.y, pc.x, 0, self.r2a)
        self.b2().wait_recv()
        self.add(pc.y, pc.x, 1, self.r2b)
        SPLIT[self.name](self.zs, self.g[pc.y, pc.x, pc.c])
        for j in (2, 1, 3):
            self.z(j).start()

    def step4(self, out):
        pc = self.pc
        total = self.zs[pc.d].astype(F32)
        for j in range(1, DP_RANKS):
            self.z_in(j).wait_recv()
            total = total + self.zr[pc.ranks[j]].astype(F32)
        out[...] = total

    def finish(self):
        for c in (self.c0(), self.a1(), self.b1(), self.a2(), self.b2()):
            c.wait_send()
        for j in range(1, DP_RANKS):
            self.z(j).wait_send()


def split_in(zs, v):
    n = v.shape[1] // DP_RANKS
    for i in range(DP_RANKS):
        zs[i, :, 0:n] = v[:, i * n : (i + 1) * n]


def split_conv(zs, v):
    n = v.shape[1] // (DP_RANKS * KERNEL_TAPS)
    for i in range(DP_RANKS):
        starts = [(DP_RANKS * k + i) * n for k in range(KERNEL_TAPS)]
        zs[i, :, 0 : KERNEL_TAPS * n] = jnp.concatenate([v[:, s : s + n] for s in starts], axis=1)


def split_out(zs, v):
    n = v.shape[1] // DP_RANKS
    h = zs.shape[1]
    for i in range(DP_RANKS):
        zs[i, :, 0 : 2 * n] = jnp.concatenate(
            [v[0:h, i * n : (i + 1) * n], v[h : 2 * h, i * n : (i + 1) * n]], axis=1
        )


SPLIT = {"in": split_in, "conv": split_conv, "out": split_out}


class NormGather:
    SEMS = 7

    def __init__(self, pc, nz, nw, send, recv):
        self.pc, self.nz, self.nw, self.send, self.recv = pc, nz, nw, send, recv

    def z(self, j, p):
        pc = self.pc
        return remote(self.nz.at[p], self.nz.at[p], self.send.at[j - 1], self.recv.at[p], pc.zn[j - 1])

    def start(self):
        for j in range(1, DP_RANKS):
            self.z(j, self.pc.d).start()

    def stage(self, k):
        pc = self.pc
        ref = (self.nw.at[pc.y, pc.x, pc.c], self.nw.at[pc.y, pc.x], self.nw.at[pc.y])[k]
        return remote(ref, ref, self.send.at[3 + k], self.recv.at[4 + k], (pc.sib, pc.xn, pc.yn)[k])

    def stage_in(self, k):
        pc = self.pc
        ref = (self.nw.at[pc.y, pc.x, pc.oc], self.nw.at[pc.y, pc.ox], self.nw.at[pc.oy])[k]
        return remote(ref, ref, self.send.at[3 + k], self.recv.at[4 + k], (pc.sib, pc.xn, pc.yn)[k])

    def own(self):
        pc = self.pc
        for j in range(1, DP_RANKS):
            self.z(j, pc.ranks[j]).wait_recv()
        self.nw[pc.y, pc.x, pc.c] = jnp.concatenate([self.nz[i][0:2] for i in range(DP_RANKS)], axis=0)
        self.stage(0).start()

    def next(self, k):
        self.stage_in(k).wait_recv()
        if k < 2:
            self.stage(k + 1).start()

    def whole(self, width):
        return jnp.concatenate([self.nw[f // 4, (f // 2) % 2, f % 2][:, 0:width] for f in range(PLANE)], axis=1)

    def finish(self):
        for j in range(1, DP_RANKS):
            self.z(j, self.pc.d).wait_send()
        for k in range(3):
            self.stage(k).wait_send()


class SmallSum:
    SEMS = 7

    def __init__(self, pc, acc, got, zgot, send, recv):
        self.pc, self.acc, self.got, self.zgot, self.send, self.recv = pc, acc, got, zgot, send, recv

    def stage(self, k):
        pc = self.pc
        return remote(
            self.acc.at[k], self.got.at[k], self.send.at[k], self.recv.at[4 + k], (pc.sib, pc.xn, pc.yn)[k]
        )

    def z(self, j):
        pc = self.pc
        return remote(self.acc.at[3], self.zgot.at[pc.d], self.send.at[2 + j], self.recv.at[pc.d], pc.zn[j - 1])

    def z_in(self, j):
        pc = self.pc
        p = pc.ranks[j]
        return remote(self.acc.at[3], self.zgot.at[p], self.send.at[2 + j], self.recv.at[p], pc.zn[j - 1])

    def start(self):
        self.stage(0).start()

    def next(self, k):
        self.stage(k).wait_recv()
        self.acc[k + 1] = self.acc[k] + self.got[k]
        if k < 2:
            self.stage(k + 1).start()
        else:
            for j in range(1, DP_RANKS):
                self.z(j).start()

    def total(self):
        for j in range(1, DP_RANKS):
            self.z_in(j).wait_recv()
        self.zgot[self.pc.d] = self.acc[3]
        return (self.zgot[0] + self.zgot[1]) + (self.zgot[2] + self.zgot[3])

    def finish(self):
        for k in range(3):
            self.stage(k).wait_send()
        for j in range(1, DP_RANKS):
            self.z(j).wait_send()


def norm_back(n, r, gain, bias, e, sums, row):
    dz = e * gelu_grad(n * gain + bias)
    width = n.shape[1]
    sums[row : row + 1, 0:width] += jnp.sum(dz * n, axis=0, keepdims=True)
    sums[row + 1 : row + 2, 0:width] += jnp.sum(dz, axis=0, keepdims=True)
    dn = dz * gain
    m1 = jnp.mean(dn, axis=-1, keepdims=True)
    m2 = jnp.mean(dn * n, axis=-1, keepdims=True)
    return r * (dn - m1 - n * m2)


def block_kernel(refs):
    r = refs
    pc = Place()
    tokens, cot_in, lens, labels = r.tokens, r.cot_in, r.lens, r.labels
    x, cot, act_a, n_b, act_c = r.x, r.cot, r.act_a, r.n_b, r.act_c
    scale, sums, tail_rows = r.scale, r.sums, r.tail
    b_even, b_odd, g_even, g_odd, back_t = r.b_even, r.b_odd, r.g_even, r.g_odd, r.back_t
    rows, width = x.shape
    inner = n_b.shape[1]
    slots = lens.shape[0]
    seq = rows // slots
    blocks = seq // BLOCK
    grad_a = act_c

    wide = {"in": r.w_in, "conv": r.w_conv, "out": r.w_out}
    gather = {n: Gather(pc, n, wide[n], getattr(r, "zg_" + n), getattr(r, "gs_" + n), getattr(r, "gr_" + n)) for n in NAMES}
    norm_gather = NormGather(pc, r.nz, r.nw, r.ns, r.nr)
    small = SmallSum(pc, r.sm_acc, r.sm_got, r.sm_z, r.sm_s, r.sm_r)

    load_x = pltpu.make_async_copy(tokens, x, r.io.at[0])
    load_cot = pltpu.make_async_copy(cot_in, cot, r.io.at[1])
    load_x.start()

    cols = r.p_in.shape[0]
    r.nz[pc.d, 0:2, 0:cols] = r.p_norms[...].astype(BF16).astype(F32)
    barrier(pc)
    norm_gather.start()
    r.zg_in[pc.d, :, 0 : r.p_in.shape[1]] = r.p_in[...].astype(BF16)
    gather["in"].start()
    depth = r.p_conv.shape[1]
    for k in range(KERNEL_TAPS):
        r.zg_conv[pc.d, :, k * depth : (k + 1) * depth] = r.p_conv[k].T.astype(BF16)
    p_out = r.p_out[...].T.astype(BF16)
    h_out = r.zg_out.shape[1]
    r.zg_out[pc.d, :, 0 : 2 * depth] = jnp.concatenate([p_out[0:h_out], p_out[h_out : 2 * h_out]], axis=1)

    sums[...] = jnp.zeros_like(sums)
    pad = jnp.zeros((HALO, inner), BF16)
    for s in range(slots):
        for buf in (b_even, g_even):
            buf[s, 0:HALO, :] = pad
            buf[s, seq + HALO : seq + 2 * HALO, :] = pad

    def kept(s, first, count):
        return first + lax.broadcasted_iota(jnp.int32, (count, 1), 0) < lens[s]

    lab = labels[...]
    place = (
        lax.broadcasted_iota(jnp.int32, lab.shape, 0) * lab.shape[1] + lax.broadcasted_iota(jnp.int32, lab.shape, 1)
    )
    valid = place < 0
    for s in range(slots):
        valid = valid | ((place >= s * seq) & (place < s * seq + lens[s]))
    lane = lax.broadcasted_iota(jnp.int32, (1, inner), 1)
    counts = jnp.zeros((1, inner), F32)
    for c in range(TYPES):
        hits = jnp.sum(jnp.where(valid & (lab == c), 1.0, 0.0), keepdims=True)
        counts = counts + jnp.where(lane == c, hits, 0.0)

    load_x.wait()
    load_cot.start()
    strip = BLOCK // 2

    def first_stats(i):
        at = block(i, strip)
        n, rs = stats(x[at, :].astype(F32))
        x[at, :] = n.astype(BF16)
        scale[at, 0:1] = rs

    loop(rows // strip, first_stats)
    norm_gather.own()
    gather["in"].own()
    gather["conv"].start()
    for k in range(3):
        norm_gather.next(k)
    r.norms[...] = norm_gather.whole(cols)
    norms = r.norms
    gain_a = jnp.concatenate([norms[0:1, :], norms[1:2, :]], axis=1)
    bias_a = jnp.concatenate([norms[2:3, :], norms[3:4, :]], axis=1)
    gain_b, bias_b, gain_c, bias_c = (norms[i : i + 1, :] for i in range(4, 8))

    def first_act(i):
        at = block(i, strip)
        act_a[at, :] = gelu(x[at, :].astype(F32) * gain_a + bias_a).astype(BF16)

    half_way = rows // strip // 2
    loop(half_way, first_act)
    gather["in"].from_x()
    gather["in"].from_y()
    loop(half_way, lambda i: first_act(i + half_way))
    gather["in"].from_diagonal()
    gather["conv"].own()
    gather["out"].start()
    gather["in"].from_sibling()
    w_in = r.w_in
    w_conv = r.w_conv
    w_out = r.w_out

    def flat(w):
        v = w[...]
        return v.reshape(PLANE * v.shape[3], v.shape[4])

    def shifted_store(even, odd, s, i, value):
        even[s, pl.ds(pl.multiple_of(i * BLOCK + HALO, 16), BLOCK), :] = value.astype(BF16)
        before = jnp.where(i == 0, 0.0, tail_rows[...])
        late = value[BLOCK - 8 :]
        odd[s, block(i, BLOCK), :] = jnp.concatenate([before, value[: BLOCK - 8]], axis=0).astype(BF16)
        odd[s, pl.ds(pl.multiple_of((i + 1) * BLOCK, 16), 16), :] = jnp.concatenate(
            [late, jnp.zeros_like(late)], axis=0
        ).astype(BF16)
        tail_rows[...] = late

    def taps(even, odd, s, first, count, sign):
        out = []
        for k in range(KERNEL_TAPS):
            off = sign * DILATION_STRIDE * (k - KERNEL_TAPS // 2)
            buf, base = (even, HALO) if off % 16 == 0 else (odd, 8)
            at = base + off + first
            at = at if isinstance(at, int) else pl.multiple_of(at, 16)
            out.append(buf[s, pl.ds(at, count), :])
        return out

    def second(s, i):
        at = pl.ds(pl.multiple_of(s * seq + i * BLOCK, BLOCK), BLOCK)
        n, rs = stats(dot_nt(act_a[at, :], flat(w_in)))
        n_b[at, :] = n.astype(BF16)
        scale[at, 1:2] = rs
        a = jnp.where(kept(s, i * BLOCK, BLOCK), gelu(n * gain_b + bias_b), 0.0)
        shifted_store(b_even, b_odd, s, i, a)

    for s in range(slots):
        hooks = {blocks - 1: [gather["conv"].from_x, gather["conv"].from_y]} if s == 0 else None
        loop(blocks, functools.partial(second, s), hooks)
    gather["conv"].from_diagonal()
    gather["out"].own()
    gather["conv"].from_sibling()

    def phase_three(n_c, token_rows):
        def third(s, i):
            at = pl.ds(pl.multiple_of(s * seq + i * BLOCK, BLOCK), BLOCK)
            stacked = jnp.concatenate(taps(b_even, b_odd, s, i * BLOCK, BLOCK, 1), axis=1)
            n, rs = stats(dot_nt(stacked, flat(w_conv)))
            n_c[at, :] = n.astype(BF16)
            scale[at, 2:3] = rs
            act_c[at, :] = jnp.where(kept(s, i * BLOCK, BLOCK), gelu(n * gain_c + bias_c), 0.0).astype(BF16)

        for s in range(slots):
            hooks = (
                {1: [gather["out"].from_x, gather["out"].from_y], blocks - 1: [gather["out"].from_diagonal]}
                if s == slots - 1
                else None
            )
            loop(blocks, functools.partial(third, s), hooks)
        gather["out"].from_sibling()

        def mixed_copy(j):
            k = lax.rem(j, 3)
            return pltpu.make_async_copy(token_rows.at[k], r.mixed.at[block(j, BLOCK), :], r.io.at[2 + k])

        def token_copy(j):
            k = lax.rem(j, 3)
            return pltpu.make_async_copy(tokens.at[block(j, BLOCK), :], token_rows.at[k], r.io.at[5 + k])

        token_copy(0).start()

        def fourth(s, i):
            j = s * blocks + i
            at = block(j, BLOCK)
            last = slots * blocks - 1

            @pl.when(j >= 2)
            def _():
                mixed_copy(j - 2).wait()

            @pl.when(j < last)
            def _():
                token_copy(j + 1).start()

            k = lax.rem(j, 3)
            hid_c = dot_nt(act_c[at, :], flat(w_out))
            token_copy(j).wait()
            token_rows[k] = (token_rows[k].astype(F32) + hid_c).astype(BF16)
            mixed_copy(j).start()
            e = jnp.where(kept(s, i * BLOCK, BLOCK), dot_nn(cot[at, :], flat(w_out)), 0.0)
            back = norm_back(n_c[at, :].astype(F32), scale[at, 2:3], gain_c, bias_c, e, sums, 4)
            shifted_store(g_even, g_odd, s, i, back)
            back_t[:, at] = back.astype(BF16).T

        load_cot.wait()
        for s in range(slots):
            loop(blocks, functools.partial(fourth, s))
        mixed_copy(slots * blocks - 2).wait()
        mixed_copy(slots * blocks - 1).wait()

        chunk = 256
        tall = r.g_out.shape[3]

        def out_grad(lo):
            part = dot_tn(cot[:, lo : lo + chunk], act_c[...]).astype(BF16)
            for f in range(lo // tall, -(-(lo + chunk) // tall)):
                a, b = max(lo, f * tall), min(lo + chunk, (f + 1) * tall)
                r.g_out[f // 4, (f // 2) % 2, f % 2, a - f * tall : b - f * tall, :] = part[a - lo : b - lo]

        for lo in range(0, width, chunk):
            once(out_grad, lo)

    pl.run_scoped(
        phase_three,
        pltpu.VMEM((rows, inner), BF16),
        pltpu.VMEM((3, BLOCK, width), BF16),
    )

    def scatter_of(n, g):
        return Scatter(
            pc, n, g, getattr(r, "rcv_" + n), getattr(r, "r1a_" + n), getattr(r, "r1b_" + n), getattr(r, "r2a_" + n), getattr(r, "r2b_" + n), getattr(r, "zg_" + n),
            getattr(r, "zr_" + n), getattr(r, "ss_" + n), getattr(r, "sr_" + n),
        )

    for c in [norm_gather] + [gather[n] for n in NAMES]:
        c.finish()

    def phase_five(g_in, g_conv):
        sc_out = scatter_of("out", r.g_out)
        sc_conv = scatter_of("conv", g_conv)
        sc_in = scatter_of("in", g_in)
        sc_out.start()
        def conv_grad(k):
            off = DILATION_STRIDE * (k - KERNEL_TAPS // 2)
            buf, base = (b_even, HALO) if off % 16 == 0 else (b_odd, 8)
            for lo in range(0, inner, CONV_LANES):
                hi = min(lo + CONV_LANES, inner)
                total = None
                for s in range(slots):
                    p = dot_nn(back_t[:, s * seq : (s + 1) * seq], buf[s, base + off : base + off + seq, lo:hi])
                    total = p if total is None else total + p
                g_conv[:, :, :, :, k * inner + lo : k * inner + hi] = total.astype(BF16).reshape(
                    (2, 2, 2, inner // PLANE, hi - lo)
                )

        for k in range(KERNEL_TAPS):
            once(conv_grad, k)
            if k == 1:
                sc_out.step1()
        sc_conv.start()

        def sixth(s, i):
            at = block(s * blocks + i, BLOCK)
            xs = taps(g_even, g_odd, s, i * BLOCK, BLOCK, -1)
            e = None
            for k in range(KERNEL_TAPS):
                wk = w_conv[:, :, :, :, k * inner : (k + 1) * inner].reshape(inner, inner)
                p = dot_nn(xs[k], wk)
                e = p if e is None else e + p
            e = jnp.where(kept(s, i * BLOCK, BLOCK), e, 0.0)
            back = norm_back(n_b[at, :].astype(F32), scale[at, 1:2], gain_b, bias_b, e, sums, 2).astype(BF16)
            grad_a[at, :] = back
            back_t[:, at] = back.T

        for s in range(slots):
            if s == 0:
                hooks = {0: [sc_out.step2], 1: [sc_conv.step1], blocks - 1: [sc_out.step3]}
            else:
                hooks = {1: [lambda: sc_out.step4(r.s_out)], blocks - 1: [sc_conv.step2]}
            loop(blocks, functools.partial(sixth, s), hooks)

        chunk = 256
        n_chunks = width // chunk

        def in_grad(j):
            part = dot_nn(back_t[...], act_a[:, j * chunk : (j + 1) * chunk]).astype(BF16)
            g_in[:, :, :, :, j * chunk : (j + 1) * chunk] = part.reshape(2, 2, 2, inner // PLANE, chunk)

        for j in range(n_chunks):
            once(in_grad, j)
        sc_in.start()

        def out_copy(at):
            return pltpu.make_async_copy(cot.at[at, :], r.grad_tokens.at[at, :], r.io.at[8])

        def eighth(i):
            at = block(i, BLOCK)
            e = dot_nn(grad_a[at, :], flat(w_in))
            back = norm_back(x[at, :].astype(F32), scale[at, 0:1], gain_a, bias_a, e, sums, 0)
            cot[at, :] = (cot[at, :].astype(F32) + back).astype(BF16)
            out_copy(at).start()

        n_eight = rows // BLOCK
        hooks = {
            0: [sc_in.step1],
            1: [sc_conv.step3],
            3: [sc_in.step2],
            5: [lambda: sc_conv.step4(r.s_conv)],
            6: [sc_in.step3],
        }
        loop(n_eight, eighth, hooks)
        first = small.acc
        first[0] = jnp.concatenate(
            [
                sums[0:1, 0:inner],
                sums[0:1, inner : 2 * inner],
                sums[1:2, 0:inner],
                sums[1:2, inner : 2 * inner],
                sums[2:6, 0:inner],
                counts,
                jnp.zeros((7, inner), F32),
            ],
            axis=0,
        )
        small.start()
        sc_in.step4(r.s_in)
        for k in range(3):
            small.next(k)
        total = small.total()
        r.s_counts[...] = total[8:16, 0:128]
        mine = jnp.zeros((8, cols), F32)
        for f in range(PLANE):
            mine = mine + jnp.where(pc.f == f, total[0:8, f * cols : (f + 1) * cols], 0.0)
        pair = jnp.zeros((2, cols), F32)
        for i in range(DP_RANKS):
            pair = pair + jnp.where(pc.d == i, mine[2 * i : 2 * i + 2], 0.0)
        r.s_norms[...] = pair
        for c in (sc_out, sc_conv, sc_in, small):
            c.finish()
        pltpu.make_async_copy(cot, r.grad_tokens, r.io.at[8]).wait()

    pl.run_scoped(
        phase_five,
        pltpu.VMEM(r.w_in.shape, BF16),
        pltpu.VMEM(r.w_conv.shape, BF16),
    )


def run_block(tokens, cotangent, lengths, labels, w_in, w_conv, w_out, norm_params):
    rows, width = tokens.shape
    cols, rank_in = w_in.shape
    depth = w_conv.shape[1]
    inner = cols * PLANE
    slots = lengths.shape[0]
    seq = rows // slots
    V = pltpu.VMEM
    dma = pltpu.SemaphoreType.DMA
    shapes = {
        "in": (cols, width, cols, round_up(rank_in)),
        "conv": (cols, KERNEL_TAPS * inner, cols, round_up(KERNEL_TAPS * depth)),
        "out": (w_out.shape[1], inner, w_out.shape[1] // 2, round_up(2 * depth)),
    }
    inputs = dict(
        lens=(lengths, pltpu.SMEM),
        tokens=(tokens, pl.ANY),
        cot_in=(cotangent, pl.ANY),
        labels=(labels.reshape(rows // 128, 128), V),
        p_in=(w_in, V),
        p_conv=(w_conv, V),
        p_out=(w_out, V),
        p_norms=(norm_params, V),
    )
    outputs = dict(
        mixed=((rows, width), BF16, pl.ANY),
        grad_tokens=((rows, width), BF16, pl.ANY),
        s_counts=((8, 128), F32, V),
        s_norms=(norm_params.shape, F32, V),
    )
    scratch = dict(
        x=V((rows, width), BF16),
        cot=V((rows, width), BF16),
        act_a=V((rows, width), BF16),
        n_b=V((rows, inner), BF16),
        act_c=V((rows, inner), BF16),
        scale=V((rows, 8), F32),
        sums=V((8, width), F32),
        tail=V((8, inner), F32),
        norms=V((8, inner), F32),
        back_t=V((inner, rows), BF16),
        io=dma((9,)),
        nz=V((DP_RANKS, 8, 128), F32),
        nw=V((2, 2, 2, 8, 128), F32),
        ns=dma((NormGather.SEMS,)),
        nr=dma((NormGather.SEMS,)),
        sm_acc=V((4, 16, inner), F32),
        sm_got=V((3, 16, inner), F32),
        sm_z=V((DP_RANKS, 16, inner), F32),
        sm_s=dma((SmallSum.SEMS,)),
        sm_r=dma((SmallSum.SEMS,)),
        g_out=V((2, 2, 2) + shapes["out"][:2], BF16),
    )
    halo_rows = V((slots, seq + 2 * HALO, inner), BF16)
    scratch.update(b_even=halo_rows, b_odd=halo_rows, g_even=halo_rows, g_odd=halo_rows)
    for n, (h, lanes, hz, lz) in shapes.items():
        outputs["s_" + n] = ((hz, lz), F32, V)
        size = [
            tuple(len(range(*c.indices(e))) for c, e in zip(cut, (h, lanes))) for cut in halves(n, (h, lanes))
        ]
        scratch["w_" + n] = V((2, 2, 2, h, lanes), BF16)
        scratch["zg_" + n] = V((DP_RANKS, hz, lz), BF16)
        scratch["gs_" + n] = dma((Gather.SEMS,))
        scratch["gr_" + n] = dma((Gather.SEMS,))
        scratch["rcv_" + n] = V((2, 2, h, lanes), BF16)
        scratch["r1a_" + n] = V((2,) + size[0], BF16)
        scratch["r1b_" + n] = V((2,) + size[1], BF16)
        scratch["r2a_" + n] = V(size[0], BF16)
        scratch["r2b_" + n] = V(size[1], BF16)
        scratch["zr_" + n] = V((DP_RANKS, hz, lz), BF16)
        scratch["ss_" + n] = dma((Scatter.SEMS,))
        scratch["sr_" + n] = dma((Scatter.SEMS,))
    names = list(inputs) + list(outputs) + list(scratch)
    work = 6 * rows * (2 * width * inner + KERNEL_TAPS * inner * inner)
    out = pl.pallas_call(
        lambda *refs: block_kernel(SimpleNamespace(**dict(zip(names, refs)))),
        out_shape=tuple(jax.ShapeDtypeStruct(s, t) for s, t, _ in outputs.values()),
        in_specs=[pl.BlockSpec(memory_space=m) for _, m in inputs.values()],
        out_specs=tuple(pl.BlockSpec(memory_space=m) for _, _, m in outputs.values()),
        scratch_shapes=list(scratch.values()),
        compiler_params=pltpu.CompilerParams(
            collective_id=0, has_side_effects=True, vmem_limit_bytes=VMEM_BYTES
        ),
        cost_estimate=pl.CostEstimate(flops=work, bytes_accessed=8 * rows * width, transcendentals=0),
        name="residual_block",
    )(*(a for a, _ in inputs.values()))
    return dict(zip(outputs, out))


VMEM_BYTES = 63 * 1024 * 1024


def finish_kernel(n_copies, refs):
    r = refs
    rows = r.mixed.shape[0] // n_copies
    come, go = [], []
    for i in range(n_copies):
        for src, mid, dst in ((r.mixed, r.hold_mixed, r.new_mixed), (r.grad_tokens, r.hold_grad, r.new_grad_tokens)):
            at = pl.ds(i * rows, rows)
            sem = r.big_sem.at[len(come)]
            come.append(pltpu.make_async_copy(src.at[at, :], mid.at[at, :], sem))
            go.append(pltpu.make_async_copy(mid.at[at, :], dst.at[at, :], sem))
    loads = {}
    for n in STEP_ORDER:
        for kind in ("s_", "w_", "m_", "v_"):
            k = kind + n
            loads[k] = pltpu.make_async_copy(getattr(r, k), getattr(r, "b" + k), r.in_sem.at[len(loads)])
            loads[k].start()
    loads["s_counts"] = pltpu.make_async_copy(r.s_counts, r.bs_counts, r.in_sem.at[len(loads)])
    loads["s_counts"].start()
    for c in come:
        c.start()
    stores = []

    def pass_on(first, last):
        for c, g in zip(come[first:last], go[first:last]):
            c.wait()
            g.start()

    def store(k):
        stores.append(pltpu.make_async_copy(getattr(r, "o" + k), getattr(r, "n" + k), r.out_sem.at[len(stores)]))
        stores[-1].start()

    def step(n, at, grad, rate, decay):
        new = adamw(getattr(r, "bw_" + n)[at], getattr(r, "bm_" + n)[at], getattr(r, "bv_" + n)[at], grad, rate, decay)
        for kind, value in zip(("ow_", "om_", "ov_"), new):
            getattr(r, kind + n)[at] = value

    def ready(n):
        for kind in ("s_", "w_", "m_", "v_"):
            loads[kind + n].wait()

    def done(n):
        for kind in ("w_", "m_", "v_"):
            store(kind + n)

    everything = (slice(None), slice(None))
    ready("conv")
    depth = r.bw_conv.shape[1]
    for k in range(KERNEL_TAPS):
        grad = r.bs_conv[:, k * depth : (k + 1) * depth].T
        step("conv", (k,), grad, 0.5 * (KERNEL_TAPS * INNER) ** (-0.5), 0.01)
    done("conv")
    pass_on(0, n_copies)
    ready("in")
    step("in", everything, r.bs_in[:, 0 : r.bw_in.shape[1]], 0.5 * D ** (-0.5), 0.01)
    done("in")
    ready("out")
    flat = r.bs_out[...]
    grad = jnp.concatenate([flat[:, 0:depth].T, flat[:, depth : 2 * depth].T], axis=1)
    step("out", everything, grad, 0.5 * (INNER // 2) ** (-0.5), 0.01)
    done("out")
    ready("norms")
    step("norms", everything, r.bs_norms[...], 0.3, 0.0)
    done("norms")
    pass_on(n_copies, 2 * n_copies)
    loads["s_counts"].wait()
    r.type_counts[...] = r.bs_counts[0, 0:TYPES].astype(jnp.int32)
    for c in stores + go:
        c.wait()


STEP_ORDER = ("conv", "in", "out", "norms")
BIG_COPIES = 4


def run_finish(res, weights, means, squares):
    V, dma = pltpu.VMEM, pltpu.SemaphoreType.DMA
    inputs = {k: res[k] for k in ("mixed", "grad_tokens", "s_counts")}
    for n in STEP_ORDER:
        inputs["s_" + n] = res["s_" + n]
        for kind, arrays in (("w_", weights), ("m_", means), ("v_", squares)):
            inputs[kind + n] = arrays[n]
    outputs = {"new_" + k: res[k] for k in ("mixed", "grad_tokens")}
    for kind in ("w_", "m_", "v_"):
        for n in ("in", "conv", "out", "norms"):
            outputs["n" + kind + n] = weights[n]
    scratch = {}
    for k, a in inputs.items():
        if k[1] == "_":
            scratch["b" + k] = V(a.shape, a.dtype)
    for k, a in outputs.items():
        if k[2] == "_":
            scratch["o" + k[1:]] = V(a.shape, a.dtype)
    whole = V(res["mixed"].shape, BF16)
    scratch.update(hold_mixed=whole, hold_grad=whole)
    scratch.update(in_sem=dma((17,)), out_sem=dma((12,)), big_sem=dma((2 * BIG_COPIES,)))
    shapes = [jax.ShapeDtypeStruct(a.shape, a.dtype) for a in outputs.values()]
    names = list(inputs) + list(outputs) + ["type_counts"] + list(scratch)
    hbm = pl.BlockSpec(memory_space=pl.ANY)
    out = pl.pallas_call(
        lambda *refs: finish_kernel(BIG_COPIES, SimpleNamespace(**dict(zip(names, refs)))),
        out_shape=tuple(shapes) + (jax.ShapeDtypeStruct((TYPES,), jnp.int32),),
        in_specs=[hbm] * len(inputs),
        out_specs=(hbm,) * len(outputs) + (pl.BlockSpec(memory_space=V),),
        scratch_shapes=list(scratch.values()),
        compiler_params=pltpu.CompilerParams(vmem_limit_bytes=VMEM_BYTES),
        name="finish",
    )(*inputs.values())
    return out


def fused_body(
    tokens,
    cotangent,
    lengths,
    labels,
    w_in,
    w_conv,
    w_out,
    norm_params,
    mean_w_in,
    mean_w_conv,
    mean_w_out,
    mean_norms,
    square_w_in,
    square_w_conv,
    square_w_out,
    square_norms,
):
    res = run_block(tokens, cotangent, lengths, labels, w_in.T, w_conv, w_out, norm_params)
    new = run_finish(
        res,
        dict(zip(NAMES + ("norms",), (w_in.T, w_conv, w_out, norm_params))),
        dict(zip(NAMES + ("norms",), (mean_w_in.T, mean_w_conv, mean_w_out, mean_norms))),
        dict(zip(NAMES + ("norms",), (square_w_in.T, square_w_conv, square_w_out, square_norms))),
    )
    mixed, grad_tokens, *steps, counts = new
    for i in (0, 4, 8):
        steps[i] = steps[i].T
    return (mixed, grad_tokens, counts) + tuple(steps)


def solution(mesh):
    fused = mesh.shape["dp"] == DP_RANKS and mesh.shape["fsdp"] == PLANE
    return jax.shard_map(
        fused_body if fused else plain_body,
        mesh=mesh,
        in_specs=(
            P(("dp", "fsdp"), None),
            P(("dp", "fsdp"), None),
            P(("dp", "fsdp")),
            P(("dp", "fsdp")),
            P("dp", "fsdp"),
            P(None, "dp", "fsdp"),
            P("dp", "fsdp"),
            P("dp", "fsdp"),
            P("dp", "fsdp"),
            P(None, "dp", "fsdp"),
            P("dp", "fsdp"),
            P("dp", "fsdp"),
            P("dp", "fsdp"),
            P(None, "dp", "fsdp"),
            P("dp", "fsdp"),
            P("dp", "fsdp"),
        ),
        out_specs=(
            P(("dp", "fsdp"), None),
            P(("dp", "fsdp"), None),
            P(),
            P("dp", "fsdp"),
            P(None, "dp", "fsdp"),
            P("dp", "fsdp"),
            P("dp", "fsdp"),
            P("dp", "fsdp"),
            P(None, "dp", "fsdp"),
            P("dp", "fsdp"),
            P("dp", "fsdp"),
            P("dp", "fsdp"),
            P(None, "dp", "fsdp"),
            P("dp", "fsdp"),
            P("dp", "fsdp"),
        ),
        check_vma=False,
    )
```

```python
import functools
from types import SimpleNamespace

import jax
import jax.numpy as jnp
from jax import lax
from jax.experimental import pallas as pl
from jax.experimental.pallas import tpu as pltpu
from jax.sharding import PartitionSpec as P

D = 1280
INNER = 640
KERNEL_TAPS = 5
DILATION_STRIDE = 8
TYPES = 25
STEP = 5


EPSILON = 1e-05


def plain_normalize(value, gain, bias):
    center = value - jnp.mean(value, axis=-1, keepdims=True)
    spread = jnp.mean(center * center, axis=-1, keepdims=True)
    return center * lax.rsqrt(spread + EPSILON) * gain + bias


def activate(value):
    return jax.nn.gelu(value, approximate=True)


def norm_piece(value, gain, bias):
    return activate(plain_normalize(value, gain, bias))


def gather_params(first, second, third, fourth):
    part = (
        lax.all_gather(first, "fsdp", axis=1, tiled=True),
        lax.all_gather(second, "fsdp", axis=2, tiled=True),
        lax.all_gather(third, "fsdp", axis=1, tiled=True),
        lax.all_gather(fourth, "fsdp", axis=1, tiled=True),
    )
    return (
        lax.all_gather(part[0], "dp", axis=0, tiled=True),
        lax.all_gather(part[1], "dp", axis=1, tiled=True),
        lax.all_gather(part[2], "dp", axis=0, tiled=True),
        lax.all_gather(part[3], "dp", axis=0, tiled=True),
    )


def reduce_grads(first, second, third, fourth):
    part = (
        lax.psum_scatter(first, "fsdp", scatter_dimension=1, tiled=True),
        lax.psum_scatter(second, "fsdp", scatter_dimension=2, tiled=True),
        lax.psum_scatter(third, "fsdp", scatter_dimension=1, tiled=True),
        lax.psum_scatter(fourth, "fsdp", scatter_dimension=1, tiled=True),
    )
    return (
        lax.psum_scatter(
            part[0].astype(jnp.bfloat16), "dp", scatter_dimension=0, tiled=True
        ).astype(jnp.float32),
        lax.psum_scatter(
            part[1].astype(jnp.bfloat16), "dp", scatter_dimension=1, tiled=True
        ).astype(jnp.float32),
        lax.psum_scatter(
            part[2].astype(jnp.bfloat16), "dp", scatter_dimension=0, tiled=True
        ).astype(jnp.float32),
        lax.psum_scatter(
            part[3].astype(jnp.bfloat16), "dp", scatter_dimension=0, tiled=True
        ).astype(jnp.float32),
    )


def stack_taps(value_rows):
    sequence_rows = value_rows.shape[1]
    half_width = KERNEL_TAPS // 2
    padded_input = jnp.pad(
        value_rows, ((0, 0), (half_width * DILATION_STRIDE, half_width * DILATION_STRIDE), (0, 0))
    )
    return jnp.concatenate(
        [
            padded_input[
                :, tap_index * DILATION_STRIDE : tap_index * DILATION_STRIDE + sequence_rows
            ]
            for tap_index in range(KERNEL_TAPS)
        ],
        axis=-1,
    )


def unstack_taps(gradient_tree, sequence_rows):
    half_width = KERNEL_TAPS // 2
    padded_input = jnp.pad(
        gradient_tree,
        ((0, 0), (half_width * DILATION_STRIDE, half_width * DILATION_STRIDE), (0, 0), (0, 0)),
    )
    total_count = padded_input[
        :, 2 * half_width * DILATION_STRIDE : 2 * half_width * DILATION_STRIDE + sequence_rows, 0
    ]
    for tap_index in range(1, KERNEL_TAPS):
        start_offset = (2 * half_width - tap_index) * DILATION_STRIDE
        total_count = (
            total_count + padded_input[:, start_offset : start_offset + sequence_rows, tap_index]
        )
    return total_count


def adamw(master, mean_old, square_old, grad, rate, decay):
    mean_new = 0.5 * mean_old + 0.5 * grad
    square_new = 0.6 * square_old + 0.4 * grad * grad
    mean_hat = mean_new / (1.0 - 0.5**STEP)
    square_hat = square_new / (1.0 - 0.6**STEP)
    weight = master - rate * (mean_hat / (jnp.sqrt(square_hat) + 1e-08) + decay * master)
    return (weight, mean_new, square_new)


def contract_rows(left, right):
    return lax.dot_general(
        left, right, (((0,), (0,)), ((), ())), preferred_element_type=jnp.float32
    )


def contract_cols(left, right):
    return lax.dot_general(
        left, right, (((1,), (1,)), ((), ())), preferred_element_type=jnp.float32
    )


def plain_body(
    tokens,
    cotangent,
    lengths,
    labels,
    w_in,
    w_conv,
    w_out,
    norm_params,
    mean_w_in,
    mean_w_conv,
    mean_w_out,
    mean_norms,
    square_w_in,
    square_w_conv,
    square_w_out,
    square_norms,
):
    slots = lengths.shape[0]
    rows = tokens.shape[0]
    sequence_rows = rows // slots
    places = lax.broadcasted_iota(jnp.int32, (slots, sequence_rows), 1)
    valid = (places < lengths[:, None]).reshape(rows, 1)
    keep = valid.astype(jnp.float32)
    full_in, full_conv, full_out, full_norms = gather_params(
        w_in.astype(jnp.bfloat16),
        w_conv.astype(jnp.bfloat16),
        w_out.astype(jnp.bfloat16),
        norm_params.astype(jnp.bfloat16),
    )
    inner = full_in.shape[1]
    norms = full_norms.astype(jnp.float32)
    gain_a = norms[0:2].reshape(2 * inner)
    bias_a = norms[2:4].reshape(2 * inner)
    source = tokens.astype(jnp.float32)

    def masked_piece(value, gain, bias):
        return norm_piece(value, gain, bias) * keep

    act_a, back_a = jax.vjp(norm_piece, source, gain_a, bias_a)
    low_a = act_a.astype(jnp.bfloat16)
    hid_a = jnp.dot(low_a, full_in, preferred_element_type=jnp.float32)
    middle_activation, back_b = jax.vjp(masked_piece, hid_a, norms[4], norms[5])
    low_b = middle_activation.astype(jnp.bfloat16).reshape(slots, sequence_rows, inner)
    tap_weights = stack_taps(low_b).reshape(rows, KERNEL_TAPS * inner)
    conv_flat = full_conv.reshape(KERNEL_TAPS * inner, inner)
    middle_hidden = jnp.dot(tap_weights, conv_flat, preferred_element_type=jnp.float32)
    act_c, back_c = jax.vjp(norm_piece, middle_hidden, norms[6], norms[7])
    low_c = act_c.astype(jnp.bfloat16)
    hid_c = jnp.dot(low_c, full_out, preferred_element_type=jnp.float32)
    mixed = (source + keep * hid_c).astype(jnp.bfloat16)
    upstream = cotangent.astype(jnp.float32)
    grad_c = (keep * upstream).astype(jnp.bfloat16)
    grad_out = contract_rows(low_c, grad_c)
    d_act_c = contract_cols(grad_c, full_out)
    d_hid_b, d_gain_c, d_bias_c = back_c(d_act_c)
    grad_b = d_hid_b.astype(jnp.bfloat16)
    grad_conv = contract_rows(tap_weights, grad_b).reshape(KERNEL_TAPS, inner, inner)
    d_taps = contract_cols(grad_b, conv_flat)
    d_act_b = unstack_taps(
        d_taps.reshape(slots, sequence_rows, KERNEL_TAPS, inner), sequence_rows
    ).reshape(rows, inner)
    d_hid_a, d_gain_b, d_bias_b = back_b(d_act_b)
    grad_a = d_hid_a.astype(jnp.bfloat16)
    grad_in = contract_rows(low_a, grad_a)
    d_act_a = contract_cols(grad_a, full_in)
    d_source, d_gain_a, d_bias_a = back_a(d_act_a)
    grad_tokens = (upstream + d_source).astype(jnp.bfloat16)
    grad_norms = jnp.concatenate(
        [
            d_gain_a.reshape(2, inner),
            d_bias_a.reshape(2, inner),
            d_gain_b[None],
            d_bias_b[None],
            d_gain_c[None],
            d_bias_c[None],
        ],
        axis=0,
    )
    sum_in, sum_conv, sum_out, sum_norms = reduce_grads(grad_in, grad_conv, grad_out, grad_norms)
    kinds = lax.broadcasted_iota(jnp.int32, (1, TYPES), 1)
    hits = (labels[:, None] == kinds) & valid
    local_counts = jnp.sum(hits.astype(jnp.int32), axis=0)
    type_counts = lax.psum(local_counts, ("dp", "fsdp"))
    new_in = adamw(w_in, mean_w_in, square_w_in, sum_in, 0.5 * D ** (-0.5), 0.01)
    new_conv = adamw(
        w_conv, mean_w_conv, square_w_conv, sum_conv, 0.5 * (KERNEL_TAPS * INNER) ** (-0.5), 0.01
    )
    new_out = adamw(w_out, mean_w_out, square_w_out, sum_out, 0.5 * (INNER // 2) ** (-0.5), 0.01)
    new_norm = adamw(norm_params, mean_norms, square_norms, sum_norms, 0.3, 0.0)
    return (
        mixed,
        grad_tokens,
        type_counts,
        new_in[0],
        new_conv[0],
        new_out[0],
        new_norm[0],
        new_in[1],
        new_conv[1],
        new_out[1],
        new_norm[1],
        new_in[2],
        new_conv[2],
        new_out[2],
        new_norm[2],
    )


F32, BF16 = jnp.float32, jnp.bfloat16
MESH = pl.DeviceIdType.MESH
DP_RANKS, PLANE = 4, 8
HALO = (KERNEL_TAPS // 2) * DILATION_STRIDE
GELU_SCALE, GELU_CUBE = 0.7978845608, 0.044715
BLOCK = 256
UNROLL = 2


def dot_nn(a, b):
    return lax.dot_general(a, b, (((1,), (0,)), ((), ())), preferred_element_type=F32)


def dot_nt(a, b):
    return lax.dot_general(a, b, (((1,), (1,)), ((), ())), preferred_element_type=F32)


def dot_tn(a, b):
    return lax.dot_general(a, b, (((0,), (0,)), ((), ())), preferred_element_type=F32)


def gelu(z):
    t = jnp.tanh(z * (GELU_SCALE + (GELU_SCALE * GELU_CUBE) * (z * z)))
    h = 0.5 * z
    return h + h * t


def gelu_grad(z):
    zz = z * z
    t = jnp.tanh(z * (GELU_SCALE + (GELU_SCALE * GELU_CUBE) * zz))
    slope = z * (GELU_SCALE + (3.0 * GELU_SCALE * GELU_CUBE) * zz)
    return 0.5 * (1.0 + t + (1.0 - t * t) * slope)


def stats(x):
    c = x - jnp.mean(x, axis=-1, keepdims=True)
    r = lax.rsqrt(jnp.mean(c * c, axis=-1, keepdims=True) + EPSILON)
    return c * r, r


def loop(n, step, hooks=None):
    def one(i, carry):
        step(i)
        for at, calls in (hooks or {}).items():

            @pl.when(i == at)
            def _(calls=calls):
                for call in calls:
                    call()

        return carry

    lax.fori_loop(0, n, one, 0)


def once(step, i):
    step(i)


def block(i, n):
    return pl.ds(pl.multiple_of(i * n, n), n)


def round_up(n, m=128):
    return -(-n // m) * m


class Place:
    def __init__(self):
        self.d = lax.axis_index("dp")
        f = lax.axis_index("fsdp")
        self.f = f
        self.c, self.x, self.y = f % 2, (f // 2) % 2, f // 4
        self.oc, self.ox, self.oy = 1 - self.c, 1 - self.x, 1 - self.y
        self.ranks = [(self.d + j) % DP_RANKS for j in range(DP_RANKS)]
        self.sib = {"fsdp": f + 1 - 2 * self.c}
        self.xn = {"fsdp": f + 2 - 4 * self.x}
        self.yn = {"fsdp": f + 4 - 8 * self.y}
        self.zn = [{"dp": p} for p in self.ranks[1:]]


def barrier(pc):
    sem = pltpu.get_barrier_semaphore()
    peers = [pc.sib, pc.xn, pc.yn] + pc.zn
    for p in peers:
        pl.semaphore_signal(sem, inc=1, device_id=p, device_id_type=MESH)
    pl.semaphore_wait(sem, len(peers))


def remote(src, dst, send, recv, device):
    return pltpu.make_async_remote_copy(
        src_ref=src, dst_ref=dst, send_sem=send, recv_sem=recv, device_id=device, device_id_type=MESH
    )


class Unit:
    def __init__(self, name, first=0, count=0):
        self.name, self.first, self.count = name, first, count
        self.lead = (pl.ds(first, count),) if count else ()
        self.taps = [(k,) for k in range(count)] or [()]

    def tap(self, k):
        return (k[0] + self.first,) if k else ()

    def halves(self, h, lanes):
        if self.name == "out":
            return (slice(0, h // 2), slice(None)), (slice(h // 2, h), slice(None))
        cut = lanes // 2 // 128 * 128
        if self.first == 0:
            cut = lanes - cut
        return (slice(None), slice(0, cut)), (slice(None), slice(cut, lanes))

    def sizes(self, h, lanes):
        return [tuple(len(range(*c.indices(e))) for c, e in zip(cut, (h, lanes))) for cut in self.halves(h, lanes)]


UNITS = (Unit("in"), Unit("c0", 0, 3), Unit("c1", 3, 2), Unit("out"))


class Gather:
    SEMS = 13

    def __init__(self, pc, unit, w, zr, send, recv):
        self.pc, self.unit, self.w, self.zr, self.send, self.recv = pc, unit, w, zr, send, recv
        self.cut = unit.halves(*w.shape[-2:])
        self.sent = []

    def z(self, j):
        pc = self.pc
        mine = self.zr.at[pc.d]
        return remote(mine, mine, self.send.at[j - 1], self.recv.at[pc.d], pc.zn[j - 1])

    def z_in(self, j):
        pc = self.pc
        p = pc.ranks[j]
        return remote(self.zr.at[p], self.zr.at[p], self.send.at[j - 1], self.recv.at[p], pc.zn[j - 1])

    def start(self):
        for j in (2, 1, 3):
            self.z(j).start()

    def go(self, ref, i, device):
        c = remote(ref, ref, self.send.at[i], self.recv.at[i], device)
        c.start()
        self.sent.append((i, ref, device))

    def arrived(self, i, ref):
        remote(ref, ref, self.send.at[i], self.recv.at[i], self.pc.sib).wait_recv()

    def at(self, y, x, c, half=None):
        part = self.cut[half] if half is not None else (slice(None), slice(None))
        return self.w.at[self.unit.lead + (y, x, c) + part]

    def own(self):
        pc = self.pc
        for j in range(1, DP_RANKS):
            self.z_in(j).wait_recv()
        self.assemble()
        mine = self.at(pc.y, pc.x, pc.c)
        self.go(mine, 4, pc.xn)
        self.go(mine, 5, pc.yn)
        self.go(mine, 8, pc.sib)

    def assemble(self):
        own = (self.pc.y, self.pc.x, self.pc.c)
        h = self.zr.shape[1]
        n = self.w.shape[-1] // DP_RANKS
        pieces = [self.zr[i] for i in range(DP_RANKS)]
        if self.unit.name == "out":
            for part in range(2):
                joined = jnp.concatenate([p[:, part * n : (part + 1) * n] for p in pieces], axis=1)
                self.w[own + (slice(part * h, (part + 1) * h),)] = joined
            return
        for k in self.unit.taps:
            at = k[0] * n if k else 0
            self.w[self.unit.tap(k) + own] = jnp.concatenate([p[:, at : at + n] for p in pieces], axis=1)

    def from_x(self):
        pc = self.pc
        r = self.at(pc.y, pc.ox, pc.c)
        self.arrived(4, r)
        self.go(self.at(pc.y, pc.ox, pc.c, 1), 7, pc.yn)
        self.go(r, 9, pc.sib)

    def from_y(self):
        pc = self.pc
        r = self.at(pc.oy, pc.x, pc.c)
        self.arrived(5, r)
        self.go(self.at(pc.oy, pc.x, pc.c, 0), 6, pc.xn)
        self.go(r, 10, pc.sib)

    def from_diagonal(self):
        pc = self.pc
        for half in (0, 1):
            r = self.at(pc.oy, pc.ox, pc.c, half)
            self.arrived(6 + half, r)
            self.go(r, 11 + half, pc.sib)

    def from_sibling(self):
        pc = self.pc
        o = pc.oc
        self.arrived(8, self.at(pc.y, pc.x, o))
        self.arrived(9, self.at(pc.y, pc.ox, o))
        self.arrived(10, self.at(pc.oy, pc.x, o))
        for half in (0, 1):
            self.arrived(11 + half, self.at(pc.oy, pc.ox, o, half))

    def finish(self):
        for j in range(1, DP_RANKS):
            self.z(j).wait_send()
        for i, ref, device in self.sent:
            remote(ref, ref, self.send.at[i], self.recv.at[i], device).wait_send()


class Scatter:
    SEMS = 9

    def __init__(self, pc, unit, g, rcv, r1a, r1b, r2a, r2b, zs, zr, send, recv):
        self.pc, self.unit, self.g, self.rcv = pc, unit, g, rcv
        self.r1a, self.r1b, self.r2a, self.r2b = r1a, r1b, r2a, r2b
        self.zs, self.zr, self.send, self.recv = zs, zr, send, recv
        self.cut = unit.halves(*g.shape[-2:])

    def copy(self, i, at, dst, device):
        return remote(self.g.at[self.unit.lead + at], dst, self.send.at[i], self.recv.at[i], device)

    def c0(self):
        pc = self.pc
        every = slice(None)
        return self.copy(0, (every, every, pc.oc), self.rcv, pc.sib)

    def a1(self):
        pc = self.pc
        return self.copy(1, (slice(None), pc.ox, pc.c) + self.cut[0], self.r1a, pc.xn)

    def b1(self):
        pc = self.pc
        return self.copy(2, (pc.oy, slice(None), pc.c) + self.cut[1], self.r1b, pc.yn)

    def a2(self):
        pc = self.pc
        return self.copy(3, (pc.oy, pc.x, pc.c) + self.cut[0], self.r2a, pc.yn)

    def b2(self):
        pc = self.pc
        return self.copy(4, (pc.y, pc.ox, pc.c) + self.cut[1], self.r2b, pc.xn)

    def z(self, j):
        pc = self.pc
        return remote(self.zs.at[pc.ranks[j]], self.zr.at[pc.d], self.send.at[4 + j], self.recv.at[5 + pc.d], pc.zn[j - 1])

    def z_in(self, j):
        pc = self.pc
        p = pc.ranks[j]
        return remote(self.zs.at[p], self.zr.at[p], self.send.at[4 + j], self.recv.at[5 + p], pc.zn[j - 1])

    def start(self):
        self.c0().start()

    def add(self, at, ref, ref_at):
        for k in self.unit.taps:
            idx = self.unit.tap(k) + at
            self.g[idx] = (self.g[idx].astype(F32) + ref[k + ref_at].astype(F32)).astype(BF16)

    def step1(self):
        pc = self.pc
        self.c0().wait_recv()
        for y in range(2):
            for x in range(2):
                self.add((y, x, pc.c), self.rcv, (y, x))
        self.a1().start()
        self.b1().start()

    def step2(self):
        pc = self.pc
        own = (pc.y, pc.x, pc.c)
        self.a1().wait_recv()
        self.add((pc.oy, pc.x, pc.c) + self.cut[0], self.r1a, (pc.oy,))
        self.a2().start()
        self.b1().wait_recv()
        self.add((pc.y, pc.ox, pc.c) + self.cut[1], self.r1b, (pc.ox,))
        self.b2().start()
        self.add(own + self.cut[0], self.r1a, (pc.y,))
        self.add(own + self.cut[1], self.r1b, (pc.x,))

    def step3(self):
        pc = self.pc
        own = (pc.y, pc.x, pc.c)
        self.a2().wait_recv()
        self.add(own + self.cut[0], self.r2a, ())
        self.b2().wait_recv()
        self.add(own + self.cut[1], self.r2b, ())
        self.split(own)
        for j in (2, 1, 3):
            self.z(j).start()

    def split(self, own):
        h = self.zs.shape[1]
        n = self.g.shape[-1] // DP_RANKS
        if self.unit.name == "out":
            v = self.g[own]
            for i in range(DP_RANKS):
                at = slice(i * n, (i + 1) * n)
                self.zs[i, :, 0 : 2 * n] = jnp.concatenate([v[0:h, at], v[h : 2 * h, at]], axis=1)
            return
        parts = [self.g[self.unit.tap(k) + own] for k in self.unit.taps]
        for i in range(DP_RANKS):
            at = slice(i * n, (i + 1) * n)
            self.zs[i, :, 0 : len(parts) * n] = jnp.concatenate([v[:, at] for v in parts], axis=1)

    def step4(self, out):
        pc = self.pc
        total = self.zs[pc.d].astype(F32)
        for j in range(1, DP_RANKS):
            self.z_in(j).wait_recv()
            total = total + self.zr[pc.ranks[j]].astype(F32)
        out[...] = total

    def finish(self):
        for c in (self.c0(), self.a1(), self.b1(), self.a2(), self.b2()):
            c.wait_send()
        for j in range(1, DP_RANKS):
            self.z(j).wait_send()


class NormGather:
    SEMS = 7

    def __init__(self, pc, nz, nw, send, recv):
        self.pc, self.nz, self.nw, self.send, self.recv = pc, nz, nw, send, recv

    def z(self, j, p):
        pc = self.pc
        return remote(self.nz.at[p], self.nz.at[p], self.send.at[j - 1], self.recv.at[p], pc.zn[j - 1])

    def start(self):
        for j in range(1, DP_RANKS):
            self.z(j, self.pc.d).start()

    def stage(self, k):
        pc = self.pc
        ref = (self.nw.at[pc.y, pc.x, pc.c], self.nw.at[pc.y, pc.x], self.nw.at[pc.y])[k]
        return remote(ref, ref, self.send.at[3 + k], self.recv.at[4 + k], (pc.sib, pc.xn, pc.yn)[k])

    def stage_in(self, k):
        pc = self.pc
        ref = (self.nw.at[pc.y, pc.x, pc.oc], self.nw.at[pc.y, pc.ox], self.nw.at[pc.oy])[k]
        return remote(ref, ref, self.send.at[3 + k], self.recv.at[4 + k], (pc.sib, pc.xn, pc.yn)[k])

    def own(self):
        pc = self.pc
        for j in range(1, DP_RANKS):
            self.z(j, pc.ranks[j]).wait_recv()
        self.nw[pc.y, pc.x, pc.c] = jnp.concatenate([self.nz[i][0:2] for i in range(DP_RANKS)], axis=0)
        self.stage(0).start()

    def next(self, k):
        self.stage_in(k).wait_recv()
        if k < 2:
            self.stage(k + 1).start()

    def whole(self, width):
        return jnp.concatenate([self.nw[f // 4, (f // 2) % 2, f % 2][:, 0:width] for f in range(PLANE)], axis=1)

    def finish(self):
        for j in range(1, DP_RANKS):
            self.z(j, self.pc.d).wait_send()
        for k in range(3):
            self.stage(k).wait_send()


class SmallSum:
    SEMS = 7

    def __init__(self, pc, acc, got, zgot, send, recv):
        self.pc, self.acc, self.got, self.zgot, self.send, self.recv = pc, acc, got, zgot, send, recv

    def stage(self, k):
        pc = self.pc
        return remote(
            self.acc.at[k], self.got.at[k], self.send.at[k], self.recv.at[4 + k], (pc.sib, pc.xn, pc.yn)[k]
        )

    def z(self, j):
        pc = self.pc
        return remote(self.acc.at[3], self.zgot.at[pc.d], self.send.at[2 + j], self.recv.at[pc.d], pc.zn[j - 1])

    def z_in(self, j):
        pc = self.pc
        p = pc.ranks[j]
        return remote(self.acc.at[3], self.zgot.at[p], self.send.at[2 + j], self.recv.at[p], pc.zn[j - 1])

    def start(self):
        self.stage(0).start()

    def next(self, k):
        self.stage(k).wait_recv()
        self.acc[k + 1] = self.acc[k] + self.got[k]
        if k < 2:
            self.stage(k + 1).start()
        else:
            for j in range(1, DP_RANKS):
                self.z(j).start()

    def total(self):
        for j in range(1, DP_RANKS):
            self.z_in(j).wait_recv()
        self.zgot[self.pc.d] = self.acc[3]
        return (self.zgot[0] + self.zgot[1]) + (self.zgot[2] + self.zgot[3])

    def finish(self):
        for k in range(3):
            self.stage(k).wait_send()
        for j in range(1, DP_RANKS):
            self.z(j).wait_send()


def norm_back(n, r, gain, bias, e, sums, row):
    dz = e * gelu_grad(n * gain + bias)
    width = n.shape[1]
    sums[row : row + 1, 0:width] += jnp.sum(dz * n, axis=0, keepdims=True)
    sums[row + 1 : row + 2, 0:width] += jnp.sum(dz, axis=0, keepdims=True)
    dn = dz * gain
    m1 = jnp.mean(dn, axis=-1, keepdims=True)
    m2 = jnp.mean(dn * n, axis=-1, keepdims=True)
    return r * (dn - m1 - n * m2)


def block_kernel(r):
    pc = Place()
    x, cot, act_a, n_b, act_c = r.x, r.cot, r.act_a, r.n_b, r.act_c
    scale, sums, tail_rows = r.scale, r.sums, r.tail
    b_even, b_odd, g_even, g_odd, back_t = r.b_even, r.b_odd, r.g_even, r.g_odd, r.back_t
    rows, width = x.shape
    inner = n_b.shape[1]
    slots = r.lens.shape[0]
    seq = rows // slots
    blocks = seq // BLOCK
    grad_a = act_c

    wide = dict(zip([u.name for u in UNITS], (r.w_in, r.w_conv, r.w_conv, r.w_out)))
    own = {u.name: SimpleNamespace(**{k: getattr(r, k + u.name) for k in UNIT_SCRATCH}) for u in UNITS}
    pull = [Gather(pc, u, wide[u.name], own[u.name].zg_, own[u.name].gs_, own[u.name].gr_) for u in UNITS]
    get_in, get_c0, get_c1, get_out = pull

    def scatter(u, g):
        m = own[u.name]
        return Scatter(pc, u, g, m.rcv_, m.r1a_, m.r1b_, m.r2a_, m.r2b_, m.zg_, m.zr_, m.ss_, m.sr_)

    norm_gather = NormGather(pc, r.nz, r.nw, r.ns, r.nr)
    small = SmallSum(pc, r.sm_acc, r.sm_got, r.sm_z, r.sm_s, r.sm_r)

    load_x = pltpu.make_async_copy(r.tokens, x, r.io.at[0])
    load_cot = pltpu.make_async_copy(r.cot_in, cot, r.io.at[1])
    save_act = pltpu.make_async_copy(act_c, r.act_out, r.io.at[2])
    save_w = pltpu.make_async_copy(r.w_out, r.w_saved, r.io.at[3])
    load_x.start()

    cols = r.p_in.shape[0]
    r.nz[pc.d, 0:2, 0:cols] = r.p_norms[...].astype(BF16).astype(F32)
    barrier(pc)
    norm_gather.start()
    r.zg_in[pc.d, :, 0 : r.p_in.shape[1]] = r.p_in[...].astype(BF16)
    get_in.start()
    depth = r.p_conv.shape[1]
    for g in (get_c0, get_c1):
        for k in range(g.unit.count):
            g.zr[pc.d, :, k * depth : (k + 1) * depth] = r.p_conv[g.unit.first + k].T.astype(BF16)
    p_out = r.p_out[...].T.astype(BF16)
    h_out = r.zg_out.shape[1]
    r.zg_out[pc.d, :, 0 : 2 * depth] = jnp.concatenate([p_out[0:h_out], p_out[h_out : 2 * h_out]], axis=1)

    sums[...] = jnp.zeros_like(sums)
    pad = jnp.zeros((HALO, inner), BF16)
    for s in range(slots):
        for buf in (b_even, g_even):
            buf[s, 0:HALO, :] = pad
            buf[s, seq + HALO : seq + 2 * HALO, :] = pad

    def kept(s, first, count):
        return first + lax.broadcasted_iota(jnp.int32, (count, 1), 0) < r.lens[s]

    lab = r.labels[...]
    place = (
        lax.broadcasted_iota(jnp.int32, lab.shape, 0) * lab.shape[1] + lax.broadcasted_iota(jnp.int32, lab.shape, 1)
    )
    valid = place < 0
    for s in range(slots):
        valid = valid | ((place >= s * seq) & (place < s * seq + r.lens[s]))
    lane = lax.broadcasted_iota(jnp.int32, (1, inner), 1)
    counts = jnp.zeros((1, inner), F32)
    for c in range(TYPES):
        hits = jnp.sum(jnp.where(valid & (lab == c), 1.0, 0.0), keepdims=True)
        counts = counts + jnp.where(lane == c, hits, 0.0)
    small.acc[0, 8:9, :] = counts

    load_x.wait()
    load_cot.start()
    strip = BLOCK // 2
    strips = rows // strip

    def first_stats(i):
        at = block(i, strip)
        n, rs = stats(x[at, :].astype(F32))
        x[at, :] = n.astype(BF16)
        scale[at, 0:1] = rs

    loop(
        strips,
        first_stats,
        {
            strips // 4: [norm_gather.own],
            strips // 2: [lambda: norm_gather.next(0)],
            strips * 3 // 4: [get_c0.start, lambda: norm_gather.next(1)],
        },
    )
    norm_gather.next(2)
    get_in.own()
    r.norms[...] = norm_gather.whole(cols)
    norms = r.norms
    gain_a = jnp.concatenate([norms[0:1, :], norms[1:2, :]], axis=1)
    bias_a = jnp.concatenate([norms[2:3, :], norms[3:4, :]], axis=1)
    gain_b, bias_b, gain_c, bias_c = (norms[i : i + 1, :] for i in range(4, 8))

    def first_act(i):
        at = block(i, strip)
        act_a[at, :] = gelu(x[at, :].astype(F32) * gain_a + bias_a).astype(BF16)

    loop(strips, first_act)
    get_in.from_x()
    get_in.from_y()
    get_c0.own()
    get_c1.start()
    get_in.from_diagonal()
    get_in.from_sibling()
    w_in, w_conv, w_out = r.w_in, r.w_conv, r.w_out

    def flat(w):
        v = w[...]
        return v.reshape(PLANE * v.shape[3], v.shape[4])

    def skewed(steps, multiply, rest, hooks=None):
        def step(j):
            ahead = multiply(j * UNROLL)
            for u in range(UNROLL):
                now = ahead
                if u + 1 < UNROLL:
                    ahead = multiply(j * UNROLL + u + 1)
                rest(j * UNROLL + u, now)

        step.__name__ = multiply.__name__
        loop(steps // UNROLL, step, hooks)

    def place_of(j):
        return j // blocks, lax.rem(j, blocks) * BLOCK

    def shifted_store(even, odd, j, value):
        s, first = place_of(j)
        even[s, pl.ds(pl.multiple_of(first + HALO, 16), BLOCK), :] = value.astype(BF16)
        before = jnp.where(first == 0, 0.0, tail_rows[...])
        late = value[BLOCK - 8 :]
        odd[s, pl.ds(pl.multiple_of(first, 16), BLOCK), :] = jnp.concatenate(
            [before, value[: BLOCK - 8]], axis=0
        ).astype(BF16)
        odd[s, pl.ds(pl.multiple_of(first + BLOCK, 16), 16), :] = jnp.concatenate(
            [late, jnp.zeros_like(late)], axis=0
        ).astype(BF16)
        tail_rows[...] = late

    def tap_of(even, odd, k, sign):
        off = sign * DILATION_STRIDE * (k - KERNEL_TAPS // 2)
        return (even, HALO + off) if off % 16 == 0 else (odd, 8 + off)

    def taps(even, odd, j, sign):
        s, first = place_of(j)
        out = []
        for k in range(KERNEL_TAPS):
            buf, base = tap_of(even, odd, k, sign)
            out.append(buf[s, pl.ds(pl.multiple_of(first + base, 16), BLOCK), :])
        return jnp.concatenate(out, axis=1)

    def kept_in(j):
        s, first = place_of(j)
        return kept(s, first, BLOCK)

    total_blocks = slots * blocks

    def second(j):
        return dot_nt(act_a[block(j, BLOCK), :], flat(w_in))

    def second_rest(j, h):
        at = block(j, BLOCK)
        n, rs = stats(h)
        n_b[at, :] = n.astype(BF16)
        scale[at, 1:2] = rs
        shifted_store(b_even, b_odd, j, jnp.where(kept_in(j), gelu(n * gain_b + bias_b), 0.0))

    loop_end = total_blocks // UNROLL - 1
    chunk = 256
    skewed(
        total_blocks,
        second,
        second_rest,
        {0: [get_c0.from_x, get_c0.from_y], 1: [get_c1.own, get_out.start], loop_end: [get_c0.from_diagonal]},
    )
    get_c1.from_x()
    get_c1.from_y()
    get_out.own()
    get_c1.from_diagonal()
    get_c0.from_sibling()
    get_c1.from_sibling()

    def conv_rows():
        v = [w_conv[k].reshape(inner, inner) for k in range(KERNEL_TAPS)]
        return v

    def third(j):
        return dot_nt(taps(b_even, b_odd, j, 1), jnp.concatenate(conv_rows(), axis=1))

    def middle(n_c):
        def third_rest(j, h):
            at = block(j, BLOCK)
            n, rs = stats(h)
            n_c[at, :] = n.astype(BF16)
            scale[at, 2:3] = rs
            act_c[at, :] = jnp.where(kept_in(j), gelu(n * gain_c + bias_c), 0.0).astype(BF16)

        skewed(
            total_blocks,
            third,
            third_rest,
            {0: [get_out.from_x, get_out.from_y], 1: [get_out.from_diagonal], loop_end: [get_out.from_sibling]},
        )
        save_act.start()
        save_w.start()
        load_cot.wait()
        for c in [norm_gather] + pull:
            c.finish()

        tall = r.g_out.shape[3]

        def out_grad(lo):
            part = dot_tn(cot[:, lo : lo + chunk], act_c[...]).astype(BF16)
            for f in range(lo // tall, -(-(lo + chunk) // tall)):
                a, b = max(lo, f * tall), min(lo + chunk, (f + 1) * tall)
                r.g_out[f // 4, (f // 2) % 2, f % 2, a - f * tall : b - f * tall, :] = part[a - lo : b - lo]

        for lo in range(0, width, chunk):
            once(out_grad, lo)
        put_out = scatter(UNITS[3], r.g_out)
        put_out.start()

        def fourth(j):
            return dot_nn(cot[block(j, BLOCK), :], flat(w_out))

        def fourth_rest(j, h):
            at = block(j, BLOCK)
            e = jnp.where(kept_in(j), h, 0.0)
            back = norm_back(n_c[at, :].astype(F32), scale[at, 2:3], gain_c, bias_c, e, sums, 4)
            shifted_store(g_even, g_odd, j, back)
            back_t[:, at] = back.astype(BF16).T

        skewed(total_blocks, fourth, fourth_rest, {0: [put_out.step1], 2: [put_out.step2]})

    pl.run_scoped(middle, pltpu.VMEM((rows, inner), BF16))
    put_out = scatter(UNITS[3], r.g_out)

    def late(g_in, g_conv):
        put_in, put_c0, put_c1 = scatter(UNITS[0], g_in), scatter(UNITS[1], g_conv), scatter(UNITS[2], g_conv)

        def conv_grad(k):
            buf, base = tap_of(b_even, b_odd, k, 1)
            for lo in range(0, inner, chunk):
                hi = min(lo + chunk, inner)
                total = None
                for s in range(slots):
                    p = dot_nn(back_t[:, s * seq : (s + 1) * seq], buf[s, base : base + seq, lo:hi])
                    total = p if total is None else total + p
                g_conv[k, :, :, :, :, lo:hi] = total.astype(BF16).reshape((2, 2, 2, inner // PLANE, hi - lo))

        for k in range(KERNEL_TAPS):
            once(conv_grad, k)
            if k == 0:
                put_out.step3()
            if k == 2:
                put_c0.start()
            if k == 3:
                put_c0.step1()
        put_c1.start()
        save_act.wait()
        save_w.wait()

        def sixth(j):
            return dot_nn(taps(g_even, g_odd, j, -1), w_conv[...].reshape(KERNEL_TAPS * inner, inner))

        def sixth_rest(j, h):
            at = block(j, BLOCK)
            e = jnp.where(kept_in(j), h, 0.0)
            back = norm_back(n_b[at, :].astype(F32), scale[at, 1:2], gain_b, bias_b, e, sums, 2).astype(BF16)
            grad_a[at, :] = back
            back_t[:, at] = back.T

        skewed(
            total_blocks,
            sixth,
            sixth_rest,
            {
                0: [put_c1.step1, lambda: put_out.step4(r.s_out)],
                1: [put_c0.step2],
                2: [put_c1.step2],
                loop_end: [put_c0.step3],
            },
        )

        def in_grad(j):
            part = dot_nn(back_t[...], act_a[:, j * chunk : (j + 1) * chunk]).astype(BF16)
            g_in[:, :, :, :, j * chunk : (j + 1) * chunk] = part.reshape(2, 2, 2, inner // PLANE, chunk)

        for j in range(width // chunk):
            once(in_grad, j)
        put_in.start()

        def out_copy(at):
            return pltpu.make_async_copy(cot.at[at, :], r.grad_tokens.at[at, :], r.io.at[4])

        def eighth(i):
            at = block(i, BLOCK)
            e = dot_nn(grad_a[at, :], flat(w_in))
            back = norm_back(x[at, :].astype(F32), scale[at, 0:1], gain_a, bias_a, e, sums, 0)
            cot[at, :] = (cot[at, :].astype(F32) + back).astype(BF16)
            out_copy(at).start()

        loop(
            total_blocks,
            eighth,
            {
                0: [put_in.step1, put_c1.step3],
                2: [lambda: put_c0.step4(r.s_c0)],
                3: [put_in.step2],
                4: [lambda: put_c1.step4(r.s_c1)],
                6: [put_in.step3],
            },
        )
        small.acc[0, 0:8] = jnp.concatenate(
            [
                sums[0:1, 0:inner],
                sums[0:1, inner : 2 * inner],
                sums[1:2, 0:inner],
                sums[1:2, inner : 2 * inner],
                sums[2:6, 0:inner],
            ],
            axis=0,
        )
        small.start()
        for k in range(3):
            small.next(k)
        total = small.total()
        r.s_counts[...] = total[8:16, 0:128]
        mine = jnp.zeros((8, cols), F32)
        for f in range(PLANE):
            mine = mine + jnp.where(pc.f == f, total[0:8, f * cols : (f + 1) * cols], 0.0)
        pair = jnp.zeros((2, cols), F32)
        for i in range(DP_RANKS):
            pair = pair + jnp.where(pc.d == i, mine[2 * i : 2 * i + 2], 0.0)
        r.s_norms[...] = pair
        put_in.step4(r.s_in)
        for c in (put_in, put_c0, put_c1, put_out, small):
            c.finish()

        def eighth_end(_):
            pltpu.make_async_copy(cot, r.grad_tokens, r.io.at[4]).wait()

        once(eighth_end, 0)

    pl.run_scoped(late, pltpu.VMEM(r.w_in.shape, BF16), pltpu.VMEM(w_conv.shape, BF16))


UNIT_SCRATCH = ("zg_", "gs_", "gr_", "rcv_", "r1a_", "r1b_", "r2a_", "r2b_", "zr_", "ss_", "sr_")


def run_block(tokens, cotangent, lengths, labels, w_in, w_conv, w_out, norm_params):
    rows, width = tokens.shape
    cols, rank_in = w_in.shape
    depth = w_conv.shape[1]
    inner = cols * PLANE
    slots = lengths.shape[0]
    seq = rows // slots
    V = pltpu.VMEM
    dma = pltpu.SemaphoreType.DMA
    h_out = w_out.shape[1]
    inputs = dict(
        lens=(lengths, pltpu.SMEM),
        tokens=(tokens, pl.ANY),
        cot_in=(cotangent, pl.ANY),
        labels=(labels.reshape(rows // 128, 128), V),
        p_in=(w_in, V),
        p_conv=(w_conv, V),
        p_out=(w_out, V),
        p_norms=(norm_params, V),
    )
    outputs = dict(
        act_out=((rows, inner), BF16, pl.ANY),
        w_saved=((2, 2, 2, h_out, inner), BF16, pl.ANY),
        grad_tokens=((rows, width), BF16, pl.ANY),
        s_counts=((8, 128), F32, V),
        s_norms=(norm_params.shape, F32, V),
    )
    halo_rows = V((slots, seq + 2 * HALO, inner), BF16)
    taps = V((KERNEL_TAPS, 2, 2, 2, cols, inner), BF16)
    scratch = dict(
        x=V((rows, width), BF16),
        cot=V((rows, width), BF16),
        act_a=V((rows, width), BF16),
        n_b=V((rows, inner), BF16),
        act_c=V((rows, inner), BF16),
        scale=V((rows, 8), F32),
        sums=V((8, width), F32),
        tail=V((8, inner), F32),
        norms=V((8, inner), F32),
        back_t=V((inner, rows), BF16),
        b_even=halo_rows,
        b_odd=halo_rows,
        g_even=halo_rows,
        g_odd=halo_rows,
        w_in=V((2, 2, 2, cols, width), BF16),
        w_conv=taps,
        w_out=V((2, 2, 2, h_out, inner), BF16),
        g_out=V((2, 2, 2, h_out, inner), BF16),
        io=dma((5,)),
        nz=V((DP_RANKS, 8, 128), F32),
        nw=V((2, 2, 2, 8, 128), F32),
        ns=dma((NormGather.SEMS,)),
        nr=dma((NormGather.SEMS,)),
        sm_acc=V((4, 16, inner), F32),
        sm_got=V((3, 16, inner), F32),
        sm_z=V((DP_RANKS, 16, inner), F32),
        sm_s=dma((SmallSum.SEMS,)),
        sm_r=dma((SmallSum.SEMS,)),
    )
    for u in UNITS:
        lead = (u.count,) if u.count else ()
        h, lanes = (cols, width) if u.name == "in" else (h_out, inner) if u.name == "out" else (cols, inner)
        piece = rank_in if u.name == "in" else depth * (u.count or 2)
        z = (cols, round_up(piece))
        half = u.sizes(h, lanes)
        outputs["s_" + u.name] = (z, F32, V)
        shapes = (
            V((DP_RANKS,) + z, BF16),
            dma((Gather.SEMS,)),
            dma((Gather.SEMS,)),
            V(lead + (2, 2, h, lanes), BF16),
            V(lead + (2,) + half[0], BF16),
            V(lead + (2,) + half[1], BF16),
            V(lead + half[0], BF16),
            V(lead + half[1], BF16),
            V((DP_RANKS,) + z, BF16),
            dma((Scatter.SEMS,)),
            dma((Scatter.SEMS,)),
        )
        scratch.update(zip([k + u.name for k in UNIT_SCRATCH], shapes))
    names = list(inputs) + list(outputs) + list(scratch)
    work = 6 * rows * (2 * width * inner + KERNEL_TAPS * inner * inner)
    out = pl.pallas_call(
        lambda *refs: block_kernel(SimpleNamespace(**dict(zip(names, refs)))),
        out_shape=tuple(jax.ShapeDtypeStruct(s, t) for s, t, _ in outputs.values()),
        in_specs=[pl.BlockSpec(memory_space=m) for _, m in inputs.values()],
        out_specs=tuple(pl.BlockSpec(memory_space=m) for _, _, m in outputs.values()),
        scratch_shapes=list(scratch.values()),
        compiler_params=pltpu.CompilerParams(
            collective_id=0, has_side_effects=True, vmem_limit_bytes=VMEM_BYTES
        ),
        cost_estimate=pl.CostEstimate(flops=work, bytes_accessed=8 * rows * width, transcendentals=0),
        name="residual_block",
    )(*(a for a, _ in inputs.values()))
    return dict(zip(outputs, out))


VMEM_BYTES = 63 * 1024 * 1024


def finish_kernel(r):
    rows = r.tokens.shape[0] // FINISH_PARTS
    loads = {}

    def load(k, src, dst):
        loads[k] = pltpu.make_async_copy(src, dst, r.in_sem.at[len(loads)])
        loads[k].start()

    load("w", r.w_saved, r.hold_w)
    parts = [pl.ds(i * rows, rows) for i in range(FINISH_PARTS)]
    for i, at in enumerate(parts):
        load(("a", i), r.act_out.at[at, :], r.hold_act.at[at, :])
        load(("t", i), r.tokens.at[at, :], r.hold_x.at[at, :])
        load(("g", i), r.grad_tokens.at[at, :], r.hold_g.at[at, :])
        if i == 0:
            for n in STEP_ORDER:
                load("s_" + n, getattr(r, "s_" + n), getattr(r, "bs_" + n))
                for kind in ("w_", "m_", "v_"):
                    if n != "c1":
                        load(kind + n, getattr(r, kind + n), getattr(r, "b" + kind + n))
            load("n", r.s_counts, r.bs_counts)
    stores = []

    def store(src, dst):
        stores.append(pltpu.make_async_copy(src, dst, r.out_sem.at[len(stores)]))
        stores[-1].start()

    def step(n, at, grad, rate, decay):
        new = adamw(getattr(r, "bw_" + n)[at], getattr(r, "bm_" + n)[at], getattr(r, "bv_" + n)[at], grad, rate, decay)
        for kind, value in zip(("ow_", "om_", "ov_"), new):
            getattr(r, kind + n)[at] = value

    def ready(n):
        for kind in ("s_", "w_", "m_", "v_"):
            if kind + n in loads:
                loads[kind + n].wait()

    def done(n):
        for kind in ("w_", "m_", "v_"):
            store(getattr(r, "o" + kind + n), getattr(r, "n" + kind + n))

    everything = (slice(None), slice(None))
    depth = r.bw_c0.shape[1]

    def conv_step():
        ready("c0")
        ready("c1")
        for u in UNITS[1:3]:
            for k in range(u.count):
                grad = getattr(r, "bs_" + u.name)[:, k * depth : (k + 1) * depth].T
                step("c0", (u.first + k,), grad, 0.5 * (KERNEL_TAPS * INNER) ** (-0.5), 0.01)
        done("c0")

    def in_step():
        ready("in")
        step("in", everything, r.bs_in[:, 0 : r.bw_in.shape[1]], 0.5 * D ** (-0.5), 0.01)
        done("in")

    def out_step():
        ready("out")
        flat = r.bs_out[...]
        grad = jnp.concatenate([flat[:, 0:depth].T, flat[:, depth : 2 * depth].T], axis=1)
        step("out", everything, grad, 0.5 * (INNER // 2) ** (-0.5), 0.01)
        done("out")
        ready("norms")
        step("norms", everything, r.bs_norms[...], 0.3, 0.0)
        done("norms")
        loads["n"].wait()
        r.type_counts[...] = r.bs_counts[0, 0:TYPES].astype(jnp.int32)

    others = [conv_step, in_step, out_step]
    loads["w"].wait()
    for i, at in enumerate(parts):
        loads[("a", i)].wait()
        loads[("t", i)].wait()
        w = r.hold_w[...]
        hid = dot_nt(r.hold_act[at, :], w.reshape(PLANE * w.shape[3], w.shape[4]))
        r.hold_x[at, :] = (r.hold_x[at, :].astype(F32) + hid).astype(BF16)
        store(r.hold_x.at[at, :], r.new_mixed.at[at, :])
        loads[("g", i)].wait()
        store(r.hold_g.at[at, :], r.new_grad_tokens.at[at, :])
        if i < len(others):
            others[i]()
    for c in stores:
        c.wait()


STEP_ORDER = ("c0", "c1", "in", "out", "norms")
FINISH_PARTS = 4


def run_finish(res, tokens, weights, means, squares):
    V, dma = pltpu.VMEM, pltpu.SemaphoreType.DMA
    inputs = {k: res[k] for k in ("act_out", "w_saved", "grad_tokens", "s_counts")}
    inputs["tokens"] = tokens
    held = []
    for n in STEP_ORDER:
        inputs["s_" + n] = res["s_" + n]
        held.append("s_" + n)
        if n in weights:
            for kind, arrays in (("w_", weights), ("m_", means), ("v_", squares)):
                inputs[kind + n] = arrays[n]
                held.append(kind + n)
    outputs = dict(new_mixed=tokens, new_grad_tokens=tokens)
    for kind in ("w_", "m_", "v_"):
        for n, a in weights.items():
            outputs["n" + kind + n] = a
    scratch = {"b" + k: V(inputs[k].shape, F32) for k in held + ["s_counts"]}
    for kind in ("ow_", "om_", "ov_"):
        scratch.update({kind + n: V(a.shape, F32) for n, a in weights.items()})
    whole = V(tokens.shape, BF16)
    scratch.update(hold_x=whole, hold_g=whole)
    scratch["hold_act"] = V(res["act_out"].shape, BF16)
    scratch["hold_w"] = V(res["w_saved"].shape, BF16)
    scratch.update(in_sem=dma((len(held) + 2 + 3 * FINISH_PARTS,)), out_sem=dma((12 + 2 * FINISH_PARTS,)))
    shapes = [jax.ShapeDtypeStruct(a.shape, a.dtype) for a in outputs.values()]
    names = list(inputs) + list(outputs) + ["type_counts"] + list(scratch)
    hbm = pl.BlockSpec(memory_space=pl.ANY)
    return pl.pallas_call(
        lambda *refs: finish_kernel(SimpleNamespace(**dict(zip(names, refs)))),
        out_shape=tuple(shapes) + (jax.ShapeDtypeStruct((TYPES,), jnp.int32),),
        in_specs=[hbm] * len(inputs),
        out_specs=(hbm,) * len(outputs) + (pl.BlockSpec(memory_space=V),),
        scratch_shapes=list(scratch.values()),
        compiler_params=pltpu.CompilerParams(vmem_limit_bytes=VMEM_BYTES),
        name="finish",
    )(*inputs.values())


def fused_body(
    tokens,
    cotangent,
    lengths,
    labels,
    w_in,
    w_conv,
    w_out,
    norm_params,
    mean_w_in,
    mean_w_conv,
    mean_w_out,
    mean_norms,
    square_w_in,
    square_w_conv,
    square_w_out,
    square_norms,
):
    res = run_block(tokens, cotangent, lengths, labels, w_in.T, w_conv, w_out, norm_params)
    names = ("in", "c0", "out", "norms")
    new = run_finish(
        res,
        tokens,
        dict(zip(names, (w_in.T, w_conv, w_out, norm_params))),
        dict(zip(names, (mean_w_in.T, mean_w_conv, mean_w_out, mean_norms))),
        dict(zip(names, (square_w_in.T, square_w_conv, square_w_out, square_norms))),
    )
    mixed, grad_tokens, *steps, counts = new
    for i in (0, 4, 8):
        steps[i] = steps[i].T
    return (mixed, grad_tokens, counts) + tuple(steps)


def solution(mesh):
    fused = mesh.shape["dp"] == DP_RANKS and mesh.shape["fsdp"] == PLANE
    return jax.shard_map(
        fused_body if fused else plain_body,
        mesh=mesh,
        in_specs=(
            P(("dp", "fsdp"), None),
            P(("dp", "fsdp"), None),
            P(("dp", "fsdp")),
            P(("dp", "fsdp")),
            P("dp", "fsdp"),
            P(None, "dp", "fsdp"),
            P("dp", "fsdp"),
            P("dp", "fsdp"),
            P("dp", "fsdp"),
            P(None, "dp", "fsdp"),
            P("dp", "fsdp"),
            P("dp", "fsdp"),
            P("dp", "fsdp"),
            P(None, "dp", "fsdp"),
            P("dp", "fsdp"),
            P("dp", "fsdp"),
        ),
        out_specs=(
            P(("dp", "fsdp"), None),
            P(("dp", "fsdp"), None),
            P(),
            P("dp", "fsdp"),
            P(None, "dp", "fsdp"),
            P("dp", "fsdp"),
            P("dp", "fsdp"),
            P("dp", "fsdp"),
            P(None, "dp", "fsdp"),
            P("dp", "fsdp"),
            P("dp", "fsdp"),
            P("dp", "fsdp"),
            P(None, "dp", "fsdp"),
            P("dp", "fsdp"),
            P("dp", "fsdp"),
        ),
        check_vma=False,
    )
```

```python
import functools
from types import SimpleNamespace

import jax
import jax.numpy as jnp
from jax import lax
from jax.experimental import pallas as pl
from jax.experimental.pallas import tpu as pltpu
from jax.sharding import PartitionSpec as P

D = 1280
INNER = 640
KERNEL_TAPS = 5
DILATION_STRIDE = 8
TYPES = 25
STEP = 5


EPSILON = 1e-05


def plain_normalize(value, gain, bias):
    center = value - jnp.mean(value, axis=-1, keepdims=True)
    spread = jnp.mean(center * center, axis=-1, keepdims=True)
    return center * lax.rsqrt(spread + EPSILON) * gain + bias


def activate(value):
    return jax.nn.gelu(value, approximate=True)


def norm_piece(value, gain, bias):
    return activate(plain_normalize(value, gain, bias))


def gather_params(first, second, third, fourth):
    part = (
        lax.all_gather(first, "fsdp", axis=1, tiled=True),
        lax.all_gather(second, "fsdp", axis=2, tiled=True),
        lax.all_gather(third, "fsdp", axis=1, tiled=True),
        lax.all_gather(fourth, "fsdp", axis=1, tiled=True),
    )
    return (
        lax.all_gather(part[0], "dp", axis=0, tiled=True),
        lax.all_gather(part[1], "dp", axis=1, tiled=True),
        lax.all_gather(part[2], "dp", axis=0, tiled=True),
        lax.all_gather(part[3], "dp", axis=0, tiled=True),
    )


def reduce_grads(first, second, third, fourth):
    part = (
        lax.psum_scatter(first, "fsdp", scatter_dimension=1, tiled=True),
        lax.psum_scatter(second, "fsdp", scatter_dimension=2, tiled=True),
        lax.psum_scatter(third, "fsdp", scatter_dimension=1, tiled=True),
        lax.psum_scatter(fourth, "fsdp", scatter_dimension=1, tiled=True),
    )
    return (
        lax.psum_scatter(
            part[0].astype(jnp.bfloat16), "dp", scatter_dimension=0, tiled=True
        ).astype(jnp.float32),
        lax.psum_scatter(
            part[1].astype(jnp.bfloat16), "dp", scatter_dimension=1, tiled=True
        ).astype(jnp.float32),
        lax.psum_scatter(
            part[2].astype(jnp.bfloat16), "dp", scatter_dimension=0, tiled=True
        ).astype(jnp.float32),
        lax.psum_scatter(
            part[3].astype(jnp.bfloat16), "dp", scatter_dimension=0, tiled=True
        ).astype(jnp.float32),
    )


def stack_taps(value_rows):
    sequence_rows = value_rows.shape[1]
    half_width = KERNEL_TAPS // 2
    padded_input = jnp.pad(
        value_rows, ((0, 0), (half_width * DILATION_STRIDE, half_width * DILATION_STRIDE), (0, 0))
    )
    return jnp.concatenate(
        [
            padded_input[
                :, tap_index * DILATION_STRIDE : tap_index * DILATION_STRIDE + sequence_rows
            ]
            for tap_index in range(KERNEL_TAPS)
        ],
        axis=-1,
    )


def unstack_taps(gradient_tree, sequence_rows):
    half_width = KERNEL_TAPS // 2
    padded_input = jnp.pad(
        gradient_tree,
        ((0, 0), (half_width * DILATION_STRIDE, half_width * DILATION_STRIDE), (0, 0), (0, 0)),
    )
    total_count = padded_input[
        :, 2 * half_width * DILATION_STRIDE : 2 * half_width * DILATION_STRIDE + sequence_rows, 0
    ]
    for tap_index in range(1, KERNEL_TAPS):
        start_offset = (2 * half_width - tap_index) * DILATION_STRIDE
        total_count = (
            total_count + padded_input[:, start_offset : start_offset + sequence_rows, tap_index]
        )
    return total_count


def adamw(master, mean_old, square_old, grad, rate, decay):
    mean_new = 0.5 * mean_old + 0.5 * grad
    square_new = 0.6 * square_old + 0.4 * grad * grad
    mean_hat = mean_new / (1.0 - 0.5**STEP)
    square_hat = square_new / (1.0 - 0.6**STEP)
    weight = master - rate * (mean_hat / (jnp.sqrt(square_hat) + 1e-08) + decay * master)
    return (weight, mean_new, square_new)


def contract_rows(left, right):
    return lax.dot_general(
        left, right, (((0,), (0,)), ((), ())), preferred_element_type=jnp.float32
    )


def contract_cols(left, right):
    return lax.dot_general(
        left, right, (((1,), (1,)), ((), ())), preferred_element_type=jnp.float32
    )


def plain_body(
    tokens,
    cotangent,
    lengths,
    labels,
    w_in,
    w_conv,
    w_out,
    norm_params,
    mean_w_in,
    mean_w_conv,
    mean_w_out,
    mean_norms,
    square_w_in,
    square_w_conv,
    square_w_out,
    square_norms,
):
    slots = lengths.shape[0]
    rows = tokens.shape[0]
    sequence_rows = rows // slots
    places = lax.broadcasted_iota(jnp.int32, (slots, sequence_rows), 1)
    valid = (places < lengths[:, None]).reshape(rows, 1)
    keep = valid.astype(jnp.float32)
    full_in, full_conv, full_out, full_norms = gather_params(
        w_in.astype(jnp.bfloat16),
        w_conv.astype(jnp.bfloat16),
        w_out.astype(jnp.bfloat16),
        norm_params.astype(jnp.bfloat16),
    )
    inner = full_in.shape[1]
    norms = full_norms.astype(jnp.float32)
    gain_a = norms[0:2].reshape(2 * inner)
    bias_a = norms[2:4].reshape(2 * inner)
    source = tokens.astype(jnp.float32)

    def masked_piece(value, gain, bias):
        return norm_piece(value, gain, bias) * keep

    act_a, back_a = jax.vjp(norm_piece, source, gain_a, bias_a)
    low_a = act_a.astype(jnp.bfloat16)
    hid_a = jnp.dot(low_a, full_in, preferred_element_type=jnp.float32)
    middle_activation, back_b = jax.vjp(masked_piece, hid_a, norms[4], norms[5])
    low_b = middle_activation.astype(jnp.bfloat16).reshape(slots, sequence_rows, inner)
    tap_weights = stack_taps(low_b).reshape(rows, KERNEL_TAPS * inner)
    conv_flat = full_conv.reshape(KERNEL_TAPS * inner, inner)
    middle_hidden = jnp.dot(tap_weights, conv_flat, preferred_element_type=jnp.float32)
    act_c, back_c = jax.vjp(norm_piece, middle_hidden, norms[6], norms[7])
    low_c = act_c.astype(jnp.bfloat16)
    hid_c = jnp.dot(low_c, full_out, preferred_element_type=jnp.float32)
    mixed = (source + keep * hid_c).astype(jnp.bfloat16)
    upstream = cotangent.astype(jnp.float32)
    grad_c = (keep * upstream).astype(jnp.bfloat16)
    grad_out = contract_rows(low_c, grad_c)
    d_act_c = contract_cols(grad_c, full_out)
    d_hid_b, d_gain_c, d_bias_c = back_c(d_act_c)
    grad_b = d_hid_b.astype(jnp.bfloat16)
    grad_conv = contract_rows(tap_weights, grad_b).reshape(KERNEL_TAPS, inner, inner)
    d_taps = contract_cols(grad_b, conv_flat)
    d_act_b = unstack_taps(
        d_taps.reshape(slots, sequence_rows, KERNEL_TAPS, inner), sequence_rows
    ).reshape(rows, inner)
    d_hid_a, d_gain_b, d_bias_b = back_b(d_act_b)
    grad_a = d_hid_a.astype(jnp.bfloat16)
    grad_in = contract_rows(low_a, grad_a)
    d_act_a = contract_cols(grad_a, full_in)
    d_source, d_gain_a, d_bias_a = back_a(d_act_a)
    grad_tokens = (upstream + d_source).astype(jnp.bfloat16)
    grad_norms = jnp.concatenate(
        [
            d_gain_a.reshape(2, inner),
            d_bias_a.reshape(2, inner),
            d_gain_b[None],
            d_bias_b[None],
            d_gain_c[None],
            d_bias_c[None],
        ],
        axis=0,
    )
    sum_in, sum_conv, sum_out, sum_norms = reduce_grads(grad_in, grad_conv, grad_out, grad_norms)
    kinds = lax.broadcasted_iota(jnp.int32, (1, TYPES), 1)
    hits = (labels[:, None] == kinds) & valid
    local_counts = jnp.sum(hits.astype(jnp.int32), axis=0)
    type_counts = lax.psum(local_counts, ("dp", "fsdp"))
    new_in = adamw(w_in, mean_w_in, square_w_in, sum_in, 0.5 * D ** (-0.5), 0.01)
    new_conv = adamw(
        w_conv, mean_w_conv, square_w_conv, sum_conv, 0.5 * (KERNEL_TAPS * INNER) ** (-0.5), 0.01
    )
    new_out = adamw(w_out, mean_w_out, square_w_out, sum_out, 0.5 * (INNER // 2) ** (-0.5), 0.01)
    new_norm = adamw(norm_params, mean_norms, square_norms, sum_norms, 0.3, 0.0)
    return (
        mixed,
        grad_tokens,
        type_counts,
        new_in[0],
        new_conv[0],
        new_out[0],
        new_norm[0],
        new_in[1],
        new_conv[1],
        new_out[1],
        new_norm[1],
        new_in[2],
        new_conv[2],
        new_out[2],
        new_norm[2],
    )


F32, BF16 = jnp.float32, jnp.bfloat16
MESH = pl.DeviceIdType.MESH
DP_RANKS, PLANE = 4, 8
HALO = (KERNEL_TAPS // 2) * DILATION_STRIDE
GELU_SCALE, GELU_CUBE = 0.7978845608, 0.044715
BLOCK = 256
STRIP = 128
FINE = 64
UNROLL = 2


def dot_nn(a, b):
    return lax.dot_general(a, b, (((1,), (0,)), ((), ())), preferred_element_type=F32)


def dot_nt(a, b):
    return lax.dot_general(a, b, (((1,), (1,)), ((), ())), preferred_element_type=F32)


def dot_tn(a, b):
    return lax.dot_general(a, b, (((0,), (0,)), ((), ())), preferred_element_type=F32)


def gelu(z):
    t = jnp.tanh(z * (GELU_SCALE + (GELU_SCALE * GELU_CUBE) * (z * z)))
    h = 0.5 * z
    return h + h * t


def gelu_grad(z):
    zz = z * z
    t = jnp.tanh(z * (GELU_SCALE + (GELU_SCALE * GELU_CUBE) * zz))
    slope = z * (GELU_SCALE + (3.0 * GELU_SCALE * GELU_CUBE) * zz)
    return 0.5 * (1.0 + t + (1.0 - t * t) * slope)


def stats(x):
    c = x - jnp.mean(x, axis=-1, keepdims=True)
    r = lax.rsqrt(jnp.mean(c * c, axis=-1, keepdims=True) + EPSILON)
    return c * r, r


def loop(n, step, hooks=None):
    def one(i, carry):
        step(i)
        for at, calls in (hooks or {}).items():

            @pl.when(i == at)
            def _(calls=calls):
                for call in calls:
                    call()

        return carry

    lax.fori_loop(0, n, one, 0)


def once(step, i):
    step(i)


def block(i, n):
    return pl.ds(pl.multiple_of(i * n, n), n)


def round_up(n, m=128):
    return -(-n // m) * m


class Place:
    def __init__(self):
        self.d = lax.axis_index("dp")
        f = lax.axis_index("fsdp")
        self.f = f
        self.c, self.x, self.y = f % 2, (f // 2) % 2, f // 4
        self.oc, self.ox, self.oy = 1 - self.c, 1 - self.x, 1 - self.y
        self.ranks = [(self.d + j) % DP_RANKS for j in range(DP_RANKS)]
        self.sib = {"fsdp": f + 1 - 2 * self.c}
        self.xn = {"fsdp": f + 2 - 4 * self.x}
        self.yn = {"fsdp": f + 4 - 8 * self.y}
        self.zn = [{"dp": p} for p in self.ranks[1:]]
        bits = [(m // 4, m // 2 % 2, m % 2) for m in range(1, PLANE)]
        self.plane = [
            4 * (self.oy if y else self.y) + 2 * (self.ox if x else self.x) + (self.oc if c else self.c)
            for y, x, c in bits
        ]


def barrier(pc):
    sem = pltpu.get_barrier_semaphore()
    peers = [{"fsdp": p} for p in pc.plane] + pc.zn
    for p in peers:
        pl.semaphore_signal(sem, inc=1, device_id=p, device_id_type=MESH)
    pl.semaphore_wait(sem, len(peers))


def remote(src, dst, send, recv, device):
    return pltpu.make_async_remote_copy(
        src_ref=src, dst_ref=dst, send_sem=send, recv_sem=recv, device_id=device, device_id_type=MESH
    )


class Unit:
    def __init__(self, name, first=0, count=0):
        self.name, self.first, self.count = name, first, count
        self.lead = (pl.ds(first, count),) if count else ()
        self.taps = [(k,) for k in range(count)] or [()]

    def tap(self, k):
        return (k[0] + self.first,) if k else ()

    def halves(self, h, lanes):
        if self.name == "out":
            return (slice(0, h // 2), slice(None)), (slice(h // 2, h), slice(None))
        cut = lanes // 2 // 128 * 128
        if self.first == 0:
            cut = lanes - cut
        return (slice(None), slice(0, cut)), (slice(None), slice(cut, lanes))

    def sizes(self, h, lanes):
        return [tuple(len(range(*c.indices(e))) for c, e in zip(cut, (h, lanes))) for cut in self.halves(h, lanes)]


UNITS = (Unit("in"), Unit("c0", 0, 3), Unit("c1", 3, 2), Unit("out"))


class Gather:
    SEMS = 13

    def __init__(self, pc, unit, w, zr, send, recv):
        self.pc, self.unit, self.w, self.zr, self.send, self.recv = pc, unit, w, zr, send, recv
        self.cut = unit.halves(*w.shape[-2:])
        self.sent = []

    def z(self, j):
        pc = self.pc
        mine = self.zr.at[pc.d]
        return remote(mine, mine, self.send.at[j - 1], self.recv.at[pc.d], pc.zn[j - 1])

    def z_in(self, j):
        pc = self.pc
        p = pc.ranks[j]
        return remote(self.zr.at[p], self.zr.at[p], self.send.at[j - 1], self.recv.at[p], pc.zn[j - 1])

    def start(self):
        for j in (2, 1, 3):
            self.z(j).start()

    def go(self, ref, i, device):
        c = remote(ref, ref, self.send.at[i], self.recv.at[i], device)
        c.start()
        self.sent.append((i, ref, device))

    def arrived(self, i, ref):
        remote(ref, ref, self.send.at[i], self.recv.at[i], self.pc.sib).wait_recv()

    def at(self, y, x, c, half=None):
        part = self.cut[half] if half is not None else (slice(None), slice(None))
        return self.w.at[self.unit.lead + (y, x, c) + part]

    def own(self):
        pc = self.pc
        for j in range(1, DP_RANKS):
            self.z_in(j).wait_recv()
        self.assemble()
        mine = self.at(pc.y, pc.x, pc.c)
        self.go(mine, 4, pc.xn)
        self.go(mine, 5, pc.yn)
        self.go(mine, 8, pc.sib)

    def assemble(self):
        own = (self.pc.y, self.pc.x, self.pc.c)
        h = self.zr.shape[1]
        n = self.w.shape[-1] // DP_RANKS
        pieces = [self.zr[i] for i in range(DP_RANKS)]
        if self.unit.name == "out":
            for part in range(2):
                joined = jnp.concatenate([p[:, part * n : (part + 1) * n] for p in pieces], axis=1)
                self.w[own + (slice(part * h, (part + 1) * h),)] = joined
            return
        for k in self.unit.taps:
            at = k[0] * n if k else 0
            self.w[self.unit.tap(k) + own] = jnp.concatenate([p[:, at : at + n] for p in pieces], axis=1)

    def from_x(self):
        pc = self.pc
        r = self.at(pc.y, pc.ox, pc.c)
        self.arrived(4, r)
        self.go(self.at(pc.y, pc.ox, pc.c, 1), 7, pc.yn)
        self.go(r, 9, pc.sib)

    def from_y(self):
        pc = self.pc
        r = self.at(pc.oy, pc.x, pc.c)
        self.arrived(5, r)
        self.go(self.at(pc.oy, pc.x, pc.c, 0), 6, pc.xn)
        self.go(r, 10, pc.sib)

    def from_diagonal(self):
        pc = self.pc
        for half in (0, 1):
            r = self.at(pc.oy, pc.ox, pc.c, half)
            self.arrived(6 + half, r)
            self.go(r, 11 + half, pc.sib)

    def from_sibling(self):
        pc = self.pc
        o = pc.oc
        self.arrived(8, self.at(pc.y, pc.x, o))
        self.arrived(9, self.at(pc.y, pc.ox, o))
        self.arrived(10, self.at(pc.oy, pc.x, o))
        for half in (0, 1):
            self.arrived(11 + half, self.at(pc.oy, pc.ox, o, half))

    def finish(self):
        for j in range(1, DP_RANKS):
            self.z(j).wait_send()
        for i, ref, device in self.sent:
            remote(ref, ref, self.send.at[i], self.recv.at[i], device).wait_send()


class Scatter:
    SEMS = 9

    def __init__(self, pc, unit, g, rcv, r1a, r1b, r2a, r2b, zs, zr, send, recv):
        self.pc, self.unit, self.g, self.rcv = pc, unit, g, rcv
        self.r1a, self.r1b, self.r2a, self.r2b = r1a, r1b, r2a, r2b
        self.zs, self.zr, self.send, self.recv = zs, zr, send, recv
        self.cut = unit.halves(*g.shape[-2:])

    def copy(self, i, at, dst, device):
        return remote(self.g.at[self.unit.lead + at], dst, self.send.at[i], self.recv.at[i], device)

    def c0(self):
        pc = self.pc
        every = slice(None)
        return self.copy(0, (every, every, pc.oc), self.rcv, pc.sib)

    def a1(self):
        pc = self.pc
        return self.copy(1, (slice(None), pc.ox, pc.c) + self.cut[0], self.r1a, pc.xn)

    def b1(self):
        pc = self.pc
        return self.copy(2, (pc.oy, slice(None), pc.c) + self.cut[1], self.r1b, pc.yn)

    def a2(self):
        pc = self.pc
        return self.copy(3, (pc.oy, pc.x, pc.c) + self.cut[0], self.r2a, pc.yn)

    def b2(self):
        pc = self.pc
        return self.copy(4, (pc.y, pc.ox, pc.c) + self.cut[1], self.r2b, pc.xn)

    def z(self, j):
        pc = self.pc
        return remote(self.zs.at[pc.ranks[j]], self.zr.at[pc.d], self.send.at[4 + j], self.recv.at[5 + pc.d], pc.zn[j - 1])

    def z_in(self, j):
        pc = self.pc
        p = pc.ranks[j]
        return remote(self.zs.at[p], self.zr.at[p], self.send.at[4 + j], self.recv.at[5 + p], pc.zn[j - 1])

    def start(self):
        self.c0().start()

    def add(self, at, ref, ref_at):
        for k in self.unit.taps:
            idx = self.unit.tap(k) + at
            self.g[idx] = self.g[idx] + ref[k + ref_at]

    def step1(self):
        pc = self.pc
        self.c0().wait_recv()
        for y in range(2):
            for x in range(2):
                self.add((y, x, pc.c), self.rcv, (y, x))
        self.a1().start()
        self.b1().start()

    def step2(self):
        pc = self.pc
        own = (pc.y, pc.x, pc.c)
        self.a1().wait_recv()
        self.add((pc.oy, pc.x, pc.c) + self.cut[0], self.r1a, (pc.oy,))
        self.a2().start()
        self.b1().wait_recv()
        self.add((pc.y, pc.ox, pc.c) + self.cut[1], self.r1b, (pc.ox,))
        self.b2().start()
        self.add(own + self.cut[0], self.r1a, (pc.y,))
        self.add(own + self.cut[1], self.r1b, (pc.x,))

    def step3(self):
        pc = self.pc
        own = (pc.y, pc.x, pc.c)
        self.a2().wait_recv()
        self.add(own + self.cut[0], self.r2a, ())
        self.b2().wait_recv()
        self.add(own + self.cut[1], self.r2b, ())
        self.split(own)
        for j in (2, 1, 3):
            self.z(j).start()

    def split(self, own):
        h = self.zs.shape[1]
        n = self.g.shape[-1] // DP_RANKS
        if self.unit.name == "out":
            v = self.g[own]
            for i in range(DP_RANKS):
                at = slice(i * n, (i + 1) * n)
                self.zs[i, :, 0 : 2 * n] = jnp.concatenate([v[0:h, at], v[h : 2 * h, at]], axis=1)
            return
        parts = [self.g[self.unit.tap(k) + own] for k in self.unit.taps]
        for i in range(DP_RANKS):
            at = slice(i * n, (i + 1) * n)
            self.zs[i, :, 0 : len(parts) * n] = jnp.concatenate([v[:, at] for v in parts], axis=1)

    def step4(self, out):
        pc = self.pc
        total = self.zs[pc.d].astype(F32)
        for j in range(1, DP_RANKS):
            self.z_in(j).wait_recv()
            total = total + self.zr[pc.ranks[j]].astype(F32)
        out[...] = total

    def finish(self):
        for c in (self.c0(), self.a1(), self.b1(), self.a2(), self.b2()):
            c.wait_send()
        for j in range(1, DP_RANKS):
            self.z(j).wait_send()


class NormGather:
    SEMS = 7

    def __init__(self, pc, nz, nw, send, recv):
        self.pc, self.nz, self.nw, self.send, self.recv = pc, nz, nw, send, recv

    def z(self, j, p):
        pc = self.pc
        return remote(self.nz.at[p], self.nz.at[p], self.send.at[j - 1], self.recv.at[p], pc.zn[j - 1])

    def start(self):
        for j in range(1, DP_RANKS):
            self.z(j, self.pc.d).start()

    def stage(self, k):
        pc = self.pc
        ref = (self.nw.at[pc.y, pc.x, pc.c], self.nw.at[pc.y, pc.x], self.nw.at[pc.y])[k]
        return remote(ref, ref, self.send.at[3 + k], self.recv.at[4 + k], (pc.sib, pc.xn, pc.yn)[k])

    def stage_in(self, k):
        pc = self.pc
        ref = (self.nw.at[pc.y, pc.x, pc.oc], self.nw.at[pc.y, pc.ox], self.nw.at[pc.oy])[k]
        return remote(ref, ref, self.send.at[3 + k], self.recv.at[4 + k], (pc.sib, pc.xn, pc.yn)[k])

    def own(self):
        pc = self.pc
        for j in range(1, DP_RANKS):
            self.z(j, pc.ranks[j]).wait_recv()
        self.nw[pc.y, pc.x, pc.c] = jnp.concatenate([self.nz[i][0:2] for i in range(DP_RANKS)], axis=0)
        self.stage(0).start()

    def next(self, k):
        self.stage_in(k).wait_recv()
        if k < 2:
            self.stage(k + 1).start()

    def whole(self, width):
        return jnp.concatenate([self.nw[f // 4, (f // 2) % 2, f % 2][:, 0:width] for f in range(PLANE)], axis=1)

    def finish(self):
        for j in range(1, DP_RANKS):
            self.z(j, self.pc.d).wait_send()
        for k in range(3):
            self.stage(k).wait_send()


class SmallSum:
    SEMS = 10

    def __init__(self, pc, out, got, plane, zgot, send, recv):
        self.pc, self.out, self.got, self.plane, self.zgot = pc, out, got, plane, zgot
        self.send, self.recv = send, recv

    def near(self, m):
        pc = self.pc
        p = pc.plane[m]
        return remote(self.out.at[p], self.got.at[pc.f], self.send.at[m], self.recv.at[pc.f], {"fsdp": p})

    def near_in(self, m):
        p = self.pc.plane[m]
        return remote(self.out.at[p], self.got.at[p], self.send.at[m], self.recv.at[p], {"fsdp": p})

    def z(self, j):
        pc = self.pc
        return remote(self.plane, self.zgot.at[pc.d], self.send.at[6 + j], self.recv.at[PLANE + pc.d], pc.zn[j - 1])

    def z_in(self, j):
        pc = self.pc
        p = pc.ranks[j]
        return remote(self.plane, self.zgot.at[p], self.send.at[6 + j], self.recv.at[PLANE + p], pc.zn[j - 1])

    def start(self):
        for m in range(PLANE - 1):
            self.near(m).start()

    def along_z(self):
        pc = self.pc
        total = self.out[pc.f]
        for m in range(PLANE - 1):
            self.near_in(m).wait_recv()
        for m in range(PLANE - 1):
            total = total + self.got[pc.plane[m]]
        self.plane[...] = total
        for j in range(1, DP_RANKS):
            self.z(j).start()

    def total(self):
        total = self.plane[...]
        for j in range(1, DP_RANKS):
            self.z_in(j).wait_recv()
            total = total + self.zgot[self.pc.ranks[j]]
        return total

    def finish(self):
        for m in range(PLANE - 1):
            self.near(m).wait_send()
        for j in range(1, DP_RANKS):
            self.z(j).wait_send()


def lane_sum(v):
    parts = [v[:, i : i + 128] for i in range(0, v.shape[1], 128)]
    while len(parts) > 2:
        pairs = [a + b for a, b in zip(parts[::2], parts[1::2])]
        parts = pairs + parts[2 * len(pairs) :]
    return jnp.sum(sum(p.astype(F32) for p in parts), axis=1, keepdims=True)


def row_sum(v):
    parts = [v[i : i + 16] for i in range(0, v.shape[0], 16)]
    while len(parts) > 1:
        pairs = [a + b for a, b in zip(parts[::2], parts[1::2])]
        parts = pairs + parts[2 * len(pairs) :]
    f = parts[0].astype(F32)
    return f[0:8] + f[8:16]


def norm_back(n, r, gain, bias, e, sums, row):
    dz = e * gelu_grad(n * gain + bias)
    width = n.shape[1]
    sums[row : row + 1, 0:width] += jnp.sum(dz * n, axis=0, keepdims=True)
    sums[row + 1 : row + 2, 0:width] += jnp.sum(dz, axis=0, keepdims=True)
    dn = dz * gain
    m1 = jnp.mean(dn, axis=-1, keepdims=True)
    m2 = jnp.mean(dn * n, axis=-1, keepdims=True)
    return r * (dn - m1 - n * m2)


def block_kernel(r):
    pc = Place()
    x, cot, act_a, n_b, act_c = r.x, r.cot, r.act_a, r.n_b, r.act_c
    scale, sums, tail_rows = r.scale, r.sums, r.tail
    b_even, b_odd, g_even, g_odd, back_t = r.b_even, r.b_odd, r.g_even, r.g_odd, r.back_t
    rows, width = x.shape
    inner = n_b.shape[1]
    slots = r.lens.shape[0]
    seq = rows // slots
    blocks = seq // BLOCK
    grad_a = act_c

    wide = dict(zip([u.name for u in UNITS], (r.w_in, r.w_conv, r.w_conv, r.w_out)))
    own = {u.name: SimpleNamespace(**{k: getattr(r, k + u.name) for k in UNIT_SCRATCH}) for u in UNITS}
    pull = [Gather(pc, u, wide[u.name], own[u.name].zg_, own[u.name].gs_, own[u.name].gr_) for u in UNITS]
    get_in, get_c0, get_c1, get_out = pull

    def scatter(u, g):
        m = own[u.name]
        return Scatter(pc, u, g, m.rcv_, m.r1a_, m.r1b_, m.r2a_, m.r2b_, m.zg_, m.zr_, m.ss_, m.sr_)

    norm_gather = NormGather(pc, r.nz, r.nw, r.ns, r.nr)
    small = SmallSum(pc, r.sm_out, r.sm_got, r.sm_plane, r.sm_z, r.sm_s, r.sm_r)
    count_sum = SmallSum(pc, r.ct_out, r.ct_got, r.ct_plane, r.ct_z, r.ct_s, r.ct_r)

    load_x = pltpu.make_async_copy(r.tokens, x, r.io.at[0])
    load_cot = pltpu.make_async_copy(r.cot_in, cot, r.io.at[1])
    save_act = pltpu.make_async_copy(act_c, r.act_out, r.io.at[2])
    save_w = pltpu.make_async_copy(r.w_out, r.w_saved, r.io.at[3])
    load_x.start()

    cols = r.p_in.shape[0]
    r.nz[pc.d, 0:2, 0:cols] = r.p_norms[...].astype(BF16).astype(F32)
    barrier(pc)
    norm_gather.start()
    r.zg_in[pc.d, :, 0 : r.p_in.shape[1]] = r.p_in[...].astype(BF16)
    get_in.start()
    depth = r.p_conv.shape[1]
    for g in (get_c0, get_c1):
        for k in range(g.unit.count):
            g.zr[pc.d, :, k * depth : (k + 1) * depth] = r.p_conv[g.unit.first + k].T.astype(BF16)
    p_out = r.p_out[...].T.astype(BF16)
    h_out = r.zg_out.shape[1]
    r.zg_out[pc.d, :, 0 : 2 * depth] = jnp.concatenate([p_out[0:h_out], p_out[h_out : 2 * h_out]], axis=1)

    sums[...] = jnp.zeros_like(sums)
    pad = jnp.zeros((HALO, inner), BF16)
    for s in range(slots):
        for buf in (b_even, g_even):
            buf[s, 0:HALO, :] = pad
            buf[s, seq + HALO : seq + 2 * HALO, :] = pad

    def kept(s, first, count):
        return first + lax.broadcasted_iota(jnp.int32, (count, 1), 0) < r.lens[s]

    lab = r.labels[...]
    place = (
        lax.broadcasted_iota(jnp.int32, lab.shape, 0) * lab.shape[1] + lax.broadcasted_iota(jnp.int32, lab.shape, 1)
    )
    valid = place < 0
    for s in range(slots):
        valid = valid | ((place >= s * seq) & (place < s * seq + r.lens[s]))
    lane = lax.broadcasted_iota(jnp.int32, (8, 128), 1)
    counts = jnp.zeros((8, 128), F32)
    for c in range(TYPES):
        hits = jnp.sum(jnp.where(valid & (lab == c), 1.0, 0.0), keepdims=True)
        counts = counts + jnp.where(lane == c, hits, 0.0)
    for f in range(PLANE):
        r.ct_out[f] = counts
    count_sum.start()

    load_x.wait()
    load_cot.start()
    strip = STRIP
    strips = rows // strip

    def first_stats(i):
        at = block(i, strip)
        n, rs = stats(x[at, :].astype(F32))
        x[at, :] = n.astype(BF16)
        scale[at, 0:1] = rs

    loop(
        strips,
        first_stats,
        {
            strips // 4: [norm_gather.own],
            strips // 2: [lambda: norm_gather.next(0)],
            strips * 3 // 4: [get_c0.start, lambda: norm_gather.next(1)],
        },
    )
    get_in.own()
    norm_gather.next(2)
    r.norms[...] = norm_gather.whole(cols)
    norms = r.norms
    gain_a = jnp.concatenate([norms[0:1, :], norms[1:2, :]], axis=1)
    bias_a = jnp.concatenate([norms[2:3, :], norms[3:4, :]], axis=1)
    gain_b, bias_b, gain_c, bias_c = (norms[i : i + 1, :] for i in range(4, 8))

    def first_act(i):
        at = block(i, strip)
        act_a[at, :] = gelu(x[at, :].astype(F32) * gain_a + bias_a).astype(BF16)

    loop(strips, first_act)
    get_in.from_x()
    get_in.from_y()
    get_c0.own()
    get_c1.start()
    get_in.from_diagonal()
    get_in.from_sibling()
    w_in, w_conv, w_out = r.w_in, r.w_conv, r.w_out

    def flat(w):
        v = w[...]
        return v.reshape(PLANE * v.shape[3], v.shape[4])

    def skewed(steps, multiply, rest, hooks=None):
        def step(j):
            ahead = multiply(j * UNROLL)
            for u in range(UNROLL):
                now = ahead
                if u + 1 < UNROLL:
                    ahead = multiply(j * UNROLL + u + 1)
                rest(j * UNROLL + u, now)

        step.__name__ = multiply.__name__
        loop(steps // UNROLL, step, hooks)

    def place_of(j):
        return j // blocks, lax.rem(j, blocks) * BLOCK

    def shifted_store(even, odd, j, value):
        s, first = place_of(j)
        even[s, pl.ds(pl.multiple_of(first + HALO, 16), BLOCK), :] = value.astype(BF16)
        before = jnp.where(first == 0, 0.0, tail_rows[...])
        late = value[BLOCK - 8 :]
        odd[s, pl.ds(pl.multiple_of(first, 16), BLOCK), :] = jnp.concatenate(
            [before, value[: BLOCK - 8]], axis=0
        ).astype(BF16)
        odd[s, pl.ds(pl.multiple_of(first + BLOCK, 16), 16), :] = jnp.concatenate(
            [late, jnp.zeros_like(late)], axis=0
        ).astype(BF16)
        tail_rows[...] = late

    def tap_of(even, odd, k, sign):
        off = sign * DILATION_STRIDE * (k - KERNEL_TAPS // 2)
        return (even, HALO + off) if off % 16 == 0 else (odd, 8 + off)

    def taps(even, odd, j, sign):
        s, first = place_of(j)
        out = []
        for k in range(KERNEL_TAPS):
            buf, base = tap_of(even, odd, k, sign)
            out.append(buf[s, pl.ds(pl.multiple_of(first + base, 16), BLOCK), :])
        return jnp.concatenate(out, axis=1)

    def kept_in(j):
        s, first = place_of(j)
        return kept(s, first, BLOCK)

    total_blocks = slots * blocks

    def second(j):
        return dot_nt(act_a[block(j, BLOCK), :], flat(w_in))

    def second_rest(j, h):
        at = block(j, BLOCK)
        n, rs = stats(h)
        n_b[at, :] = n.astype(BF16)
        scale[at, 1:2] = rs
        shifted_store(b_even, b_odd, j, jnp.where(kept_in(j), gelu(n * gain_b + bias_b), 0.0))

    loop_end = total_blocks // UNROLL - 1
    chunk = 256
    skewed(
        total_blocks,
        second,
        second_rest,
        {loop_end // 2: [get_c1.own, get_out.start], loop_end: [get_c0.from_x, get_c0.from_y]},
    )
    get_c0.from_diagonal()
    get_c1.from_x()
    get_c1.from_y()
    get_c0.from_sibling()
    get_c1.from_diagonal()
    get_c1.from_sibling()
    get_out.own()

    def conv_rows():
        v = [w_conv[k].reshape(inner, inner) for k in range(KERNEL_TAPS)]
        return v

    def third(j):
        return dot_nt(taps(b_even, b_odd, j, 1), jnp.concatenate(conv_rows(), axis=1))

    def middle(n_c):
        def third_rest(j, h):
            at = block(j, BLOCK)
            n, rs = stats(h)
            n_c[at, :] = n.astype(BF16)
            scale[at, 2:3] = rs
            act_c[at, :] = jnp.where(kept_in(j), gelu(n * gain_c + bias_c), 0.0).astype(BF16)

        skewed(
            total_blocks,
            third,
            third_rest,
            {
                0: [count_sum.along_z],
                loop_end // 2: [get_out.from_x, get_out.from_y],
                loop_end - 1: [get_out.from_diagonal],
                loop_end: [get_out.from_sibling],
            },
        )
        save_act.start()
        save_w.start()
        load_cot.wait()
        for c in [norm_gather] + pull:
            c.finish()

        tall = r.g_out.shape[3]

        def out_grad(lo):
            part = dot_tn(cot[:, lo : lo + chunk], act_c[...]).astype(BF16)
            for f in range(lo // tall, -(-(lo + chunk) // tall)):
                a, b = max(lo, f * tall), min(lo + chunk, (f + 1) * tall)
                r.g_out[f // 4, (f // 2) % 2, f % 2, a - f * tall : b - f * tall, :] = part[a - lo : b - lo]

        for lo in range(0, width, chunk):
            once(out_grad, lo)
        put_out = scatter(UNITS[3], r.g_out)
        put_out.start()

        def fourth(j):
            return dot_nn(cot[block(j, BLOCK), :], flat(w_out))

        def fourth_rest(j, h):
            at = block(j, BLOCK)
            e = jnp.where(kept_in(j), h, 0.0)
            back = norm_back(n_c[at, :].astype(F32), scale[at, 2:3], gain_c, bias_c, e, sums, 4)
            shifted_store(g_even, g_odd, j, back)
            back_t[:, at] = back.astype(BF16).T

        skewed(total_blocks, fourth, fourth_rest, {0: [put_out.step1], 2: [put_out.step2]})

    pl.run_scoped(middle, pltpu.VMEM((rows, inner), BF16))
    put_out = scatter(UNITS[3], r.g_out)

    def late(g_in, g_conv):
        put_in, put_c0, put_c1 = scatter(UNITS[0], g_in), scatter(UNITS[1], g_conv), scatter(UNITS[2], g_conv)

        def conv_grad(k):
            buf, base = tap_of(b_even, b_odd, k, 1)
            for lo in range(0, inner, chunk):
                hi = min(lo + chunk, inner)
                total = None
                for s in range(slots):
                    p = dot_nn(back_t[:, s * seq : (s + 1) * seq], buf[s, base : base + seq, lo:hi])
                    total = p if total is None else total + p
                g_conv[k, :, :, :, :, lo:hi] = total.astype(BF16).reshape((2, 2, 2, inner // PLANE, hi - lo))

        for k in range(KERNEL_TAPS):
            once(conv_grad, k)
            if k == 0:
                put_out.step3()
            if k == 2:
                put_c0.start()
            if k == 3:
                put_c0.step1()
        put_c1.start()
        save_act.wait()
        save_w.wait()

        def sixth(j):
            return dot_nn(taps(g_even, g_odd, j, -1), w_conv[...].reshape(KERNEL_TAPS * inner, inner))

        def sixth_rest(j, h):
            at = block(j, BLOCK)
            e = jnp.where(kept_in(j), h, 0.0)
            back = norm_back(n_b[at, :].astype(F32), scale[at, 1:2], gain_b, bias_b, e, sums, 2).astype(BF16)
            grad_a[at, :] = back
            back_t[:, at] = back.T

        skewed(
            total_blocks,
            sixth,
            sixth_rest,
            {
                0: [put_c1.step1, lambda: put_out.step4(r.s_out)],
                1: [put_c0.step2],
                2: [put_c1.step2],
                loop_end: [put_c0.step3],
            },
        )

        def in_grad(j):
            part = dot_nn(back_t[...], act_a[:, j * chunk : (j + 1) * chunk]).astype(BF16)
            g_in[:, :, :, :, j * chunk : (j + 1) * chunk] = part.reshape(2, 2, 2, inner // PLANE, chunk)

        for j in range(width // chunk):
            once(in_grad, j)
        put_in.start()

        def out_copy(at):
            return pltpu.make_async_copy(cot.at[at, :], r.grad_tokens.at[at, :], r.io.at[4])

        low_gain, low_bias = gain_a.astype(BF16), bias_a.astype(BF16)

        def eighth(j):
            return dot_nn(grad_a[block(j, BLOCK), :], flat(w_in))

        def eighth_rest(j, h):
            d_gain = d_bias = None
            for at in range(0, BLOCK, FINE):
                here = pl.ds(pl.multiple_of(j * BLOCK + at, FINE), FINE)
                n = x[here, :]
                z = n * low_gain + low_bias
                zz = z * z
                t = jnp.tanh(z * (BF16(GELU_SCALE) + BF16(GELU_SCALE * GELU_CUBE) * zz))
                slope = z * (BF16(0.5 * GELU_SCALE) + BF16(1.5 * GELU_SCALE * GELU_CUBE) * zz)
                dz = h[at : at + FINE].astype(BF16) * ((BF16(0.5) + BF16(0.5) * t) + (slope - (t * t) * slope))
                a, b = row_sum(dz * n), row_sum(dz)
                d_gain, d_bias = (a, b) if d_gain is None else (d_gain + a, d_bias + b)
                dn = dz * low_gain
                m1 = lane_sum(dn) * (1.0 / width)
                m2 = lane_sum(dn * n) * (1.0 / width)
                m1, m2, rs = (jnp.broadcast_to(v, n.shape).astype(BF16) for v in (m1, m2, scale[here, 0:1]))
                cot[here, :] = cot[here, :] + rs * (dn - m1 - n * m2)
            sums[0:1, :] += jnp.sum(d_gain, axis=0, keepdims=True)
            sums[1:2, :] += jnp.sum(d_bias, axis=0, keepdims=True)
            out_copy(block(j, BLOCK)).start()

        skewed(
            total_blocks,
            eighth,
            eighth_rest,
            {
                0: [put_in.step1, put_c1.step3],
                1: [lambda: put_c0.step4(r.s_c0)],
                2: [put_in.step2],
                loop_end: [lambda: put_c1.step4(r.s_c1), put_in.step3],
            },
        )
        mine = jnp.concatenate(
            [
                sums[0:1, 0:inner],
                sums[0:1, inner : 2 * inner],
                sums[1:2, 0:inner],
                sums[1:2, inner : 2 * inner],
                sums[2:6, 0:inner],
            ],
            axis=0,
        )
        for f in range(PLANE):
            r.sm_out[f, :, 0:cols] = mine[:, f * cols : (f + 1) * cols]
        small.start()
        r.s_counts[...] = count_sum.total()
        small.along_z()
        total = small.total()
        pair = jnp.zeros((2, cols), F32)
        for i in range(DP_RANKS):
            pair = pair + jnp.where(pc.d == i, total[2 * i : 2 * i + 2, 0:cols], 0.0)
        r.s_norms[...] = pair
        put_in.step4(r.s_in)
        for c in (put_in, put_c0, put_c1, put_out, small, count_sum):
            c.finish()

        def eighth_end(_):
            pltpu.make_async_copy(cot, r.grad_tokens, r.io.at[4]).wait()

        once(eighth_end, 0)

    pl.run_scoped(late, pltpu.VMEM(r.w_in.shape, BF16), pltpu.VMEM(w_conv.shape, BF16))


UNIT_SCRATCH = ("zg_", "gs_", "gr_", "rcv_", "r1a_", "r1b_", "r2a_", "r2b_", "zr_", "ss_", "sr_")


def run_block(tokens, cotangent, lengths, labels, w_in, w_conv, w_out, norm_params):
    rows, width = tokens.shape
    cols, rank_in = w_in.shape
    depth = w_conv.shape[1]
    inner = cols * PLANE
    slots = lengths.shape[0]
    seq = rows // slots
    V = pltpu.VMEM
    dma = pltpu.SemaphoreType.DMA
    h_out = w_out.shape[1]
    inputs = dict(
        lens=(lengths, pltpu.SMEM),
        tokens=(tokens, pl.ANY),
        cot_in=(cotangent, pl.ANY),
        labels=(labels.reshape(rows // 128, 128), V),
        p_in=(w_in, V),
        p_conv=(w_conv, V),
        p_out=(w_out, V),
        p_norms=(norm_params, V),
    )
    outputs = dict(
        act_out=((rows, inner), BF16, pl.ANY),
        w_saved=((2, 2, 2, h_out, inner), BF16, pl.ANY),
        grad_tokens=((rows, width), BF16, pl.ANY),
        s_counts=((8, 128), F32, V),
        s_norms=(norm_params.shape, F32, V),
    )
    halo_rows = V((slots, seq + 2 * HALO, inner), BF16)
    taps = V((KERNEL_TAPS, 2, 2, 2, cols, inner), BF16)
    scratch = dict(
        x=V((rows, width), BF16),
        cot=V((rows, width), BF16),
        act_a=V((rows, width), BF16),
        n_b=V((rows, inner), BF16),
        act_c=V((rows, inner), BF16),
        scale=V((rows, 8), F32),
        sums=V((8, width), F32),
        tail=V((8, inner), F32),
        norms=V((8, inner), F32),
        back_t=V((inner, rows), BF16),
        b_even=halo_rows,
        b_odd=halo_rows,
        g_even=halo_rows,
        g_odd=halo_rows,
        w_in=V((2, 2, 2, cols, width), BF16),
        w_conv=taps,
        w_out=V((2, 2, 2, h_out, inner), BF16),
        g_out=V((2, 2, 2, h_out, inner), BF16),
        io=dma((5,)),
        nz=V((DP_RANKS, 8, 128), F32),
        nw=V((2, 2, 2, 8, 128), F32),
        ns=dma((NormGather.SEMS,)),
        nr=dma((NormGather.SEMS,)),
    )
    tile = (8, 128)
    for k in ("sm_", "ct_"):
        shapes = (
            V((PLANE,) + tile, F32),
            V((PLANE,) + tile, F32),
            V(tile, F32),
            V((DP_RANKS,) + tile, F32),
            dma((SmallSum.SEMS,)),
            dma((PLANE + DP_RANKS,)),
        )
        scratch.update(zip([k + n for n in ("out", "got", "plane", "z", "s", "r")], shapes))
    for u in UNITS:
        lead = (u.count,) if u.count else ()
        h, lanes = (cols, width) if u.name == "in" else (h_out, inner) if u.name == "out" else (cols, inner)
        piece = rank_in if u.name == "in" else depth * (u.count or 2)
        z = (cols, round_up(piece))
        half = u.sizes(h, lanes)
        outputs["s_" + u.name] = (z, F32, V)
        shapes = (
            V((DP_RANKS,) + z, BF16),
            dma((Gather.SEMS,)),
            dma((Gather.SEMS,)),
            V(lead + (2, 2, h, lanes), BF16),
            V(lead + (2,) + half[0], BF16),
            V(lead + (2,) + half[1], BF16),
            V(lead + half[0], BF16),
            V(lead + half[1], BF16),
            V((DP_RANKS,) + z, BF16),
            dma((Scatter.SEMS,)),
            dma((Scatter.SEMS,)),
        )
        scratch.update(zip([k + u.name for k in UNIT_SCRATCH], shapes))
    names = list(inputs) + list(outputs) + list(scratch)
    work = 6 * rows * (2 * width * inner + KERNEL_TAPS * inner * inner)
    out = pl.pallas_call(
        lambda *refs: block_kernel(SimpleNamespace(**dict(zip(names, refs)))),
        out_shape=tuple(jax.ShapeDtypeStruct(s, t) for s, t, _ in outputs.values()),
        in_specs=[pl.BlockSpec(memory_space=m) for _, m in inputs.values()],
        out_specs=tuple(pl.BlockSpec(memory_space=m) for _, _, m in outputs.values()),
        scratch_shapes=list(scratch.values()),
        compiler_params=pltpu.CompilerParams(
            collective_id=0, has_side_effects=True, vmem_limit_bytes=VMEM_BYTES
        ),
        cost_estimate=pl.CostEstimate(flops=work, bytes_accessed=8 * rows * width, transcendentals=0),
        name="residual_block",
    )(*(a for a, _ in inputs.values()))
    return dict(zip(outputs, out))


VMEM_BYTES = 63 * 1024 * 1024


def finish_kernel(r):
    rows = r.tokens.shape[0] // FINISH_PARTS
    loads = {}

    def load(k, src, dst):
        loads[k] = pltpu.make_async_copy(src, dst, r.in_sem.at[len(loads)])
        loads[k].start()

    parts = [pl.ds(i * rows, rows) for i in range(FINISH_PARTS)]
    for i, at in enumerate(parts):
        load(("a", i), r.act_out.at[at, :], r.hold_act.at[at, :])
        load(("t", i), r.tokens.at[at, :], r.hold_x.at[at, :])
        if i == 0:
            load("w", r.w_saved, r.hold_w)
        load(("g", i), r.grad_tokens.at[at, :], r.hold_g.at[at, :])
        if i == 1:
            for n in STEP_ORDER:
                load("s_" + n, getattr(r, "s_" + n), getattr(r, "bs_" + n))
                for kind in ("w_", "m_", "v_"):
                    if n != "c1":
                        load(kind + n, getattr(r, kind + n), getattr(r, "b" + kind + n))
            load("n", r.s_counts, r.bs_counts)
    stores = []

    def store(src, dst):
        stores.append(pltpu.make_async_copy(src, dst, r.out_sem.at[len(stores)]))
        stores[-1].start()

    def step(n, at, grad, rate, decay):
        new = adamw(getattr(r, "bw_" + n)[at], getattr(r, "bm_" + n)[at], getattr(r, "bv_" + n)[at], grad, rate, decay)
        for kind, value in zip(("ow_", "om_", "ov_"), new):
            getattr(r, kind + n)[at] = value

    def ready(n):
        for kind in ("s_", "w_", "m_", "v_"):
            if kind + n in loads:
                loads[kind + n].wait()

    def done(n):
        for kind in ("w_", "m_", "v_"):
            store(getattr(r, "o" + kind + n), getattr(r, "n" + kind + n))

    everything = (slice(None), slice(None))
    depth = r.bw_c0.shape[1]

    def conv_step():
        ready("c0")
        ready("c1")
        for u in UNITS[1:3]:
            for k in range(u.count):
                grad = getattr(r, "bs_" + u.name)[:, k * depth : (k + 1) * depth].T
                step("c0", (u.first + k,), grad, 0.5 * (KERNEL_TAPS * INNER) ** (-0.5), 0.01)
        done("c0")

    def in_step():
        ready("in")
        step("in", everything, r.bs_in[:, 0 : r.bw_in.shape[1]], 0.5 * D ** (-0.5), 0.01)
        done("in")

    def out_step():
        ready("out")
        flat = r.bs_out[...]
        grad = jnp.concatenate([flat[:, 0:depth].T, flat[:, depth : 2 * depth].T], axis=1)
        step("out", everything, grad, 0.5 * (INNER // 2) ** (-0.5), 0.01)
        done("out")
        ready("norms")
        step("norms", everything, r.bs_norms[...], 0.3, 0.0)
        done("norms")
        loads["n"].wait()
        r.type_counts[...] = r.bs_counts[0, 0:TYPES].astype(jnp.int32)

    others = [conv_step, in_step, out_step]
    loads["w"].wait()
    for i, at in enumerate(parts):
        loads[("a", i)].wait()
        loads[("t", i)].wait()
        w = r.hold_w[...]
        hid = dot_nt(r.hold_act[at, :], w.reshape(PLANE * w.shape[3], w.shape[4]))
        r.hold_x[at, :] = (r.hold_x[at, :].astype(F32) + hid).astype(BF16)
        store(r.hold_x.at[at, :], r.new_mixed.at[at, :])
        loads[("g", i)].wait()
        store(r.hold_g.at[at, :], r.new_grad_tokens.at[at, :])
        if 0 <= i - 2 < len(others):
            others[i - 2]()
    for c in stores:
        c.wait()


STEP_ORDER = ("c0", "c1", "in", "out", "norms")
FINISH_PARTS = 8


def run_finish(res, tokens, weights, means, squares):
    V, dma = pltpu.VMEM, pltpu.SemaphoreType.DMA
    inputs = {k: res[k] for k in ("act_out", "w_saved", "grad_tokens", "s_counts")}
    inputs["tokens"] = tokens
    held = []
    for n in STEP_ORDER:
        inputs["s_" + n] = res["s_" + n]
        held.append("s_" + n)
        if n in weights:
            for kind, arrays in (("w_", weights), ("m_", means), ("v_", squares)):
                inputs[kind + n] = arrays[n]
                held.append(kind + n)
    outputs = dict(new_mixed=tokens, new_grad_tokens=tokens)
    for kind in ("w_", "m_", "v_"):
        for n, a in weights.items():
            outputs["n" + kind + n] = a
    scratch = {"b" + k: V(inputs[k].shape, F32) for k in held + ["s_counts"]}
    for kind in ("ow_", "om_", "ov_"):
        scratch.update({kind + n: V(a.shape, F32) for n, a in weights.items()})
    whole = V(tokens.shape, BF16)
    scratch.update(hold_x=whole, hold_g=whole)
    scratch["hold_act"] = V(res["act_out"].shape, BF16)
    scratch["hold_w"] = V(res["w_saved"].shape, BF16)
    scratch.update(in_sem=dma((len(held) + 2 + 3 * FINISH_PARTS,)), out_sem=dma((12 + 2 * FINISH_PARTS,)))
    shapes = [jax.ShapeDtypeStruct(a.shape, a.dtype) for a in outputs.values()]
    names = list(inputs) + list(outputs) + ["type_counts"] + list(scratch)
    hbm = pl.BlockSpec(memory_space=pl.ANY)
    return pl.pallas_call(
        lambda *refs: finish_kernel(SimpleNamespace(**dict(zip(names, refs)))),
        out_shape=tuple(shapes) + (jax.ShapeDtypeStruct((TYPES,), jnp.int32),),
        in_specs=[hbm] * len(inputs),
        out_specs=(hbm,) * len(outputs) + (pl.BlockSpec(memory_space=V),),
        scratch_shapes=list(scratch.values()),
        compiler_params=pltpu.CompilerParams(vmem_limit_bytes=VMEM_BYTES),
        name="finish",
    )(*inputs.values())


def fused_body(
    tokens,
    cotangent,
    lengths,
    labels,
    w_in,
    w_conv,
    w_out,
    norm_params,
    mean_w_in,
    mean_w_conv,
    mean_w_out,
    mean_norms,
    square_w_in,
    square_w_conv,
    square_w_out,
    square_norms,
):
    res = run_block(tokens, cotangent, lengths, labels, w_in.T, w_conv, w_out, norm_params)
    names = ("in", "c0", "out", "norms")
    new = run_finish(
        res,
        tokens,
        dict(zip(names, (w_in.T, w_conv, w_out, norm_params))),
        dict(zip(names, (mean_w_in.T, mean_w_conv, mean_w_out, mean_norms))),
        dict(zip(names, (square_w_in.T, square_w_conv, square_w_out, square_norms))),
    )
    mixed, grad_tokens, *steps, counts = new
    for i in (0, 4, 8):
        steps[i] = steps[i].T
    return (mixed, grad_tokens, counts) + tuple(steps)


def solution(mesh):
    fused = mesh.shape["dp"] == DP_RANKS and mesh.shape["fsdp"] == PLANE
    return jax.shard_map(
        fused_body if fused else plain_body,
        mesh=mesh,
        in_specs=(
            P(("dp", "fsdp"), None),
            P(("dp", "fsdp"), None),
            P(("dp", "fsdp")),
            P(("dp", "fsdp")),
            P("dp", "fsdp"),
            P(None, "dp", "fsdp"),
            P("dp", "fsdp"),
            P("dp", "fsdp"),
            P("dp", "fsdp"),
            P(None, "dp", "fsdp"),
            P("dp", "fsdp"),
            P("dp", "fsdp"),
            P("dp", "fsdp"),
            P(None, "dp", "fsdp"),
            P("dp", "fsdp"),
            P("dp", "fsdp"),
        ),
        out_specs=(
            P(("dp", "fsdp"), None),
            P(("dp", "fsdp"), None),
            P(),
            P("dp", "fsdp"),
            P(None, "dp", "fsdp"),
            P("dp", "fsdp"),
            P("dp", "fsdp"),
            P("dp", "fsdp"),
            P(None, "dp", "fsdp"),
            P("dp", "fsdp"),
            P("dp", "fsdp"),
            P("dp", "fsdp"),
            P(None, "dp", "fsdp"),
            P("dp", "fsdp"),
            P("dp", "fsdp"),
        ),
        check_vma=False,
    )
```

```python
import functools
from types import SimpleNamespace

import jax
import jax.numpy as jnp
from jax import lax
from jax.experimental import pallas as pl
from jax.experimental.pallas import tpu as pltpu
from jax.sharding import PartitionSpec as P

D = 1280
INNER = 640
KERNEL_TAPS = 5
DILATION_STRIDE = 8
TYPES = 25
STEP = 5


EPSILON = 1e-05


def plain_normalize(value, gain, bias):
    center = value - jnp.mean(value, axis=-1, keepdims=True)
    spread = jnp.mean(center * center, axis=-1, keepdims=True)
    return center * lax.rsqrt(spread + EPSILON) * gain + bias


def activate(value):
    return jax.nn.gelu(value, approximate=True)


def norm_piece(value, gain, bias):
    return activate(plain_normalize(value, gain, bias))


def gather_params(first, second, third, fourth):
    part = (
        lax.all_gather(first, "fsdp", axis=1, tiled=True),
        lax.all_gather(second, "fsdp", axis=2, tiled=True),
        lax.all_gather(third, "fsdp", axis=1, tiled=True),
        lax.all_gather(fourth, "fsdp", axis=1, tiled=True),
    )
    return (
        lax.all_gather(part[0], "dp", axis=0, tiled=True),
        lax.all_gather(part[1], "dp", axis=1, tiled=True),
        lax.all_gather(part[2], "dp", axis=0, tiled=True),
        lax.all_gather(part[3], "dp", axis=0, tiled=True),
    )


def reduce_grads(first, second, third, fourth):
    part = (
        lax.psum_scatter(first, "fsdp", scatter_dimension=1, tiled=True),
        lax.psum_scatter(second, "fsdp", scatter_dimension=2, tiled=True),
        lax.psum_scatter(third, "fsdp", scatter_dimension=1, tiled=True),
        lax.psum_scatter(fourth, "fsdp", scatter_dimension=1, tiled=True),
    )
    return (
        lax.psum_scatter(
            part[0].astype(jnp.bfloat16), "dp", scatter_dimension=0, tiled=True
        ).astype(jnp.float32),
        lax.psum_scatter(
            part[1].astype(jnp.bfloat16), "dp", scatter_dimension=1, tiled=True
        ).astype(jnp.float32),
        lax.psum_scatter(
            part[2].astype(jnp.bfloat16), "dp", scatter_dimension=0, tiled=True
        ).astype(jnp.float32),
        lax.psum_scatter(
            part[3].astype(jnp.bfloat16), "dp", scatter_dimension=0, tiled=True
        ).astype(jnp.float32),
    )


def stack_taps(value_rows):
    sequence_rows = value_rows.shape[1]
    half_width = KERNEL_TAPS // 2
    padded_input = jnp.pad(
        value_rows, ((0, 0), (half_width * DILATION_STRIDE, half_width * DILATION_STRIDE), (0, 0))
    )
    return jnp.concatenate(
        [
            padded_input[
                :, tap_index * DILATION_STRIDE : tap_index * DILATION_STRIDE + sequence_rows
            ]
            for tap_index in range(KERNEL_TAPS)
        ],
        axis=-1,
    )


def unstack_taps(gradient_tree, sequence_rows):
    half_width = KERNEL_TAPS // 2
    padded_input = jnp.pad(
        gradient_tree,
        ((0, 0), (half_width * DILATION_STRIDE, half_width * DILATION_STRIDE), (0, 0), (0, 0)),
    )
    total_count = padded_input[
        :, 2 * half_width * DILATION_STRIDE : 2 * half_width * DILATION_STRIDE + sequence_rows, 0
    ]
    for tap_index in range(1, KERNEL_TAPS):
        start_offset = (2 * half_width - tap_index) * DILATION_STRIDE
        total_count = (
            total_count + padded_input[:, start_offset : start_offset + sequence_rows, tap_index]
        )
    return total_count


def adamw(master, mean_old, square_old, grad, rate, decay):
    mean_new = 0.5 * mean_old + 0.5 * grad
    square_new = 0.6 * square_old + 0.4 * grad * grad
    mean_hat = mean_new / (1.0 - 0.5**STEP)
    square_hat = square_new / (1.0 - 0.6**STEP)
    weight = master - rate * (mean_hat / (jnp.sqrt(square_hat) + 1e-08) + decay * master)
    return (weight, mean_new, square_new)


def contract_rows(left, right):
    return lax.dot_general(
        left, right, (((0,), (0,)), ((), ())), preferred_element_type=jnp.float32
    )


def contract_cols(left, right):
    return lax.dot_general(
        left, right, (((1,), (1,)), ((), ())), preferred_element_type=jnp.float32
    )


def plain_body(
    tokens,
    cotangent,
    lengths,
    labels,
    w_in,
    w_conv,
    w_out,
    norm_params,
    mean_w_in,
    mean_w_conv,
    mean_w_out,
    mean_norms,
    square_w_in,
    square_w_conv,
    square_w_out,
    square_norms,
):
    slots = lengths.shape[0]
    rows = tokens.shape[0]
    sequence_rows = rows // slots
    places = lax.broadcasted_iota(jnp.int32, (slots, sequence_rows), 1)
    valid = (places < lengths[:, None]).reshape(rows, 1)
    keep = valid.astype(jnp.float32)
    full_in, full_conv, full_out, full_norms = gather_params(
        w_in.astype(jnp.bfloat16),
        w_conv.astype(jnp.bfloat16),
        w_out.astype(jnp.bfloat16),
        norm_params.astype(jnp.bfloat16),
    )
    inner = full_in.shape[1]
    norms = full_norms.astype(jnp.float32)
    gain_a = norms[0:2].reshape(2 * inner)
    bias_a = norms[2:4].reshape(2 * inner)
    source = tokens.astype(jnp.float32)

    def masked_piece(value, gain, bias):
        return norm_piece(value, gain, bias) * keep

    act_a, back_a = jax.vjp(norm_piece, source, gain_a, bias_a)
    low_a = act_a.astype(jnp.bfloat16)
    hid_a = jnp.dot(low_a, full_in, preferred_element_type=jnp.float32)
    middle_activation, back_b = jax.vjp(masked_piece, hid_a, norms[4], norms[5])
    low_b = middle_activation.astype(jnp.bfloat16).reshape(slots, sequence_rows, inner)
    tap_weights = stack_taps(low_b).reshape(rows, KERNEL_TAPS * inner)
    conv_flat = full_conv.reshape(KERNEL_TAPS * inner, inner)
    middle_hidden = jnp.dot(tap_weights, conv_flat, preferred_element_type=jnp.float32)
    act_c, back_c = jax.vjp(norm_piece, middle_hidden, norms[6], norms[7])
    low_c = act_c.astype(jnp.bfloat16)
    hid_c = jnp.dot(low_c, full_out, preferred_element_type=jnp.float32)
    mixed = (source + keep * hid_c).astype(jnp.bfloat16)
    upstream = cotangent.astype(jnp.float32)
    grad_c = (keep * upstream).astype(jnp.bfloat16)
    grad_out = contract_rows(low_c, grad_c)
    d_act_c = contract_cols(grad_c, full_out)
    d_hid_b, d_gain_c, d_bias_c = back_c(d_act_c)
    grad_b = d_hid_b.astype(jnp.bfloat16)
    grad_conv = contract_rows(tap_weights, grad_b).reshape(KERNEL_TAPS, inner, inner)
    d_taps = contract_cols(grad_b, conv_flat)
    d_act_b = unstack_taps(
        d_taps.reshape(slots, sequence_rows, KERNEL_TAPS, inner), sequence_rows
    ).reshape(rows, inner)
    d_hid_a, d_gain_b, d_bias_b = back_b(d_act_b)
    grad_a = d_hid_a.astype(jnp.bfloat16)
    grad_in = contract_rows(low_a, grad_a)
    d_act_a = contract_cols(grad_a, full_in)
    d_source, d_gain_a, d_bias_a = back_a(d_act_a)
    grad_tokens = (upstream + d_source).astype(jnp.bfloat16)
    grad_norms = jnp.concatenate(
        [
            d_gain_a.reshape(2, inner),
            d_bias_a.reshape(2, inner),
            d_gain_b[None],
            d_bias_b[None],
            d_gain_c[None],
            d_bias_c[None],
        ],
        axis=0,
    )
    sum_in, sum_conv, sum_out, sum_norms = reduce_grads(grad_in, grad_conv, grad_out, grad_norms)
    kinds = lax.broadcasted_iota(jnp.int32, (1, TYPES), 1)
    hits = (labels[:, None] == kinds) & valid
    local_counts = jnp.sum(hits.astype(jnp.int32), axis=0)
    type_counts = lax.psum(local_counts, ("dp", "fsdp"))
    new_in = adamw(w_in, mean_w_in, square_w_in, sum_in, 0.5 * D ** (-0.5), 0.01)
    new_conv = adamw(
        w_conv, mean_w_conv, square_w_conv, sum_conv, 0.5 * (KERNEL_TAPS * INNER) ** (-0.5), 0.01
    )
    new_out = adamw(w_out, mean_w_out, square_w_out, sum_out, 0.5 * (INNER // 2) ** (-0.5), 0.01)
    new_norm = adamw(norm_params, mean_norms, square_norms, sum_norms, 0.3, 0.0)
    return (
        mixed,
        grad_tokens,
        type_counts,
        new_in[0],
        new_conv[0],
        new_out[0],
        new_norm[0],
        new_in[1],
        new_conv[1],
        new_out[1],
        new_norm[1],
        new_in[2],
        new_conv[2],
        new_out[2],
        new_norm[2],
    )


F32, BF16 = jnp.float32, jnp.bfloat16
MESH = pl.DeviceIdType.MESH
DP_RANKS, PLANE = 4, 8
HALO = (KERNEL_TAPS // 2) * DILATION_STRIDE
GELU_SCALE, GELU_CUBE = 0.7978845608, 0.044715
BLOCK = 256
STRIP = 128
FINE = 64
UNROLL = 2


def dot_nn(a, b):
    return lax.dot_general(a, b, (((1,), (0,)), ((), ())), preferred_element_type=F32)


def dot_nt(a, b):
    return lax.dot_general(a, b, (((1,), (1,)), ((), ())), preferred_element_type=F32)


def dot_tn(a, b):
    return lax.dot_general(a, b, (((0,), (0,)), ((), ())), preferred_element_type=F32)


def gelu(z):
    t = jnp.tanh(z * (GELU_SCALE + (GELU_SCALE * GELU_CUBE) * (z * z)))
    h = 0.5 * z
    return h + h * t


def gelu_grad(z):
    zz = z * z
    t = jnp.tanh(z * (GELU_SCALE + (GELU_SCALE * GELU_CUBE) * zz))
    slope = z * (GELU_SCALE + (3.0 * GELU_SCALE * GELU_CUBE) * zz)
    return 0.5 * (1.0 + t + (1.0 - t * t) * slope)


def stats(x):
    c = x - jnp.mean(x, axis=-1, keepdims=True)
    r = lax.rsqrt(jnp.mean(c * c, axis=-1, keepdims=True) + EPSILON)
    return c * r, r


def loop(n, step, hooks=None):
    def one(i, carry):
        step(i)
        for at, calls in (hooks or {}).items():

            @pl.when(i == at)
            def _(calls=calls):
                for call in calls:
                    call()

        return carry

    lax.fori_loop(0, n, one, 0)


def once(step, i):
    step(i)


def block(i, n):
    return pl.ds(pl.multiple_of(i * n, n), n)


def round_up(n, m=128):
    return -(-n // m) * m


class Place:
    def __init__(self):
        self.d = lax.axis_index("dp")
        f = lax.axis_index("fsdp")
        self.f = f
        self.c, self.x, self.y = f % 2, (f // 2) % 2, f // 4
        self.oc, self.ox, self.oy = 1 - self.c, 1 - self.x, 1 - self.y
        self.ranks = [(self.d + j) % DP_RANKS for j in range(DP_RANKS)]
        self.sib = {"fsdp": f + 1 - 2 * self.c}
        self.xn = {"fsdp": f + 2 - 4 * self.x}
        self.yn = {"fsdp": f + 4 - 8 * self.y}
        self.zn = [{"dp": p} for p in self.ranks[1:]]
        bits = [(m // 4, m // 2 % 2, m % 2) for m in range(1, PLANE)]
        self.plane = [
            4 * (self.oy if y else self.y) + 2 * (self.ox if x else self.x) + (self.oc if c else self.c)
            for y, x, c in bits
        ]


def barrier(pc):
    sem = pltpu.get_barrier_semaphore()
    peers = [{"fsdp": p} for p in pc.plane] + pc.zn
    for p in peers:
        pl.semaphore_signal(sem, inc=1, device_id=p, device_id_type=MESH)
    pl.semaphore_wait(sem, len(peers))


def remote(src, dst, send, recv, device):
    return pltpu.make_async_remote_copy(
        src_ref=src, dst_ref=dst, send_sem=send, recv_sem=recv, device_id=device, device_id_type=MESH
    )


class Unit:
    def __init__(self, name, first=0, count=0):
        self.name, self.first, self.count = name, first, count
        self.lead = (pl.ds(first, count),) if count else ()
        self.taps = [(k,) for k in range(count)] or [()]

    def tap(self, k):
        return (k[0] + self.first,) if k else ()

    def halves(self, h, lanes):
        if self.name == "out":
            return (slice(0, h // 2), slice(None)), (slice(h // 2, h), slice(None))
        cut = lanes // 2 // 128 * 128
        if self.first == 0:
            cut = lanes - cut
        return (slice(None), slice(0, cut)), (slice(None), slice(cut, lanes))

    def sizes(self, h, lanes):
        return [tuple(len(range(*c.indices(e))) for c, e in zip(cut, (h, lanes))) for cut in self.halves(h, lanes)]


UNITS = (Unit("in"), Unit("c0", 0, 3), Unit("c1", 3, 2), Unit("out"))


class Gather:
    SEMS = 13

    def __init__(self, pc, unit, w, zr, send, recv):
        self.pc, self.unit, self.w, self.zr, self.send, self.recv = pc, unit, w, zr, send, recv
        self.cut = unit.halves(*w.shape[-2:])
        self.sent = []

    def z(self, j):
        pc = self.pc
        mine = self.zr.at[pc.d]
        return remote(mine, mine, self.send.at[j - 1], self.recv.at[pc.d], pc.zn[j - 1])

    def z_in(self, j):
        pc = self.pc
        p = pc.ranks[j]
        return remote(self.zr.at[p], self.zr.at[p], self.send.at[j - 1], self.recv.at[p], pc.zn[j - 1])

    def start(self):
        for j in (2, 1, 3):
            self.z(j).start()

    def go(self, ref, i, device):
        c = remote(ref, ref, self.send.at[i], self.recv.at[i], device)
        c.start()
        self.sent.append((i, ref, device))

    def arrived(self, i, ref):
        remote(ref, ref, self.send.at[i], self.recv.at[i], self.pc.sib).wait_recv()

    def at(self, y, x, c, half=None):
        part = self.cut[half] if half is not None else (slice(None), slice(None))
        return self.w.at[self.unit.lead + (y, x, c) + part]

    def own(self):
        pc = self.pc
        for j in range(1, DP_RANKS):
            self.z_in(j).wait_recv()
        self.assemble()
        mine = self.at(pc.y, pc.x, pc.c)
        self.go(mine, 4, pc.xn)
        self.go(mine, 5, pc.yn)
        self.go(mine, 8, pc.sib)

    def assemble(self):
        own = (self.pc.y, self.pc.x, self.pc.c)
        h = self.zr.shape[1]
        n = self.w.shape[-1] // DP_RANKS
        pieces = [self.zr[i] for i in range(DP_RANKS)]
        if self.unit.name == "out":
            for part in range(2):
                joined = jnp.concatenate([p[:, part * n : (part + 1) * n] for p in pieces], axis=1)
                self.w[own + (slice(part * h, (part + 1) * h),)] = joined
            return
        for k in self.unit.taps:
            at = k[0] * n if k else 0
            self.w[self.unit.tap(k) + own] = jnp.concatenate([p[:, at : at + n] for p in pieces], axis=1)

    def from_x(self):
        pc = self.pc
        r = self.at(pc.y, pc.ox, pc.c)
        self.arrived(4, r)
        self.go(self.at(pc.y, pc.ox, pc.c, 1), 7, pc.yn)
        self.go(r, 9, pc.sib)

    def from_y(self):
        pc = self.pc
        r = self.at(pc.oy, pc.x, pc.c)
        self.arrived(5, r)
        self.go(self.at(pc.oy, pc.x, pc.c, 0), 6, pc.xn)
        self.go(r, 10, pc.sib)

    def from_diagonal(self):
        pc = self.pc
        for half in (0, 1):
            r = self.at(pc.oy, pc.ox, pc.c, half)
            self.arrived(6 + half, r)
            self.go(r, 11 + half, pc.sib)

    def from_sibling(self):
        pc = self.pc
        o = pc.oc
        self.arrived(8, self.at(pc.y, pc.x, o))
        self.arrived(9, self.at(pc.y, pc.ox, o))
        self.arrived(10, self.at(pc.oy, pc.x, o))
        for half in (0, 1):
            self.arrived(11 + half, self.at(pc.oy, pc.ox, o, half))

    def finish(self):
        for j in range(1, DP_RANKS):
            self.z(j).wait_send()
        for i, ref, device in self.sent:
            remote(ref, ref, self.send.at[i], self.recv.at[i], device).wait_send()


class Scatter:
    SEMS = 9

    def __init__(self, pc, unit, g, rcv, r1a, r1b, r2a, r2b, zs, zr, send, recv):
        self.pc, self.unit, self.g, self.rcv = pc, unit, g, rcv
        self.r1a, self.r1b, self.r2a, self.r2b = r1a, r1b, r2a, r2b
        self.zs, self.zr, self.send, self.recv = zs, zr, send, recv
        self.cut = unit.halves(*g.shape[-2:])

    def copy(self, i, at, dst, device):
        return remote(self.g.at[self.unit.lead + at], dst, self.send.at[i], self.recv.at[i], device)

    def c0(self):
        pc = self.pc
        every = slice(None)
        return self.copy(0, (every, every, pc.oc), self.rcv, pc.sib)

    def a1(self):
        pc = self.pc
        return self.copy(1, (slice(None), pc.ox, pc.c) + self.cut[0], self.r1a, pc.xn)

    def b1(self):
        pc = self.pc
        return self.copy(2, (pc.oy, slice(None), pc.c) + self.cut[1], self.r1b, pc.yn)

    def a2(self):
        pc = self.pc
        return self.copy(3, (pc.oy, pc.x, pc.c) + self.cut[0], self.r2a, pc.yn)

    def b2(self):
        pc = self.pc
        return self.copy(4, (pc.y, pc.ox, pc.c) + self.cut[1], self.r2b, pc.xn)

    def z(self, j):
        pc = self.pc
        return remote(self.zs.at[pc.ranks[j]], self.zr.at[pc.d], self.send.at[4 + j], self.recv.at[5 + pc.d], pc.zn[j - 1])

    def z_in(self, j):
        pc = self.pc
        p = pc.ranks[j]
        return remote(self.zs.at[p], self.zr.at[p], self.send.at[4 + j], self.recv.at[5 + p], pc.zn[j - 1])

    def start(self):
        self.c0().start()

    def add(self, at, ref, ref_at):
        for k in self.unit.taps:
            idx = self.unit.tap(k) + at
            self.g[idx] = self.g[idx] + ref[k + ref_at]

    def step1(self):
        pc = self.pc
        self.c0().wait_recv()
        for y in range(2):
            for x in range(2):
                self.add((y, x, pc.c), self.rcv, (y, x))
        self.a1().start()
        self.b1().start()

    def step2(self):
        pc = self.pc
        own = (pc.y, pc.x, pc.c)
        self.a1().wait_recv()
        self.add((pc.oy, pc.x, pc.c) + self.cut[0], self.r1a, (pc.oy,))
        self.a2().start()
        self.b1().wait_recv()
        self.add((pc.y, pc.ox, pc.c) + self.cut[1], self.r1b, (pc.ox,))
        self.b2().start()
        self.add(own + self.cut[0], self.r1a, (pc.y,))
        self.add(own + self.cut[1], self.r1b, (pc.x,))

    def step3(self):
        pc = self.pc
        own = (pc.y, pc.x, pc.c)
        self.a2().wait_recv()
        self.add(own + self.cut[0], self.r2a, ())
        self.b2().wait_recv()
        self.add(own + self.cut[1], self.r2b, ())
        self.split(own)
        for j in (2, 1, 3):
            self.z(j).start()

    def split(self, own):
        h = self.zs.shape[1]
        n = self.g.shape[-1] // DP_RANKS
        if self.unit.name == "out":
            v = self.g[own]
            for i in range(DP_RANKS):
                at = slice(i * n, (i + 1) * n)
                self.zs[i, :, 0 : 2 * n] = jnp.concatenate([v[0:h, at], v[h : 2 * h, at]], axis=1)
            return
        parts = [self.g[self.unit.tap(k) + own] for k in self.unit.taps]
        for i in range(DP_RANKS):
            at = slice(i * n, (i + 1) * n)
            self.zs[i, :, 0 : len(parts) * n] = jnp.concatenate([v[:, at] for v in parts], axis=1)

    def step4(self, out):
        pc = self.pc
        total = self.zs[pc.d].astype(F32)
        for j in range(1, DP_RANKS):
            self.z_in(j).wait_recv()
            total = total + self.zr[pc.ranks[j]].astype(F32)
        out[...] = total

    def finish(self):
        for c in (self.c0(), self.a1(), self.b1(), self.a2(), self.b2()):
            c.wait_send()
        for j in range(1, DP_RANKS):
            self.z(j).wait_send()


class NormGather:
    SEMS = 7

    def __init__(self, pc, nz, nw, send, recv):
        self.pc, self.nz, self.nw, self.send, self.recv = pc, nz, nw, send, recv

    def z(self, j, p):
        pc = self.pc
        return remote(self.nz.at[p], self.nz.at[p], self.send.at[j - 1], self.recv.at[p], pc.zn[j - 1])

    def start(self):
        for j in range(1, DP_RANKS):
            self.z(j, self.pc.d).start()

    def stage(self, k):
        pc = self.pc
        ref = (self.nw.at[pc.y, pc.x, pc.c], self.nw.at[pc.y, pc.x], self.nw.at[pc.y])[k]
        return remote(ref, ref, self.send.at[3 + k], self.recv.at[4 + k], (pc.sib, pc.xn, pc.yn)[k])

    def stage_in(self, k):
        pc = self.pc
        ref = (self.nw.at[pc.y, pc.x, pc.oc], self.nw.at[pc.y, pc.ox], self.nw.at[pc.oy])[k]
        return remote(ref, ref, self.send.at[3 + k], self.recv.at[4 + k], (pc.sib, pc.xn, pc.yn)[k])

    def own(self):
        pc = self.pc
        for j in range(1, DP_RANKS):
            self.z(j, pc.ranks[j]).wait_recv()
        self.nw[pc.y, pc.x, pc.c] = jnp.concatenate([self.nz[i][0:2] for i in range(DP_RANKS)], axis=0)
        self.stage(0).start()

    def next(self, k):
        self.stage_in(k).wait_recv()
        if k < 2:
            self.stage(k + 1).start()

    def whole(self, width):
        return jnp.concatenate([self.nw[f // 4, (f // 2) % 2, f % 2][:, 0:width] for f in range(PLANE)], axis=1)

    def finish(self):
        for j in range(1, DP_RANKS):
            self.z(j, self.pc.d).wait_send()
        for k in range(3):
            self.stage(k).wait_send()


class SmallSum:
    SEMS = 10

    def __init__(self, pc, out, got, plane, zgot, send, recv):
        self.pc, self.out, self.got, self.plane, self.zgot = pc, out, got, plane, zgot
        self.send, self.recv = send, recv

    def near(self, m):
        pc = self.pc
        p = pc.plane[m]
        return remote(self.out.at[p], self.got.at[pc.f], self.send.at[m], self.recv.at[pc.f], {"fsdp": p})

    def near_in(self, m):
        p = self.pc.plane[m]
        return remote(self.out.at[p], self.got.at[p], self.send.at[m], self.recv.at[p], {"fsdp": p})

    def z(self, j):
        pc = self.pc
        return remote(self.plane, self.zgot.at[pc.d], self.send.at[6 + j], self.recv.at[PLANE + pc.d], pc.zn[j - 1])

    def z_in(self, j):
        pc = self.pc
        p = pc.ranks[j]
        return remote(self.plane, self.zgot.at[p], self.send.at[6 + j], self.recv.at[PLANE + p], pc.zn[j - 1])

    def start(self):
        for m in range(PLANE - 1):
            self.near(m).start()

    def along_z(self):
        pc = self.pc
        total = self.out[pc.f]
        for m in range(PLANE - 1):
            self.near_in(m).wait_recv()
        for m in range(PLANE - 1):
            total = total + self.got[pc.plane[m]]
        self.plane[...] = total
        for j in range(1, DP_RANKS):
            self.z(j).start()

    def total(self):
        total = self.plane[...]
        for j in range(1, DP_RANKS):
            self.z_in(j).wait_recv()
            total = total + self.zgot[self.pc.ranks[j]]
        return total

    def finish(self):
        for m in range(PLANE - 1):
            self.near(m).wait_send()
        for j in range(1, DP_RANKS):
            self.z(j).wait_send()


def lane_sum(v):
    parts = [v[:, i : i + 128] for i in range(0, v.shape[1], 128)]
    while len(parts) > 2:
        pairs = [a + b for a, b in zip(parts[::2], parts[1::2])]
        parts = pairs + parts[2 * len(pairs) :]
    return jnp.sum(sum(p.astype(F32) for p in parts), axis=1, keepdims=True)


def row_sum(v):
    parts = [v[i : i + 16] for i in range(0, v.shape[0], 16)]
    while len(parts) > 1:
        pairs = [a + b for a, b in zip(parts[::2], parts[1::2])]
        parts = pairs + parts[2 * len(pairs) :]
    f = parts[0].astype(F32)
    return f[0:8] + f[8:16]


def norm_back(n, r, gain, bias, e, sums, row):
    dz = e * gelu_grad(n * gain + bias)
    width = n.shape[1]
    sums[row : row + 1, 0:width] += jnp.sum(dz * n, axis=0, keepdims=True)
    sums[row + 1 : row + 2, 0:width] += jnp.sum(dz, axis=0, keepdims=True)
    dn = dz * gain
    m1 = jnp.mean(dn, axis=-1, keepdims=True)
    m2 = jnp.mean(dn * n, axis=-1, keepdims=True)
    return r * (dn - m1 - n * m2)


def block_kernel(r):
    pc = Place()
    x, cot, act_a, n_b, act_c = r.x, r.cot, r.act_a, r.n_b, r.act_c
    scale, sums, tail_rows = r.scale, r.sums, r.tail
    b_even, b_odd, g_even, g_odd, back_t = r.b_even, r.b_odd, r.g_even, r.g_odd, r.back_t
    rows, width = x.shape
    inner = n_b.shape[1]
    slots = r.lens.shape[0]
    seq = rows // slots
    blocks = seq // BLOCK
    grad_a = act_c

    wide = dict(zip([u.name for u in UNITS], (r.w_in, r.w_conv, r.w_conv, r.w_out)))
    own = {u.name: SimpleNamespace(**{k: getattr(r, k + u.name) for k in UNIT_SCRATCH}) for u in UNITS}
    pull = [Gather(pc, u, wide[u.name], own[u.name].zg_, own[u.name].gs_, own[u.name].gr_) for u in UNITS]
    get_in, get_c0, get_c1, get_out = pull

    def scatter(u, g):
        m = own[u.name]
        return Scatter(pc, u, g, m.rcv_, m.r1a_, m.r1b_, m.r2a_, m.r2b_, m.zg_, m.zr_, m.ss_, m.sr_)

    norm_gather = NormGather(pc, r.nz, r.nw, r.ns, r.nr)
    small = SmallSum(pc, r.sm_out, r.sm_got, r.sm_plane, r.sm_z, r.sm_s, r.sm_r)
    count_sum = SmallSum(pc, r.ct_out, r.ct_got, r.ct_plane, r.ct_z, r.ct_s, r.ct_r)

    load_x = pltpu.make_async_copy(r.tokens, x, r.io.at[0])
    load_cot = pltpu.make_async_copy(r.cot_in, cot, r.io.at[1])
    save_act = pltpu.make_async_copy(act_c, r.act_out, r.io.at[2])
    save_w = pltpu.make_async_copy(r.w_out, r.w_saved, r.io.at[3])
    load_x.start()

    cols = r.p_in.shape[0]
    r.nz[pc.d, 0:2, 0:cols] = r.p_norms[...].astype(BF16).astype(F32)
    barrier(pc)
    norm_gather.start()
    r.zg_in[pc.d, :, 0 : r.p_in.shape[1]] = r.p_in[...].astype(BF16)
    get_in.start()
    depth = r.p_conv.shape[1]
    for g in (get_c0, get_c1):
        for k in range(g.unit.count):
            g.zr[pc.d, :, k * depth : (k + 1) * depth] = r.p_conv[g.unit.first + k].T.astype(BF16)
    p_out = r.p_out[...].T.astype(BF16)
    h_out = r.zg_out.shape[1]
    r.zg_out[pc.d, :, 0 : 2 * depth] = jnp.concatenate([p_out[0:h_out], p_out[h_out : 2 * h_out]], axis=1)

    sums[...] = jnp.zeros_like(sums)
    pad = jnp.zeros((HALO, inner), BF16)
    for s in range(slots):
        for buf in (b_even, g_even):
            buf[s, 0:HALO, :] = pad
            buf[s, seq + HALO : seq + 2 * HALO, :] = pad

    def kept(s, first, count):
        return first + lax.broadcasted_iota(jnp.int32, (count, 1), 0) < r.lens[s]

    lab = r.labels[...]
    place = (
        lax.broadcasted_iota(jnp.int32, lab.shape, 0) * lab.shape[1] + lax.broadcasted_iota(jnp.int32, lab.shape, 1)
    )
    valid = place < 0
    for s in range(slots):
        valid = valid | ((place >= s * seq) & (place < s * seq + r.lens[s]))
    lane = lax.broadcasted_iota(jnp.int32, (8, 128), 1)
    counts = jnp.zeros((8, 128), F32)
    for c in range(TYPES):
        hits = jnp.sum(jnp.where(valid & (lab == c), 1.0, 0.0), keepdims=True)
        counts = counts + jnp.where(lane == c, hits, 0.0)
    for f in range(PLANE):
        r.ct_out[f] = counts
    count_sum.start()

    load_x.wait()
    load_cot.start()
    strip = STRIP
    strips = rows // strip

    def first_stats(i):
        at = block(i, strip)
        n, rs = stats(x[at, :].astype(F32))
        x[at, :] = n.astype(BF16)
        scale[at, 0:1] = rs

    loop(
        strips,
        first_stats,
        {
            strips // 4: [norm_gather.own],
            strips // 2: [lambda: norm_gather.next(0)],
            strips * 3 // 4: [get_c0.start, lambda: norm_gather.next(1)],
        },
    )
    get_in.own()
    norm_gather.next(2)
    r.norms[...] = norm_gather.whole(cols)
    norms = r.norms
    gain_a = jnp.concatenate([norms[0:1, :], norms[1:2, :]], axis=1)
    bias_a = jnp.concatenate([norms[2:3, :], norms[3:4, :]], axis=1)
    gain_b, bias_b, gain_c, bias_c = (norms[i : i + 1, :] for i in range(4, 8))

    def first_act(i):
        at = block(i, strip)
        act_a[at, :] = gelu(x[at, :].astype(F32) * gain_a + bias_a).astype(BF16)

    loop(strips, first_act)
    get_in.from_x()
    get_in.from_y()
    get_c0.own()
    get_c1.start()
    get_in.from_diagonal()
    get_in.from_sibling()
    w_in, w_conv, w_out = r.w_in, r.w_conv, r.w_out

    def flat(w):
        v = w[...]
        return v.reshape(PLANE * v.shape[3], v.shape[4])

    def skewed(steps, multiply, rest, hooks=None):
        def step(j):
            ahead = multiply(j * UNROLL)
            for u in range(UNROLL):
                now = ahead
                if u + 1 < UNROLL:
                    ahead = multiply(j * UNROLL + u + 1)
                rest(j * UNROLL + u, now)

        step.__name__ = multiply.__name__
        loop(steps // UNROLL, step, hooks)

    def place_of(j):
        return j // blocks, lax.rem(j, blocks) * BLOCK

    def shifted_store(even, odd, j, value):
        s, first = place_of(j)
        even[s, pl.ds(pl.multiple_of(first + HALO, 16), BLOCK), :] = value.astype(BF16)
        before = jnp.where(first == 0, 0.0, tail_rows[...])
        late = value[BLOCK - 8 :]
        odd[s, pl.ds(pl.multiple_of(first, 16), BLOCK), :] = jnp.concatenate(
            [before, value[: BLOCK - 8]], axis=0
        ).astype(BF16)
        odd[s, pl.ds(pl.multiple_of(first + BLOCK, 16), 16), :] = jnp.concatenate(
            [late, jnp.zeros_like(late)], axis=0
        ).astype(BF16)
        tail_rows[...] = late

    def tap_of(even, odd, k, sign):
        off = sign * DILATION_STRIDE * (k - KERNEL_TAPS // 2)
        return (even, HALO + off) if off % 16 == 0 else (odd, 8 + off)

    def taps(even, odd, j, sign):
        s, first = place_of(j)
        out = []
        for k in range(KERNEL_TAPS):
            buf, base = tap_of(even, odd, k, sign)
            out.append(buf[s, pl.ds(pl.multiple_of(first + base, 16), BLOCK), :])
        return jnp.concatenate(out, axis=1)

    def kept_in(j):
        s, first = place_of(j)
        return kept(s, first, BLOCK)

    total_blocks = slots * blocks

    def second(j):
        return dot_nt(act_a[block(j, BLOCK), :], flat(w_in))

    def second_rest(j, h):
        at = block(j, BLOCK)
        n, rs = stats(h)
        n_b[at, :] = n.astype(BF16)
        scale[at, 1:2] = rs
        shifted_store(b_even, b_odd, j, jnp.where(kept_in(j), gelu(n * gain_b + bias_b), 0.0))

    loop_end = total_blocks // UNROLL - 1
    chunk = 256
    skewed(
        total_blocks,
        second,
        second_rest,
        {loop_end // 2: [get_c1.own, get_out.start], loop_end: [get_c0.from_x, get_c0.from_y]},
    )
    get_c0.from_diagonal()
    get_c1.from_x()
    get_c1.from_y()
    get_c0.from_sibling()
    get_c1.from_diagonal()
    get_c1.from_sibling()
    get_out.own()

    def conv_rows():
        v = [w_conv[k].reshape(inner, inner) for k in range(KERNEL_TAPS)]
        return v

    def third(j):
        return dot_nt(taps(b_even, b_odd, j, 1), jnp.concatenate(conv_rows(), axis=1))

    def middle(n_c):
        def third_rest(j, h):
            at = block(j, BLOCK)
            n, rs = stats(h)
            n_c[at, :] = n.astype(BF16)
            scale[at, 2:3] = rs
            act_c[at, :] = jnp.where(kept_in(j), gelu(n * gain_c + bias_c), 0.0).astype(BF16)

        skewed(
            total_blocks,
            third,
            third_rest,
            {
                0: [count_sum.along_z],
                loop_end // 2: [get_out.from_x, get_out.from_y],
                loop_end: [get_out.from_diagonal],
            },
        )
        save_act.start()
        load_cot.wait()

        tall = r.g_out.shape[3]

        def out_grad(lo):
            part = dot_tn(cot[:, lo : lo + chunk], act_c[...]).astype(BF16)
            for f in range(lo // tall, -(-(lo + chunk) // tall)):
                a, b = max(lo, f * tall), min(lo + chunk, (f + 1) * tall)
                r.g_out[f // 4, (f // 2) % 2, f % 2, a - f * tall : b - f * tall, :] = part[a - lo : b - lo]

        for lo in range(0, width, chunk):
            once(out_grad, lo)
        get_out.from_sibling()
        save_w.start()
        for c in [norm_gather] + pull:
            c.finish()
        put_out = scatter(UNITS[3], r.g_out)
        put_out.start()

        def fourth(j):
            return dot_nn(cot[block(j, BLOCK), :], flat(w_out))

        def fourth_rest(j, h):
            at = block(j, BLOCK)
            e = jnp.where(kept_in(j), h, 0.0)
            back = norm_back(n_c[at, :].astype(F32), scale[at, 2:3], gain_c, bias_c, e, sums, 4)
            shifted_store(g_even, g_odd, j, back)
            back_t[:, at] = back.astype(BF16).T

        skewed(total_blocks, fourth, fourth_rest, {0: [put_out.step1], loop_end: [put_out.step2]})

    pl.run_scoped(middle, pltpu.VMEM((rows, inner), BF16))
    put_out = scatter(UNITS[3], r.g_out)

    def late(g_in, g_conv):
        put_in, put_c0, put_c1 = scatter(UNITS[0], g_in), scatter(UNITS[1], g_conv), scatter(UNITS[2], g_conv)

        def conv_grad(k):
            buf, base = tap_of(b_even, b_odd, k, 1)
            for lo in range(0, inner, chunk):
                hi = min(lo + chunk, inner)
                total = None
                for s in range(slots):
                    p = dot_nn(back_t[:, s * seq : (s + 1) * seq], buf[s, base : base + seq, lo:hi])
                    total = p if total is None else total + p
                g_conv[k, :, :, :, :, lo:hi] = total.astype(BF16).reshape((2, 2, 2, inner // PLANE, hi - lo))

        for k in range(KERNEL_TAPS):
            once(conv_grad, k)
            if k == 1:
                put_out.step3()
            if k == 2:
                put_c0.start()
            if k == 3:
                put_c0.step1()
        put_c1.start()
        save_act.wait()
        save_w.wait()

        def sixth(j):
            return dot_nn(taps(g_even, g_odd, j, -1), w_conv[...].reshape(KERNEL_TAPS * inner, inner))

        def sixth_rest(j, h):
            at = block(j, BLOCK)
            e = jnp.where(kept_in(j), h, 0.0)
            back = norm_back(n_b[at, :].astype(F32), scale[at, 1:2], gain_b, bias_b, e, sums, 2).astype(BF16)
            grad_a[at, :] = back
            back_t[:, at] = back.T

        skewed(
            total_blocks,
            sixth,
            sixth_rest,
            {
                0: [put_c1.step1, lambda: put_out.step4(r.s_out)],
                1: [put_c0.step2],
                2: [put_c1.step2],
                loop_end: [put_c0.step3],
            },
        )

        def in_grad(j):
            part = dot_nn(back_t[...], act_a[:, j * chunk : (j + 1) * chunk]).astype(BF16)
            g_in[:, :, :, :, j * chunk : (j + 1) * chunk] = part.reshape(2, 2, 2, inner // PLANE, chunk)

        for j in range(width // chunk):
            once(in_grad, j)
        put_in.start()

        def out_copy(at):
            return pltpu.make_async_copy(cot.at[at, :], r.grad_tokens.at[at, :], r.io.at[4])

        low_gain, low_bias = gain_a.astype(BF16), bias_a.astype(BF16)

        def eighth(j):
            return dot_nn(grad_a[block(j, BLOCK), :], flat(w_in))

        def eighth_rest(j, h):
            d_gain = d_bias = None
            for at in range(0, BLOCK, FINE):
                here = pl.ds(pl.multiple_of(j * BLOCK + at, FINE), FINE)
                n = x[here, :]
                z = n * low_gain + low_bias
                zz = z * z
                t = jnp.tanh(z * (BF16(GELU_SCALE) + BF16(GELU_SCALE * GELU_CUBE) * zz))
                slope = z * (BF16(0.5 * GELU_SCALE) + BF16(1.5 * GELU_SCALE * GELU_CUBE) * zz)
                dz = h[at : at + FINE].astype(BF16) * ((BF16(0.5) + BF16(0.5) * t) + (slope - (t * t) * slope))
                a, b = row_sum(dz * n), row_sum(dz)
                d_gain, d_bias = (a, b) if d_gain is None else (d_gain + a, d_bias + b)
                dn = dz * low_gain
                m1 = lane_sum(dn) * (1.0 / width)
                m2 = lane_sum(dn * n) * (1.0 / width)
                m1, m2, rs = (jnp.broadcast_to(v, n.shape).astype(BF16) for v in (m1, m2, scale[here, 0:1]))
                cot[here, :] = cot[here, :] + rs * (dn - m1 - n * m2)
            sums[0:1, :] += jnp.sum(d_gain, axis=0, keepdims=True)
            sums[1:2, :] += jnp.sum(d_bias, axis=0, keepdims=True)
            out_copy(block(j, BLOCK)).start()

        skewed(
            total_blocks,
            eighth,
            eighth_rest,
            {
                0: [put_in.step1, put_c1.step3],
                2: [put_in.step2],
                loop_end: [put_in.step3],
            },
        )
        mine = jnp.concatenate(
            [
                sums[0:1, 0:inner],
                sums[0:1, inner : 2 * inner],
                sums[1:2, 0:inner],
                sums[1:2, inner : 2 * inner],
                sums[2:6, 0:inner],
            ],
            axis=0,
        )
        for f in range(PLANE):
            r.sm_out[f, :, 0:cols] = mine[:, f * cols : (f + 1) * cols]
        small.start()
        r.s_counts[...] = count_sum.total()
        put_c0.step4(r.s_c0)
        small.along_z()
        put_c1.step4(r.s_c1)
        total = small.total()
        pair = jnp.zeros((2, cols), F32)
        for i in range(DP_RANKS):
            pair = pair + jnp.where(pc.d == i, total[2 * i : 2 * i + 2, 0:cols], 0.0)
        r.s_norms[...] = pair
        put_in.step4(r.s_in)
        for c in (put_in, put_c0, put_c1, put_out, small, count_sum):
            c.finish()

        def eighth_end(_):
            pltpu.make_async_copy(cot, r.grad_tokens, r.io.at[4]).wait()

        once(eighth_end, 0)

    pl.run_scoped(late, pltpu.VMEM(r.w_in.shape, BF16), pltpu.VMEM(w_conv.shape, BF16))


UNIT_SCRATCH = ("zg_", "gs_", "gr_", "rcv_", "r1a_", "r1b_", "r2a_", "r2b_", "zr_", "ss_", "sr_")


def run_block(tokens, cotangent, lengths, labels, w_in, w_conv, w_out, norm_params):
    rows, width = tokens.shape
    cols, rank_in = w_in.shape
    depth = w_conv.shape[1]
    inner = cols * PLANE
    slots = lengths.shape[0]
    seq = rows // slots
    V = pltpu.VMEM
    dma = pltpu.SemaphoreType.DMA
    h_out = w_out.shape[1]
    inputs = dict(
        lens=(lengths, pltpu.SMEM),
        tokens=(tokens, pl.ANY),
        cot_in=(cotangent, pl.ANY),
        labels=(labels.reshape(rows // 128, 128), V),
        p_in=(w_in, V),
        p_conv=(w_conv, V),
        p_out=(w_out, V),
        p_norms=(norm_params, V),
    )
    outputs = dict(
        act_out=((rows, inner), BF16, pl.ANY),
        w_saved=((2, 2, 2, h_out, inner), BF16, pl.ANY),
        grad_tokens=((rows, width), BF16, pl.ANY),
        s_counts=((8, 128), F32, V),
        s_norms=(norm_params.shape, F32, V),
    )
    halo_rows = V((slots, seq + 2 * HALO, inner), BF16)
    taps = V((KERNEL_TAPS, 2, 2, 2, cols, inner), BF16)
    scratch = dict(
        x=V((rows, width), BF16),
        cot=V((rows, width), BF16),
        act_a=V((rows, width), BF16),
        n_b=V((rows, inner), BF16),
        act_c=V((rows, inner), BF16),
        scale=V((rows, 8), F32),
        sums=V((8, width), F32),
        tail=V((8, inner), F32),
        norms=V((8, inner), F32),
        back_t=V((inner, rows), BF16),
        b_even=halo_rows,
        b_odd=halo_rows,
        g_even=halo_rows,
        g_odd=halo_rows,
        w_in=V((2, 2, 2, cols, width), BF16),
        w_conv=taps,
        w_out=V((2, 2, 2, h_out, inner), BF16),
        g_out=V((2, 2, 2, h_out, inner), BF16),
        io=dma((5,)),
        nz=V((DP_RANKS, 8, 128), F32),
        nw=V((2, 2, 2, 8, 128), F32),
        ns=dma((NormGather.SEMS,)),
        nr=dma((NormGather.SEMS,)),
    )
    tile = (8, 128)
    for k in ("sm_", "ct_"):
        shapes = (
            V((PLANE,) + tile, F32),
            V((PLANE,) + tile, F32),
            V(tile, F32),
            V((DP_RANKS,) + tile, F32),
            dma((SmallSum.SEMS,)),
            dma((PLANE + DP_RANKS,)),
        )
        scratch.update(zip([k + n for n in ("out", "got", "plane", "z", "s", "r")], shapes))
    for u in UNITS:
        lead = (u.count,) if u.count else ()
        h, lanes = (cols, width) if u.name == "in" else (h_out, inner) if u.name == "out" else (cols, inner)
        piece = rank_in if u.name == "in" else depth * (u.count or 2)
        z = (cols, round_up(piece))
        half = u.sizes(h, lanes)
        outputs["s_" + u.name] = (z, F32, V)
        shapes = (
            V((DP_RANKS,) + z, BF16),
            dma((Gather.SEMS,)),
            dma((Gather.SEMS,)),
            V(lead + (2, 2, h, lanes), BF16),
            V(lead + (2,) + half[0], BF16),
            V(lead + (2,) + half[1], BF16),
            V(lead + half[0], BF16),
            V(lead + half[1], BF16),
            V((DP_RANKS,) + z, BF16),
            dma((Scatter.SEMS,)),
            dma((Scatter.SEMS,)),
        )
        scratch.update(zip([k + u.name for k in UNIT_SCRATCH], shapes))
    names = list(inputs) + list(outputs) + list(scratch)
    work = 6 * rows * (2 * width * inner + KERNEL_TAPS * inner * inner)
    out = pl.pallas_call(
        lambda *refs: block_kernel(SimpleNamespace(**dict(zip(names, refs)))),
        out_shape=tuple(jax.ShapeDtypeStruct(s, t) for s, t, _ in outputs.values()),
        in_specs=[pl.BlockSpec(memory_space=m) for _, m in inputs.values()],
        out_specs=tuple(pl.BlockSpec(memory_space=m) for _, _, m in outputs.values()),
        scratch_shapes=list(scratch.values()),
        compiler_params=pltpu.CompilerParams(
            collective_id=0, has_side_effects=True, vmem_limit_bytes=VMEM_BYTES
        ),
        cost_estimate=pl.CostEstimate(flops=work, bytes_accessed=8 * rows * width, transcendentals=0),
        name="residual_block",
    )(*(a for a, _ in inputs.values()))
    return dict(zip(outputs, out))


VMEM_BYTES = 63 * 1024 * 1024


def finish_kernel(r):
    rows = r.tokens.shape[0] // FINISH_PARTS
    loads = {}

    def load(k, src, dst):
        loads[k] = pltpu.make_async_copy(src, dst, r.in_sem.at[len(loads)])
        loads[k].start()

    parts = [pl.ds(i * rows, rows) for i in range(FINISH_PARTS)]
    for i, at in enumerate(parts):
        load(("a", i), r.act_out.at[at, :], r.hold_act.at[at, :])
        load(("t", i), r.tokens.at[at, :], r.hold_x.at[at, :])
        if i == 0:
            load("w", r.w_saved, r.hold_w)
        if i > 0:
            load(("g", i - 1), r.grad_tokens.at[parts[i - 1], :], r.hold_g.at[parts[i - 1], :])
        if i == 3:
            for n in STEP_ORDER:
                load("s_" + n, getattr(r, "s_" + n), getattr(r, "bs_" + n))
                for kind in ("w_", "m_", "v_"):
                    if n != "c1":
                        load(kind + n, getattr(r, kind + n), getattr(r, "b" + kind + n))
            load("n", r.s_counts, r.bs_counts)
    load(("g", len(parts) - 1), r.grad_tokens.at[parts[-1], :], r.hold_g.at[parts[-1], :])
    stores = []

    def store(src, dst):
        stores.append(pltpu.make_async_copy(src, dst, r.out_sem.at[len(stores)]))
        stores[-1].start()

    def step(n, at, grad, rate, decay):
        new = adamw(getattr(r, "bw_" + n)[at], getattr(r, "bm_" + n)[at], getattr(r, "bv_" + n)[at], grad, rate, decay)
        for kind, value in zip(("ow_", "om_", "ov_"), new):
            getattr(r, kind + n)[at] = value

    def ready(n):
        for kind in ("s_", "w_", "m_", "v_"):
            if kind + n in loads:
                loads[kind + n].wait()

    def done(n):
        for kind in ("w_", "m_", "v_"):
            store(getattr(r, "o" + kind + n), getattr(r, "n" + kind + n))

    everything = (slice(None), slice(None))
    depth = r.bw_c0.shape[1]

    def conv_step():
        ready("c0")
        ready("c1")
        for u in UNITS[1:3]:
            for k in range(u.count):
                grad = getattr(r, "bs_" + u.name)[:, k * depth : (k + 1) * depth].T
                step("c0", (u.first + k,), grad, 0.5 * (KERNEL_TAPS * INNER) ** (-0.5), 0.01)
        done("c0")

    def in_step():
        ready("in")
        step("in", everything, r.bs_in[:, 0 : r.bw_in.shape[1]], 0.5 * D ** (-0.5), 0.01)
        done("in")

    def out_step():
        ready("out")
        flat = r.bs_out[...]
        grad = jnp.concatenate([flat[:, 0:depth].T, flat[:, depth : 2 * depth].T], axis=1)
        step("out", everything, grad, 0.5 * (INNER // 2) ** (-0.5), 0.01)
        done("out")
        ready("norms")
        step("norms", everything, r.bs_norms[...], 0.3, 0.0)
        done("norms")
        loads["n"].wait()
        r.type_counts[...] = r.bs_counts[0, 0:TYPES].astype(jnp.int32)

    others = [conv_step, in_step, out_step]
    loads["w"].wait()
    for i, at in enumerate(parts):
        loads[("a", i)].wait()
        loads[("t", i)].wait()
        w = r.hold_w[...]
        hid = dot_nt(r.hold_act[at, :], w.reshape(PLANE * w.shape[3], w.shape[4]))
        r.hold_x[at, :] = (r.hold_x[at, :].astype(F32) + hid).astype(BF16)
        store(r.hold_x.at[at, :], r.new_mixed.at[at, :])
        if i > 0:
            loads[("g", i - 1)].wait()
            store(r.hold_g.at[parts[i - 1], :], r.new_grad_tokens.at[parts[i - 1], :])
        if 0 <= i - 4 < len(others):
            others[i - 4]()
    loads[("g", len(parts) - 1)].wait()
    store(r.hold_g.at[parts[-1], :], r.new_grad_tokens.at[parts[-1], :])
    for c in stores:
        c.wait()


STEP_ORDER = ("c0", "c1", "in", "out", "norms")
FINISH_PARTS = 8


def run_finish(res, tokens, weights, means, squares):
    V, dma = pltpu.VMEM, pltpu.SemaphoreType.DMA
    inputs = {k: res[k] for k in ("act_out", "w_saved", "grad_tokens", "s_counts")}
    inputs["tokens"] = tokens
    held = []
    for n in STEP_ORDER:
        inputs["s_" + n] = res["s_" + n]
        held.append("s_" + n)
        if n in weights:
            for kind, arrays in (("w_", weights), ("m_", means), ("v_", squares)):
                inputs[kind + n] = arrays[n]
                held.append(kind + n)
    outputs = dict(new_mixed=tokens, new_grad_tokens=tokens)
    for kind in ("w_", "m_", "v_"):
        for n, a in weights.items():
            outputs["n" + kind + n] = a
    scratch = {"b" + k: V(inputs[k].shape, F32) for k in held + ["s_counts"]}
    for kind in ("ow_", "om_", "ov_"):
        scratch.update({kind + n: V(a.shape, F32) for n, a in weights.items()})
    whole = V(tokens.shape, BF16)
    scratch.update(hold_x=whole, hold_g=whole)
    scratch["hold_act"] = V(res["act_out"].shape, BF16)
    scratch["hold_w"] = V(res["w_saved"].shape, BF16)
    scratch.update(in_sem=dma((len(held) + 2 + 3 * FINISH_PARTS,)), out_sem=dma((12 + 2 * FINISH_PARTS,)))
    shapes = [jax.ShapeDtypeStruct(a.shape, a.dtype) for a in outputs.values()]
    names = list(inputs) + list(outputs) + ["type_counts"] + list(scratch)
    hbm = pl.BlockSpec(memory_space=pl.ANY)
    return pl.pallas_call(
        lambda *refs: finish_kernel(SimpleNamespace(**dict(zip(names, refs)))),
        out_shape=tuple(shapes) + (jax.ShapeDtypeStruct((TYPES,), jnp.int32),),
        in_specs=[hbm] * len(inputs),
        out_specs=(hbm,) * len(outputs) + (pl.BlockSpec(memory_space=V),),
        scratch_shapes=list(scratch.values()),
        compiler_params=pltpu.CompilerParams(vmem_limit_bytes=VMEM_BYTES),
        name="finish",
    )(*inputs.values())


def fused_body(
    tokens,
    cotangent,
    lengths,
    labels,
    w_in,
    w_conv,
    w_out,
    norm_params,
    mean_w_in,
    mean_w_conv,
    mean_w_out,
    mean_norms,
    square_w_in,
    square_w_conv,
    square_w_out,
    square_norms,
):
    res = run_block(tokens, cotangent, lengths, labels, w_in.T, w_conv, w_out, norm_params)
    names = ("in", "c0", "out", "norms")
    new = run_finish(
        res,
        tokens,
        dict(zip(names, (w_in.T, w_conv, w_out, norm_params))),
        dict(zip(names, (mean_w_in.T, mean_w_conv, mean_w_out, mean_norms))),
        dict(zip(names, (square_w_in.T, square_w_conv, square_w_out, square_norms))),
    )
    mixed, grad_tokens, *steps, counts = new
    for i in (0, 4, 8):
        steps[i] = steps[i].T
    return (mixed, grad_tokens, counts) + tuple(steps)


def solution(mesh):
    fused = mesh.shape["dp"] == DP_RANKS and mesh.shape["fsdp"] == PLANE
    return jax.shard_map(
        fused_body if fused else plain_body,
        mesh=mesh,
        in_specs=(
            P(("dp", "fsdp"), None),
            P(("dp", "fsdp"), None),
            P(("dp", "fsdp")),
            P(("dp", "fsdp")),
            P("dp", "fsdp"),
            P(None, "dp", "fsdp"),
            P("dp", "fsdp"),
            P("dp", "fsdp"),
            P("dp", "fsdp"),
            P(None, "dp", "fsdp"),
            P("dp", "fsdp"),
            P("dp", "fsdp"),
            P("dp", "fsdp"),
            P(None, "dp", "fsdp"),
            P("dp", "fsdp"),
            P("dp", "fsdp"),
        ),
        out_specs=(
            P(("dp", "fsdp"), None),
            P(("dp", "fsdp"), None),
            P(),
            P("dp", "fsdp"),
            P(None, "dp", "fsdp"),
            P("dp", "fsdp"),
            P("dp", "fsdp"),
            P("dp", "fsdp"),
            P(None, "dp", "fsdp"),
            P("dp", "fsdp"),
            P("dp", "fsdp"),
            P("dp", "fsdp"),
            P(None, "dp", "fsdp"),
            P("dp", "fsdp"),
            P("dp", "fsdp"),
        ),
        check_vma=False,
    )
```
